32 devices in a mesh: batch: 8 (over z, y), chan: 4 (over x, core).
Axes of the slice: x: 2, y: 2, z: 4, core: 2. Of those that a mesh axis runs over, the one named last changes fastest.
Arguments:
- features: bfloat16 [256, 256, 128], P('batch', 'chan'), may hold values from -6 to 6
- skip_feature: bfloat16 [256, 128, 128], P('batch', 'chan'), may hold values from -6 to 6
- section_ids: int32 [256], P('batch'), may hold values from 0 to 2
- micro_ids: int32 [256], P('batch'), may hold values from 0 to 3, as said below
- widener: bfloat16 [9, 2, 256, 512], P(None, None, 'chan', 'batch'), may hold values from -0.09375 to 0.09375
- refiner: bfloat16 [9, 2, 256, 256], P(None, None, 'chan', 'batch'), may hold values from -0.125 to 0.125
- squeezer: bfloat16 [16, 256, 1024], P(None, 'chan', 'batch'), may hold values from -0.09375 to 0.09375
- exciter: bfloat16 [256, 256], P('chan', 'batch'), may hold values from -0.75 to 0.75
- gain_one: float32 [256], P('chan'), may hold values from 0.5 to 1.5
- bias_one: float32 [256], P('chan'), may hold values from -3 to 3
- gain_two: float32 [256], P('chan'), may hold values from 0.5 to 1.5
- bias_two: float32 [256], P('chan'), may hold values from -3 to 3
- upstream: bfloat16 [256, 256, 256], P('batch', 'chan'), may hold values from -6 to 6
Outputs:
- output: bfloat16 [256, 256, 256], P('batch', 'chan')
- input_grad: float32 [256, 256, 128], P('batch', 'chan')
- skip_grad: float32 [256, 128, 128], P('batch', 'chan')
- widener_grad: float32 [9, 2, 256, 512], P(None, None, 'chan', 'batch')
- refiner_grad: float32 [9, 2, 256, 256], P(None, None, 'chan', 'batch')
- squeezer_grad: float32 [16, 256, 1024], P(None, 'chan', 'batch')
- exciter_grad: float32 [256, 256], P('chan', 'batch')
- norm_grads: float32 [4, 256], P(None, 'chan')
The draws below stay inside these ranges and needn't reach their ends.
Inputs may be any that keep to these rules, and one draw needn't show every extreme that they name: `micro_ids`: each of the 4 micro-batches holds exactly 64 samples.
All inputs are finite; a program needn't handle non-finite values.
Results may differ from the reference program's by a relative error of at most 0.015.
Values may be sent and summed in bfloat16 or wider, within the bound.
No kernel may reach another device: no remote copies, remote signals or barrier semaphores. Data moves between devices by JAX's collectives and lax.ppermute only.
A program may use at most 384 MiB of HBM per device.

```python
import jax
import jax.numpy as jnp
from jax import lax

CI = 512
CO = 256
CS = 1024
MB = 4
BATCH = 256


def draw_micro_ids(key, part):
    key = jax.random.fold_in(key, 7)
    shuffled = jax.random.permutation(key, BATCH)
    return (shuffled % MB).astype(jnp.int32)


def plant(values, key, low, high):
    longest = values.shape.index(max(values.shape))
    spots = []
    for shift in (0, 1):
        where = [jax.random.randint(jax.random.fold_in(key, axis), (), 0, length) for axis, length in enumerate(values.shape)]
        where[longest] = (where[longest] + shift) % values.shape[longest]
        spots.append(tuple(where))
    return values.at[spots[0]].set(low).at[spots[1]].set(high)


def level_of(rng, extent, shards, low, high):
    level, own = 1.0, jax.random.fold_in(rng, 6)
    for axis_at, blocks in shards:
        draws = jnp.exp(jax.random.uniform(jax.random.fold_in(own, axis_at), (blocks,), jnp.float32, low / len(shards), high / len(shards)))
        level = level * jnp.repeat(draws, extent[axis_at] // blocks).reshape([-1 if axis == axis_at else 1 for axis in range(len(extent))])
    return level


def centred(rng, dims, width, reach, cuts=(), held_as=jnp.bfloat16):
    drawn = width * jax.random.normal(rng, dims, jnp.float32)
    if cuts:
        drawn = drawn * level_of(rng, dims, cuts, -0.22, 0.18)
    return jnp.clip(drawn, -reach, reach).astype(held_as)


def setup_inputs(seed: int = 0) -> dict:
    key_of = jax.random.split(jax.random.key(seed), 14)
    features = centred(key_of[0], (BATCH, CI // 2, 128), 1.0, 6.0, ((0, 8), (1, 4)))
    skip_feature = centred(key_of[1], (BATCH, CS // 8, 128), 1.0, 6.0, ((0, 8), (1, 4)))
    section_ids = plant(jax.random.randint(key_of[2], (BATCH,), 0, 3), jax.random.fold_in(key_of[2], 1), 0, 2).astype(jnp.int32)
    micro_ids = draw_micro_ids(jax.random.fold_in(key_of[13], 71), 0)
    widener = centred(key_of[4], (9, 2, CO, CI), (9 * CI) ** -0.5, 0.09375, ((2, 4), (3, 8)))
    refiner = centred(key_of[5], (9, 2, CO, CO), (9 * CO) ** -0.5, 0.125, ((2, 4), (3, 8)))
    squeezer = centred(key_of[6], (16, CO, CS), (4 * CS) ** -0.5, 0.09375, ((1, 4), (2, 8)))
    exciter = centred(key_of[7], (CO, CO), (CO // 4) ** -0.5, 0.75, ((0, 4), (1, 8)))
    gain_one = jnp.clip(1.0 + 0.1 * jax.random.normal(key_of[8], (CO,), jnp.float32), 0.5, 1.5)
    bias_one = centred(key_of[9], (CO,), 0.5, 3.0, ((0, 4),), jnp.float32)
    gain_two = jnp.clip(1.0 + 0.1 * jax.random.normal(key_of[10], (CO,), jnp.float32), 0.5, 1.5)
    bias_two = centred(key_of[11], (CO,), 0.5, 3.0, ((0, 4),), jnp.float32)
    upstream = centred(key_of[12], (BATCH, CO, 256), 1.0, 6.0, ((0, 8), (1, 4)))
    return dict(features=features, skip_feature=skip_feature, section_ids=section_ids, micro_ids=micro_ids, widener=widener, refiner=refiner, squeezer=squeezer, exciter=exciter, gain_one=gain_one, bias_one=bias_one, gain_two=gain_two, bias_two=bias_two, upstream=upstream)


@jax.custom_vjp
def low(v):
    return lax.optimization_barrier(v.astype(jnp.bfloat16)).astype(jnp.float32)

@jax.custom_vjp
def low_back(v):
    return v

def low_keep(v):
    return (low(v), None)

def low_pass(kept, grad):
    return (grad,)

def back_keep(v):
    return (v, None)

def back_low(kept, grad):
    return (low(grad),)
low.defvjp(low_keep, low_pass)
low_back.defvjp(back_keep, back_low)
precise = lax.Precision.HIGHEST
epsilon = 1e-05

def conv_taps(feature, kernel):
    halves = kernel.shape[1]
    width_out = kernel.shape[2]
    width_in = kernel.shape[3]
    weights = kernel.reshape(3, 3, halves * width_out, width_in).transpose(2, 3, 0, 1)
    return lax.conv_general_dilated(feature, weights, (1, 1), ((1, 1), (1, 1)), dimension_numbers=('NCHW', 'OIHW', 'NCHW'), precision=precise)

def gated_unit(conv):
    half = conv.shape[1] // 2
    return conv[:, :half] * jax.nn.sigmoid(conv[:, half:])

def norm_group(values, gain, shift, onehot):
    entries = BATCH // MB * 256
    totals = jnp.dot(onehot.T, lax.optimization_barrier(jnp.sum(values, axis=(2, 3))), precision=precise)
    means = totals / entries
    centered = values - jnp.dot(onehot, means, precision=precise)[:, :, None, None]
    spread = jnp.dot(onehot.T, lax.optimization_barrier(jnp.sum(centered * centered, axis=(2, 3))), precision=precise) / entries
    scaled = centered * jnp.dot(onehot, lax.rsqrt(spread + epsilon), precision=precise)[:, :, None, None]
    return scaled * gain[None, :, None, None] + shift[None, :, None, None]

def forward(features, skip_feature, widener, refiner, squeezer, exciter, gain_one, bias_one, gain_two, bias_two, onehot):
    samples = features.shape[0]
    upsampled = jnp.repeat(jnp.repeat(features.reshape(samples, -1, 8, 8), 2, axis=2), 2, axis=3)
    conv_one = low_back(conv_taps(upsampled, widener))
    norm_one = norm_group(gated_unit(conv_one), gain_one, bias_one, onehot)
    hidden = low(norm_one)
    conv_two = low_back(conv_taps(hidden, refiner))
    norm_two = norm_group(gated_unit(conv_two), gain_two, bias_two, onehot)
    pooled = skip_feature.reshape(samples, -1, 16)
    squeezed = low_back(jnp.einsum('toc,bct->bo', squeezer, pooled, precision=precise))
    swish = low(squeezed * jax.nn.sigmoid(squeezed))
    excited = low_back(jnp.einsum('oc,bc->bo', exciter, swish, precision=precise))
    return norm_two * jax.nn.sigmoid(excited)[:, :, None, None]

def reference(features, skip_feature, section_ids, micro_ids, widener, refiner, squeezer, exciter, gain_one, bias_one, gain_two, bias_two, upstream):
    onehot = (micro_ids[:, None] == jnp.arange(MB, dtype=jnp.int32)[None, :]).astype(jnp.float32)
    weight_of = jnp.where(section_ids == 0, 1.0, jnp.where(section_ids == 1, 2.0, 4.0)).astype(jnp.float32)
    params = tuple((item.astype(jnp.float32) for item in (features, skip_feature, widener, refiner, squeezer, exciter, gain_one, bias_one, gain_two, bias_two)))

    def apply(*values):
        return forward(*values, onehot)
    result, pullback = jax.vjp(apply, *params)
    cotangent = upstream.astype(jnp.float32).reshape(result.shape) * weight_of[:, None, None, None]
    grads = pullback(cotangent)
    output = result.reshape(BATCH, CO, 256).astype(jnp.bfloat16)
    norm_grads = jnp.stack([grads[6], grads[7], grads[8], grads[9]], axis=0)
    return (output, grads[0], grads[1], grads[2], grads[3], grads[4], grads[5], norm_grads)
```

```python
import jax
import jax.numpy as jnp
from jax import lax
from jax.experimental import pallas as pl
from jax.experimental.pallas import tpu as pltpu
from jax.sharding import PartitionSpec as P

MB = 4
epsilon = 1e-05
f32 = jnp.float32
bf16 = jnp.bfloat16
MIB = 2**20

NT = (((1,), (1,)), ((), ()))
TN = (((0,), (0,)), ((), ()))


def dot(a, b, dims=None):
    if dims is None:
        return jnp.dot(a, b, preferred_element_type=f32)
    return lax.dot_general(a, b, dims, preferred_element_type=f32)


def call(body, outs, args, name, scratch=(), flops=0, smem=1, limit=48):
    outs = [jax.ShapeDtypeStruct(shape, dtype) for shape, dtype in outs]
    moved = sum(a.size * a.dtype.itemsize for a in args) + sum(
        o.size * o.dtype.itemsize for o in outs
    )
    specs = [pl.BlockSpec(memory_space=pltpu.SMEM)] * smem + [
        pl.BlockSpec(memory_space=pltpu.VMEM)
    ] * (len(args) - smem)
    return pl.pallas_call(
        body,
        out_shape=outs,
        in_specs=specs,
        out_specs=[pl.BlockSpec(memory_space=pltpu.VMEM)] * len(outs),
        scratch_shapes=list(scratch),
        compiler_params=pltpu.CompilerParams(vmem_limit_bytes=limit * MIB),
        cost_estimate=pl.CostEstimate(
            flops=int(flops), bytes_accessed=int(moved), transcendentals=0
        ),
        name=name,
    )(*args)


def iota(shape, dim):
    return lax.broadcasted_iota(jnp.int32, shape, dim)


def onehot(cond):
    return jnp.where(cond, 1.0, 0.0).astype(f32).astype(bf16)


def eye(n):
    return onehot(iota((n, n), 0) == iota((n, n), 1))


def sixteen_swap():
    r, q = iota((256, 256), 0), iota((256, 256), 1)
    return onehot(((r % 16) == (q // 16)) & ((r // 16) == (q % 16)))


def tree(parts):
    parts = list(parts)
    while len(parts) > 1:
        parts = [parts[n] + parts[n + 1] for n in range(0, len(parts), 2)]
    return parts[0]


def pack_body(w, r, e, wout, rout):
    wout[...] = jnp.concatenate([w[:, 0], w[:, 1]], axis=-1)
    slots = [r[q // 2, q % 2] for q in range(18)] + [e[...], jnp.zeros_like(e[...])]
    for row in range(5):
        rout[row] = jnp.concatenate(slots[4 * row : 4 * row + 4], axis=-1)


def widener_body(idx, *refs):
    own, other, out = refs[:8], refs[8:16], refs[16]
    core = idx[2]
    for blocks, side in ((own, core), (other, 1 - core)):
        for half in range(2):
            rows = pl.ds(pl.multiple_of(half * 128 + side * 64, 64), 64)
            lanes = slice(half * 64, half * 64 + 64)
            for group in range(4):
                w = [
                    jnp.concatenate(
                        [blocks[2 * group][t][:, lanes], blocks[2 * group + 1][t][:, lanes]],
                        axis=-1,
                    ).astype(f32)
                    for t in range(9)
                ]
                down = {
                    (0, 0): w[0:3],
                    (0, 1): [w[3 + s] + w[6 + s] for s in range(3)],
                    (1, 0): [w[s] + w[3 + s] for s in range(3)],
                    (1, 1): w[6:9],
                }
                for a in range(2):
                    for u in range(2):
                        d = down[(a, u)]
                        across = {
                            (0, 0): d[0],
                            (0, 1): d[1] + d[2],
                            (1, 0): d[0] + d[1],
                            (1, 1): d[2],
                        }
                        for b in range(2):
                            for v in range(2):
                                out[
                                    a * 8 + b * 4 + u * 2 + v,
                                    rows,
                                    group * 128 : group * 128 + 128,
                                ] = across[(b, v)].astype(bf16)


def refiner_select(base, chip):
    r, q = iota((1024, 1024), 0), iota((1024, 1024), 1)
    channel = ((r // 128) ^ base) * 32 + r % 32
    return onehot((((r // 32) % 4) == (q // 256)) & ((channel ^ (chip * 128)) == (q % 256)))


def refiner_body(idx, *refs):
    own, other, out, ex = refs[:8], refs[8:16], refs[16], refs[17]
    base, core, chip = idx[0], idx[2], idx[3]
    select = refiner_select(base, chip)
    for blocks, side in ((own, core), (other, 1 - core)):
        rows = pl.multiple_of(side * 64, 64)
        raw = jnp.concatenate([blocks[k][...].reshape(320, 128) for k in range(8)], axis=-1)
        got = dot(raw, select).astype(bf16)
        for q in range(18):
            piece = got[(q // 4) * 64 : (q // 4) * 64 + 64, (q % 4) * 256 : (q % 4) * 256 + 256]
            out[q // 2, pl.ds(rows + (q % 2) * 128, 64), :] = piece
        ex[pl.ds(rows, 64), :] = got[256:320, 512:768]


def feature_select(base, place):
    r, q = iota((512, 512), 0), iota((512, 512), 1)
    kept = r % 256
    have = (((kept // 64) ^ place) * 64 + kept % 64) * 2 + r // 256
    want = ((q // 64) ^ base) * 64 + q % 64
    return onehot(have == want)


def feature_body(idx, b0, b1, b2, b3, out, turned):
    ident = eye(128)

    def turn(s, carry):
        x = jnp.concatenate([b0[s], b1[s], b2[s], b3[s]], axis=0)
        t = dot(ident, x, NT).astype(bf16)
        turned[s] = jnp.concatenate([t[:64], t[64:]], axis=-1)
        return carry

    lax.fori_loop(0, 16, turn, 0)
    swap = sixteen_swap()
    select = feature_select(idx[0], idx[1])
    zero = jnp.zeros((10, 16, 512), bf16)
    out[0] = zero
    out[9] = zero
    out[:, 0] = zero
    out[:, 9] = zero
    for block in range(4):
        a = turned[:, block * 16 : block * 16 + 16, :].reshape(256, 512)
        c = dot(dot(swap, a).astype(bf16), select).astype(bf16)
        out[1 + 2 * block : 3 + 2 * block, 1:9] = c.reshape(2, 8, 16, 512)


def input_back_body(idx, d, w, b0, b1, b2, b3, turned):
    swap = sixteen_swap()
    select = feature_select(idx[0], idx[1])

    def block_step(block, carry):
        parts = []
        for a in range(2):
            for b in range(2):
                for u in range(2):
                    for v in range(2):
                        parts.append(
                            d[a, b, pl.ds(2 * block + 2 - u - a, 2), 2 - v - b : 10 - v - b].reshape(
                                256, 256
                            )
                        )
        x = dot(jnp.concatenate(parts, axis=-1), w[...].reshape(4096, 512)).astype(bf16)
        x = dot(x, select, NT).astype(bf16)
        x = dot(swap, x).astype(bf16)
        turned[:, pl.ds(pl.multiple_of(block * 16, 16), 16), :] = x.reshape(16, 16, 512)
        return carry

    lax.fori_loop(0, 4, block_step, 0)
    ident = eye(256)

    def turn(s, carry):
        t = turned[s]
        t = jnp.concatenate([t[:, :256], t[:, 256:]], axis=0)
        o = dot(ident, t, NT).astype(bf16)
        b0[s] = o[0:64]
        b1[s] = o[64:128]
        b2[s] = o[128:192]
        b3[s] = o[192:256]
        return carry

    lax.fori_loop(0, 16, turn, 0)


def upstream_body(idx, own, other, out, turned):
    first = idx[2] == 0
    ident = eye(256)

    def turn(s, carry):
        p, q = own[s], other[s]
        lo = jnp.where(first, p, q)
        hi = jnp.where(first, q, p)
        turned[s] = dot(ident, jnp.concatenate([lo, hi], axis=0), NT).astype(bf16)
        return carry

    lax.fori_loop(0, 16, turn, 0)
    swap = sixteen_swap()

    def mix(y, carry):
        a = turned[:, pl.ds(pl.multiple_of(y * 16, 16), 16), :].reshape(256, 128)
        out[y] = dot(swap, a).astype(bf16).reshape(16, 16, 128)
        return carry

    lax.fori_loop(0, 16, mix, 0)


def over_samples(mask, values):
    return jnp.concatenate(
        [jnp.sum(mask[m] * values, axis=0, keepdims=True) for m in range(MB)], axis=0
    )


def per_sample(mask, rows):
    return sum(mask[m] * rows[m : m + 1] for m in range(MB))


def local_stats(mask, mean_s, squares_s):
    ones = jnp.ones_like(mean_s)
    n = over_samples(mask, ones) * 256.0
    mean = over_samples(mask, mean_s) * 256.0 / jnp.maximum(n, 1.0)
    gap = mean_s - per_sample(mask, mean)
    squares = over_samples(mask, squares_s + 256.0 * gap * gap)
    return n, mean, squares


def total_stats(messages, entries):
    parts = [(g[0:4], g[4:8], g[8:12]) for g in messages]
    mean = tree([n * m for n, m, _ in parts]) / entries
    squares = tree([q + n * (m - mean) * (m - mean) for n, m, q in parts])
    inverse = lax.rsqrt(squares / entries + epsilon)
    return mean, inverse


def message_list(refs):
    return [ref[c] for ref in refs for c in range(ref.shape[0])]


def conv_one_body(x, w, mask, glu, sig, msg):
    total = jnp.zeros((16, 128), f32)
    for a in range(2):
        for b in range(2):
            kept = []
            for u in range(2):
                for v in range(2):
                    kept.append(x[u + a : u + a + 8, v + b : v + b + 8].reshape(1024, 512))
            base = a * 8 + b * 4
            rhs = jnp.concatenate([w[base + n] for n in range(4)], axis=-1)
            c = dot(jnp.concatenate(kept, axis=-1), rhs, NT)
            s = 1.0 / (1.0 + jnp.exp(-c[:, 128:]))
            g = (c[:, :128] * s).reshape(8, 8, 16, 128)
            sig[a, b] = s.reshape(8, 8, 16, 128)
            glu[a, b] = g
            total = total + jnp.sum(g, axis=(0, 1))
    mean_s = total * (1.0 / 256.0)

    def spread(n, acc):
        gap = glu[n // 16, (n // 8) % 2, n % 8] - mean_s[None]
        return acc + jnp.sum(gap * gap, axis=0)

    squares = lax.fori_loop(0, 32, spread, jnp.zeros((16, 128), f32))
    n, mean, squares = local_stats(mask[...], mean_s, squares)
    msg[0:4] = n
    msg[4:8] = mean
    msg[8:12] = squares
    msg[12:16] = jnp.zeros((4, 128), f32)


def make_hidden_body(entries):
    def body(glu, mask, gains, *refs):
        out, stat = refs[-2], refs[-1]
        mean, inverse = total_stats(message_list(refs[:-2]), entries)
        m = mask[...]
        mean_s, inverse_s = per_sample(m, mean), per_sample(m, inverse)
        stat[0] = mean_s
        stat[1] = inverse_s
        gain, shift = gains[0:1], gains[1:2]

        def step(i, carry):
            for a in range(2):
                for b in range(2):
                    h = ((glu[a, b, i] - mean_s) * inverse_s) * gain + shift
                    out[i, a, :, b] = h.astype(bf16)
            return carry

        lax.fori_loop(0, 8, step, 0)

    return body


def conv_two_body(own, other, w, up, mask, pull, held, glu, sig, sums, msg):
    zero = jnp.zeros((18, 16, 256), bf16)
    held[0] = zero
    held[17] = zero
    held[:, 0] = zero
    held[:, 17] = zero
    held[1:17, 1:17, :, 0:128] = own[...]
    held[1:17, 1:17, :, 128:256] = other[...]

    def rows(step, total):
        y = step * 4
        lhs = jnp.concatenate(
            [
                held[pl.ds(y + t // 3, 4), t % 3 : t % 3 + 16].reshape(1024, 256)
                for t in range(9)
            ],
            axis=-1,
        )
        rhs = jnp.concatenate([w[t] for t in range(9)], axis=-1)
        c = dot(lhs, rhs, NT)
        s = 1.0 / (1.0 + jnp.exp(-c[:, 128:]))
        g = (c[:, :128] * s).reshape(4, 16, 16, 128)
        sig[pl.ds(y, 4)] = s.reshape(4, 16, 16, 128)
        glu[pl.ds(y, 4)] = g
        return total + jnp.sum(g, axis=(0, 1))

    total = lax.fori_loop(0, 4, rows, jnp.zeros((16, 128), f32))
    mean_s = total * (1.0 / 256.0)

    def spread(y, acc):
        gap = glu[y] - mean_s[None]
        u = up[y].astype(f32)
        return (
            acc[0] + jnp.sum(gap * gap, axis=0),
            acc[1] + jnp.sum(u, axis=0),
            acc[2] + jnp.sum(u * gap, axis=0),
        )

    none = jnp.zeros((16, 128), f32)
    squares, plain, cross = lax.fori_loop(0, 16, spread, (none, none, none))
    sums[0] = mean_s
    sums[1] = plain
    sums[2] = cross
    m = mask[...]
    n, mean, squares = local_stats(m, mean_s, squares)
    factor = pull[0] * pull[1]
    msg[0:4] = n
    msg[4:8] = mean
    msg[8:12] = squares
    msg[12:16] = over_samples(m, factor * plain)
    msg[16:20] = over_samples(m, factor * (cross + plain * (mean_s - per_sample(m, mean))))
    msg[20:24] = jnp.zeros((4, 128), f32)


def make_back_two_body(entries):
    def body(glu, sig, up, mask, pull, gains, sums, w, *refs):
        grad, own, other, small, stat = refs[-5:]
        messages = message_list(refs[:-5])
        mean, inverse = total_stats(messages, entries)
        plain = tree([g[12:16] for g in messages])
        cross = inverse * tree([g[16:20] + g[12:16] * (g[4:8] - mean) for g in messages])
        m = mask[...]
        mean_s, inverse_s = per_sample(m, mean), per_sample(m, inverse)
        gain, shift = gains[2:3], gains[3:4]
        stat[0] = mean_s
        stat[1] = inverse_s
        weight, gate = pull[0], pull[1]
        centred = sums[2] + sums[1] * (sums[0] - mean_s)
        small[0:16] = weight * (gain * inverse_s * centred + shift * sums[1])
        small[16:17] = jnp.sum(cross, axis=0, keepdims=True)
        small[17:18] = jnp.sum(plain, axis=0, keepdims=True)
        small[18:24] = jnp.zeros((6, 128), f32)
        plain_s = per_sample(m, plain) * (1.0 / entries)
        cross_s = per_sample(m, cross) * (1.0 / entries)
        scale = inverse_s * gain
        factor = weight * gate
        zero = jnp.zeros((18, 16, 256), bf16)
        grad[0] = zero
        grad[17] = zero
        grad[:, 0] = zero
        grad[:, 17] = zero

        def step(y, carry):
            g = glu[y]
            s = sig[y]
            hat = (g - mean_s) * inverse_s
            d = scale * (up[y].astype(f32) * factor - plain_s - hat * cross_s)
            grad[y + 1, 1:17, :, 0:128] = (d * s).astype(bf16)
            grad[y + 1, 1:17, :, 128:256] = (d * g * (1.0 - s)).astype(bf16)
            return carry

        lax.fori_loop(0, 16, step, 0)

        def rows(step, carry):
            y = step * 4
            lhs = jnp.concatenate(
                [
                    grad[pl.ds(y + 2 - t // 3, 4), 2 - t % 3 : 18 - t % 3].reshape(1024, 256)
                    for t in range(9)
                ],
                axis=-1,
            )
            c = dot(lhs, w[...].reshape(2304, 256)).astype(bf16)
            own[pl.ds(y, 4)] = c[:, :128].reshape(4, 16, 16, 128)
            other[pl.ds(y, 4)] = c[:, 128:].reshape(4, 16, 16, 128)
            return carry

        lax.fori_loop(0, 4, rows, 0)

    return body


def output_body(idx, glu, stat, pull, gains, own, other, turned):
    swap = sixteen_swap()
    mean_s, inverse_s = stat[0], stat[1]
    gain, shift = gains[2:3], gains[3:4]
    gate = pull[1]

    def step(y, carry):
        o = (((glu[y] - mean_s) * inverse_s) * gain + shift) * gate
        o = dot(swap, o.astype(bf16).reshape(256, 128)).astype(bf16)
        turned[:, pl.ds(pl.multiple_of(y * 16, 16), 16), :] = o.reshape(16, 16, 128)
        return carry

    lax.fori_loop(0, 16, step, 0)
    ident = eye(128)
    first = idx[2] == 0

    def turn(s, carry):
        t = dot(ident, turned[s], NT).astype(bf16)
        own[s] = jnp.where(first, t[:64], t[64:])
        other[s] = jnp.where(first, t[64:], t[:64])
        return carry

    lax.fori_loop(0, 16, turn, 0)


def refiner_grad_body(idx, grad, held, own, other, work):
    base, core, chip = idx[0], idx[2], idx[3]

    def tap(t, carry):
        d = grad[1:17, 1:17].reshape(4096, 256)
        h = held[pl.ds(t // 3, 16), pl.ds(t % 3, 16)].reshape(4096, 256)
        work[t] = dot(d, h, TN).astype(bf16)
        return carry

    lax.fori_loop(0, 9, tap, 0)
    select = refiner_select(base, chip)
    for out, side in ((own, core), (other, 1 - core)):
        start = pl.multiple_of(side * 64, 64)
        rows = []
        for row in range(5):
            pieces = []
            for q in range(4 * row, 4 * row + 4):
                if q < 18:
                    pieces.append(work[q // 2, pl.ds(start + (q % 2) * 128, 64), :])
                else:
                    pieces.append(jnp.zeros((64, 256), bf16))
            rows.append(jnp.concatenate(pieces, axis=-1))
        got = dot(jnp.concatenate(rows, axis=0), select, NT).astype(bf16)
        for k in range(8):
            out[k] = got[:, k * 128 : k * 128 + 128].reshape(5, 64, 128)


def refiner_sum_body(*refs):
    out = refs[-1]
    total = tree([ref[...].astype(f32) for ref in refs[:-1]])
    for q in range(18):
        out[q // 2, q % 2] = total[q // 4][:, (q % 4) * 32 : (q % 4) * 32 + 32]


def first_sums_body(glu, own, other, mask, stat, msg):
    mean_s, inverse_s = stat[0], stat[1]

    def step(i, acc):
        plain, cross = acc
        for a in range(2):
            for b in range(2):
                d = own[i, a, :, b].astype(f32) + other[i, a, :, b].astype(f32)
                plain = plain + jnp.sum(d, axis=0)
                cross = cross + jnp.sum(d * (glu[a, b, i] - mean_s), axis=0)
        return plain, cross

    none = jnp.zeros((16, 128), f32)
    plain, cross = lax.fori_loop(0, 8, step, (none, none))
    m = mask[...]
    msg[0:4] = over_samples(m, plain)
    msg[4:8] = over_samples(m, cross * inverse_s)


def make_back_one_body(entries):
    def body(glu, sig, own, other, mask, stat, gains, *refs):
        grad, small = refs[-2:]
        messages = message_list(refs[:-2])
        plain = tree([g[0:4] for g in messages])
        cross = tree([g[4:8] for g in messages])
        small[0:1] = jnp.sum(cross, axis=0, keepdims=True)
        small[1:2] = jnp.sum(plain, axis=0, keepdims=True)
        small[2:8] = jnp.zeros((6, 128), f32)
        m = mask[...]
        plain_s = per_sample(m, plain) * (1.0 / entries)
        cross_s = per_sample(m, cross) * (1.0 / entries)
        mean_s, inverse_s = stat[0], stat[1]
        scale = inverse_s * gains[0:1]
        zero = jnp.zeros((10, 16, 256), bf16)
        for a in range(2):
            for b in range(2):
                grad[a, b, 0] = zero
                grad[a, b, 9] = zero
                grad[a, b, :, 0] = zero
                grad[a, b, :, 9] = zero

        def step(i, carry):
            for a in range(2):
                for b in range(2):
                    g = glu[a, b, i]
                    s = sig[a, b, i]
                    hat = (g - mean_s) * inverse_s
                    d = own[i, a, :, b].astype(f32) + other[i, a, :, b].astype(f32)
                    d = scale * (d - plain_s - hat * cross_s)
                    grad[a, b, i + 1, 1:9, :, 0:128] = (d * s).astype(bf16)
                    grad[a, b, i + 1, 1:9, :, 128:256] = (d * g * (1.0 - s)).astype(bf16)
            return carry

        lax.fori_loop(0, 8, step, 0)

    return body


def widener_grad_body(idx, grad, x, own, other, work):
    core = idx[2]

    def phase(n, carry):
        a, b = n // 2, n % 2
        d = grad[a, b, 1:9, 1:9].reshape(1024, 256)
        for u in range(2):
            for v in range(2):
                f = x[pl.ds(u + a, 8), pl.ds(v + b, 8)].reshape(1024, 512)
                work[n, 2 * u + v] = dot(d, f, TN)
        return carry

    lax.fori_loop(0, 4, phase, 0)
    source = {0: (0, 0), 1: (1, 0), 2: (1, 1)}
    for out, side in ((own, core), (other, 1 - core)):
        start = pl.multiple_of(side * 64, 64)
        for pair in range(4):
            lanes = slice(pair * 128, pair * 128 + 128)
            for r in range(3):
                for s in range(3):
                    both = []
                    for half in range(2):
                        rows = pl.ds(start + half * 128, 64)
                        both.append(
                            sum(
                                work[2 * a + b, 2 * source[r][a] + source[s][b], rows, lanes]
                                for a in range(2)
                                for b in range(2)
                            )
                        )
                    first, second = both
                    out[2 * pair, 3 * r + s] = jnp.concatenate(
                        [first[:, :64], second[:, :64]], axis=-1
                    ).astype(bf16)
                    out[2 * pair + 1, 3 * r + s] = jnp.concatenate(
                        [first[:, 64:], second[:, 64:]], axis=-1
                    ).astype(bf16)


def widener_sum_body(*refs):
    out = refs[-1]
    for t in range(9):
        total = tree([ref[t].astype(f32) for ref in refs[:-1]])
        out[t, 0] = total[:, :64]
        out[t, 1] = total[:, 64:]


def swap_with(v, axis, k):
    return lax.ppermute(v, axis, [(n, n ^ k) for n in range(lax.axis_size(axis))])


def on_device(
    features,
    skip_feature,
    section_ids,
    micro_ids,
    widener,
    refiner,
    squeezer,
    exciter,
    gain_one,
    bias_one,
    gain_two,
    bias_two,
    upstream,
):
    nb = lax.axis_size("batch")
    eight = nb == 8
    samples = features.shape[0]
    entries = float(samples * nb // MB * 256)
    i = lax.axis_index("batch")
    j = lax.axis_index("chan")
    core, chip = j % 2, j // 2
    base = i if eight else 0 * i
    idx = jnp.stack([base, j, core, chip]).astype(jnp.int32)

    def half(v, which):
        return lax.dynamic_slice_in_dim(v, which * 16, 16, axis=0)

    def natural(own, other, axis):
        return jnp.where(
            core == 0,
            jnp.concatenate([own, other], axis=axis),
            jnp.concatenate([other, own], axis=axis),
        )

    if eight:
        wide, fine = call(
            pack_body,
            [((9, 64, 128), bf16), ((5, 64, 128), bf16)],
            (widener, refiner, exciter),
            "pack",
            smem=0,
        )
        f_keep, f_send = half(features, core), half(features, 1 - core)
        f_blocks = [f_keep] + [
            swap_with(f_send if k % 2 else f_keep, "chan", k) for k in range(1, 4)
        ]
        wide_own = [wide] + [swap_with(wide, "batch", k) for k in range(1, 8)]
        fine_own = [fine] + [swap_with(fine, "batch", k) for k in range(1, 8)]
    else:
        f_keep, f_send = half(features, core), half(features, 1 - core)
        f_blocks = [f_keep] + [
            swap_with(f_send if k % 2 else f_keep, "chan", k) for k in range(1, 4)
        ]
        w_all = lax.all_gather(widener, "batch", axis=3, tiled=True)
        r_all = lax.all_gather(refiner, "batch", axis=3, tiled=True)
        e_all = lax.all_gather(exciter, "batch", axis=1, tiled=True)
        w_all = w_all.reshape(9, 2, 64, 8, 64).transpose(3, 0, 2, 1, 4).reshape(8, 9, 64, 128)
        r_all = jnp.concatenate(
            [r_all.reshape(18, 64, 256), e_all[None], jnp.zeros((1, 64, 256), bf16)], axis=0
        )
        r_all = r_all.reshape(5, 4, 64, 8, 32).transpose(3, 0, 2, 1, 4).reshape(8, 5, 64, 128)
        wide_own = [w_all[k] for k in range(8)]
        fine_own = [r_all[k] for k in range(8)]
    wide_other = [swap_with(v, "chan", 1) for v in wide_own]
    fine_other = [swap_with(v, "chan", 1) for v in fine_own]

    gains = jnp.stack([gain_one, bias_one, gain_two, bias_two], axis=0)
    gains = natural(gains, swap_with(gains, "chan", 1), 1)
    ids = half(micro_ids, core)
    mask = jnp.broadcast_to(
        (ids[None, :, None] == jnp.arange(MB, dtype=jnp.int32)[:, None, None]).astype(f32),
        (MB, 16, 128),
    )
    weight_of = jnp.where(section_ids == 0, 1.0, jnp.where(section_ids == 1, 2.0, 4.0)).astype(f32)
    weight = jnp.broadcast_to(half(weight_of, core)[:, None], (16, 128))

    def share(msg):
        pair = jnp.stack([msg, swap_with(msg, "chan", 1)], axis=0)
        if eight:
            return [pair] + [swap_with(pair, "batch", k) for k in range(1, 8)]
        rows = lax.all_gather(pair, "batch")
        return [rows.reshape((-1,) + msg.shape)]

    (field,) = call(
        feature_body,
        [((10, 10, 16, 512), bf16)],
        (idx, *f_blocks),
        "features_turned",
        scratch=[pltpu.VMEM((16, 64, 512), bf16)],
        flops=1.4e9,
    )
    (wide_w,) = call(
        widener_body,
        [((16, 256, 512), bf16)],
        (idx, *wide_own, *wide_other),
        "widener_taps",
        flops=1e8,
    )
    glu_one, sig_one, msg_one = call(
        conv_one_body,
        [((2, 2, 8, 8, 16, 128), f32), ((2, 2, 8, 8, 16, 128), f32), ((16, 128), f32)],
        (field, wide_w, mask),
        "conv_one",
        flops=4.3e9,
        smem=0,
    )
    shared_one = share(msg_one)
    hidden, stat_one = call(
        make_hidden_body(entries),
        [((8, 2, 8, 2, 16, 128), bf16), ((2, 16, 128), f32)],
        (glu_one, mask, gains, *shared_one),
        "hidden",
        flops=1e7,
        smem=0,
    )
    hidden = hidden.reshape(16, 16, 16, 128)
    hidden_other = swap_with(hidden, "chan", 2)

    skip_full = lax.all_gather(skip_feature, "chan", axis=1, tiled=True)
    squeezer_full = lax.all_gather(squeezer, "batch", axis=2, tiled=True)
    pooled = skip_full.reshape(samples, -1, 16)
    squeezed = jnp.einsum("toc,bct->bo", squeezer_full, pooled, preferred_element_type=f32)
    squeeze_sig = jax.nn.sigmoid(squeezed)
    swish = (squeezed * squeeze_sig).astype(bf16)
    swish_full = lax.all_gather(swish, "chan", axis=1, tiled=True)
    exciter_full = lax.all_gather(exciter, "batch", axis=1, tiled=True)
    excited = jnp.einsum("oc,bc->bo", exciter_full, swish_full, preferred_element_type=f32)
    gate = jax.nn.sigmoid(excited)
    gate_mine = natural(half(gate, core), swap_with(half(gate, 1 - core), "chan", 1), 1)
    pull = jnp.stack([weight, gate_mine], axis=0)

    u_keep = half(upstream, core)
    u_other = swap_with(half(upstream, 1 - core), "chan", 1)
    (up,) = call(
        upstream_body,
        [((16, 16, 16, 128), bf16)],
        (idx, u_keep, u_other),
        "upstream_turned",
        scratch=[pltpu.VMEM((16, 256, 128), bf16)],
        flops=1.2e9,
    )
    fine_w, _ = call(
        refiner_body,
        [((9, 256, 256), bf16), ((128, 256), bf16)],
        (idx, *fine_own, *fine_other),
        "refiner_taps",
        flops=1.3e9,
    )
    held, glu_two, sig_two, sums_two, msg_two = call(
        conv_two_body,
        [
            ((18, 18, 16, 256), bf16),
            ((16, 16, 16, 128), f32),
            ((16, 16, 16, 128), f32),
            ((3, 16, 128), f32),
            ((24, 128), f32),
        ],
        (hidden, hidden_other, fine_w, up, mask, pull),
        "conv_two",
        flops=4.9e9,
        smem=0,
    )
    shared_two = share(msg_two)
    grad_two, dh_own, dh_send, small_two, stat_two = call(
        make_back_two_body(entries),
        [
            ((18, 18, 16, 256), bf16),
            ((16, 16, 16, 128), bf16),
            ((16, 16, 16, 128), bf16),
            ((24, 128), f32),
            ((2, 16, 128), f32),
        ],
        (glu_two, sig_two, up, mask, pull, gains, sums_two, fine_w, *shared_two),
        "back_two",
        flops=4.9e9,
        smem=0,
    )
    dh_other = swap_with(dh_send, "chan", 2)
    out_own, out_send = call(
        output_body,
        [((16, 64, 256), bf16), ((16, 64, 256), bf16)],
        (idx, glu_two, stat_two, pull, gains),
        "output_turned",
        scratch=[pltpu.VMEM((16, 256, 128), bf16)],
        flops=1.2e9,
    )
    output = natural(out_own, swap_with(out_send, "chan", 1), 0)
    fine_keep, fine_send = call(
        refiner_grad_body,
        [((8, 5, 64, 128), bf16), ((8, 5, 64, 128), bf16)],
        (idx, grad_two, held),
        "refiner_grad",
        scratch=[pltpu.VMEM((9, 256, 256), bf16)],
        flops=6e9,
    )

    def scatter(keep, send, body, shape, name, unpack):
        total = (keep.astype(f32) + swap_with(send, "chan", 1).astype(f32)).astype(bf16)
        if eight:
            parts = [total[0]] + [swap_with(total[k], "batch", k) for k in range(1, 8)]
            return call(body, [(shape, f32)], parts, name, smem=0)[0]
        return unpack(total)

    def unpack_fine(total):
        v = total.reshape(8, 5, 64, 4, 32).transpose(1, 3, 2, 0, 4).reshape(20, 64, 256)[:18]
        v = v.reshape(9, 2, 64, 256).astype(f32)
        return lax.psum_scatter(v, "batch", scatter_dimension=3, tiled=True)

    def unpack_wide(total):
        v = total.reshape(8, 9, 64, 2, 64).transpose(1, 3, 2, 0, 4).reshape(9, 2, 64, 512)
        return lax.psum_scatter(v.astype(f32), "batch", scatter_dimension=3, tiled=True)

    refiner_sum = scatter(
        fine_keep, fine_send, refiner_sum_body, refiner.shape, "refiner_sum", unpack_fine
    )

    by_phase = (8, 2, 8, 2, 16, 128)
    dh_own, dh_other = dh_own.reshape(by_phase), dh_other.reshape(by_phase)
    (msg_three,) = call(
        first_sums_body,
        [((8, 128), f32)],
        (glu_one, dh_own, dh_other, mask, stat_one),
        "first_sums",
        flops=1e7,
        smem=0,
    )
    shared_three = share(msg_three)
    grad_one, small_one = call(
        make_back_one_body(entries),
        [((2, 2, 10, 10, 16, 256), bf16), ((8, 128), f32)],
        (glu_one, sig_one, dh_own, dh_other, mask, stat_one, gains, *shared_three),
        "back_one",
        flops=1e7,
        smem=0,
    )
    wide_keep, wide_send = call(
        widener_grad_body,
        [((8, 9, 64, 128), bf16), ((8, 9, 64, 128), bf16)],
        (idx, grad_one, field),
        "widener_grad",
        scratch=[pltpu.VMEM((4, 4, 256, 512), f32)],
        flops=4.3e9,
    )
    widener_sum = scatter(
        wide_keep, wide_send, widener_sum_body, widener.shape, "widener_sum", unpack_wide
    )
    blocks = call(
        input_back_body,
        [((16, 64, 128), bf16)] * 4,
        (idx, grad_one, wide_w),
        "input_back",
        scratch=[pltpu.VMEM((16, 64, 512), bf16)],
        flops=6e9,
    )
    got = [blocks[0]] + [swap_with(blocks[k], "chan", k) for k in range(1, 4)]
    input_grad = natural(
        got[0].astype(f32) + got[2].astype(f32), got[1].astype(f32) + got[3].astype(f32), 0
    )

    grad_gate = small_two[0:16]
    lo, hi = grad_gate[:, :64], grad_gate[:, 64:]
    keep, send = jnp.where(core == 0, lo, hi), jnp.where(core == 0, hi, lo)
    grad_gate = natural(keep, swap_with(send, "chan", 1), 0)
    grad_excited = (grad_gate * gate * (1.0 - gate)).astype(bf16)
    exciter_grad = jnp.einsum("bo,bc->oc", grad_excited, swish_full, preferred_element_type=f32)
    partial_swish = jnp.einsum("bo,oc->bc", grad_excited, exciter_full, preferred_element_type=f32)
    grad_swish = lax.psum_scatter(
        partial_swish.astype(bf16), "chan", scatter_dimension=1, tiled=True
    ).astype(f32)
    grad_squeezed = (grad_swish * squeeze_sig * (1.0 + squeezed * (1.0 - squeeze_sig))).astype(bf16)
    squeezer_grad = jnp.einsum("bo,bct->toc", grad_squeezed, pooled, preferred_element_type=f32)
    partial_pooled = jnp.einsum(
        "bo,toc->bct", grad_squeezed, squeezer_full, preferred_element_type=f32
    ).reshape(samples, -1, 128)
    skip_grad = lax.psum_scatter(
        partial_pooled.astype(bf16), "chan", scatter_dimension=1, tiled=True
    ).astype(f32)
    squeezer_sum = lax.psum_scatter(squeezer_grad, "batch", scatter_dimension=2, tiled=True)
    exciter_sum = lax.psum_scatter(exciter_grad, "batch", scatter_dimension=1, tiled=True)

    norms = jnp.concatenate([small_one[0:2], small_two[16:18]], axis=0)
    norm_grads = jnp.where(core == 0, norms[:, :64], norms[:, 64:])
    return (
        output,
        input_grad,
        skip_grad,
        widener_sum,
        refiner_sum,
        squeezer_sum,
        exciter_sum,
        norm_grads,
    )


def solution(mesh):
    placed = (
        P("batch", "chan", None),
        P("batch", "chan", None),
        P("batch"),
        P("batch"),
        P(None, None, "chan", "batch"),
        P(None, None, "chan", "batch"),
        P(None, "chan", "batch"),
        P("chan", "batch"),
        P("chan"),
        P("chan"),
        P("chan"),
        P("chan"),
        P("batch", "chan", None),
    )
    return jax.shard_map(
        on_device,
        mesh=mesh,
        in_specs=placed,
        out_specs=(
            P("batch", "chan", None),
            P("batch", "chan", None),
            P("batch", "chan", None),
            P(None, None, "chan", "batch"),
            P(None, None, "chan", "batch"),
            P(None, "chan", "batch"),
            P("chan", "batch"),
            P(None, "chan"),
        ),
        check_vma=False,
    )
```

```python
import jax
import jax.numpy as jnp
from jax import lax
from jax.experimental import pallas as pl
from jax.experimental.pallas import tpu as pltpu
from jax.sharding import PartitionSpec as P

MB = 4
epsilon = 1e-05
f32 = jnp.float32
bf16 = jnp.bfloat16
MIB = 2**20

NT = (((1,), (1,)), ((), ()))
TN = (((0,), (0,)), ((), ()))


def dot(a, b, dims=None):
    if dims is None:
        return jnp.dot(a, b, preferred_element_type=f32)
    return lax.dot_general(a, b, dims, preferred_element_type=f32)


class Traffic:
    def __init__(self, ins, outs, in_sems, out_sems, late):
        self.ins = [
            pltpu.make_async_copy(src, dst, in_sems.at[k]) for k, (src, dst) in enumerate(ins)
        ]
        self.outs, self.out_sems = outs, out_sems
        self.sent = {}
        for k, copy in enumerate(self.ins):
            copy.start()
        for k, copy in enumerate(self.ins):
            if k not in late:
                copy.wait()

    def need(self, *which):
        for k in which:
            self.ins[k].wait()

    def part(self, k, n, count):
        src, dst = self.outs[k]
        rows = src.shape[0] // count
        cut = pl.ds(n * rows, rows)
        return pltpu.make_async_copy(src.at[cut], dst.at[cut], self.out_sems.at[k, n])

    def send(self, k, n=0, count=1):
        self.sent[k] = count
        self.part(k, n, count).start()

    def finish(self):
        for k in range(len(self.outs)):
            if k not in self.sent:
                self.send(k)
        for k, count in self.sent.items():
            for n in range(count):
                self.part(k, n, count).wait()


def call(body, outs, args, name, scratch=(), smem=1, deps=(), late=(), plain=False):
    outs = [jax.ShapeDtypeStruct(shape, dtype) for shape, dtype in outs]
    args, deps = list(args), list(deps)
    big = len(args) - smem
    count = len(outs)
    anywhere, inside = pl.BlockSpec(memory_space=pl.ANY), pl.BlockSpec(memory_space=pltpu.VMEM)

    def kernel(*refs):
        refs = list(refs)
        scalars, refs = refs[:smem], refs[smem:]
        ins, refs = refs[:big], refs[big + len(deps) :]
        results, refs = refs[:count], refs[count:]
        if plain:
            body(*scalars, *ins, *results, *refs)
            return
        held, refs = refs[:big], refs[big:]
        made, refs = refs[:count], refs[count:]
        in_sems, out_sems = refs[0], refs[1]
        traffic = Traffic(
            list(zip(ins, held)), list(zip(made, results)), in_sems, out_sems, late
        )
        extra = (traffic,) if late else ()
        body(*extra, *scalars, *held, *made, *refs[2:])
        traffic.finish()

    own = []
    if not plain:
        own = [pltpu.VMEM(a.shape, a.dtype) for a in args[smem:]]
        own += [pltpu.VMEM(o.shape, o.dtype) for o in outs]
        own += [pltpu.SemaphoreType.DMA((big,)), pltpu.SemaphoreType.DMA((count, 8))]
    return pl.pallas_call(
        kernel,
        out_shape=outs,
        in_specs=[pl.BlockSpec(memory_space=pltpu.SMEM)] * smem
        + [inside if plain else anywhere] * big
        + [anywhere] * len(deps),
        out_specs=[inside if plain else anywhere] * count,
        scratch_shapes=own + list(scratch),
        compiler_params=pltpu.CompilerParams(
            vmem_limit_bytes=(16 if plain else 56) * MIB
        ),
        cost_estimate=pl.CostEstimate(flops=0, bytes_accessed=0, transcendentals=0),
        name=name,
    )(*args, *deps)


def after(value, *deps):
    return pl.pallas_call(
        lambda *refs: None,
        out_shape=jax.ShapeDtypeStruct(value.shape, value.dtype),
        in_specs=[pl.BlockSpec(memory_space=pl.ANY)] * (1 + len(deps)),
        out_specs=pl.BlockSpec(memory_space=pl.ANY),
        input_output_aliases={0: 0},
        name="after",
    )(value, *deps)


def iota(shape, dim):
    return lax.broadcasted_iota(jnp.int32, shape, dim)


def onehot(cond):
    return jnp.where(cond, 1.0, 0.0).astype(f32).astype(bf16)


def eye(n):
    return onehot(iota((n, n), 0) == iota((n, n), 1))


def sixteen_swap():
    r, q = iota((256, 256), 0), iota((256, 256), 1)
    return onehot(((r % 16) == (q // 16)) & ((r // 16) == (q % 16)))


def tree(parts):
    parts = list(parts)
    while len(parts) > 1:
        parts = [parts[n] + parts[n + 1] for n in range(0, len(parts), 2)]
    return parts[0]


def sigmoid(v):
    return 1.0 / (1.0 + jnp.exp(-v))


def pack_wide_body(w, out):
    packed = jnp.concatenate([w[:, 0], w[:, 1]], axis=-1)
    for k in range(8):
        out[k] = packed


def pack_fine_body(r, e, out):
    slots = [r[q // 2, q % 2] for q in range(18)] + [e[...], jnp.zeros_like(e[...])]
    for row in range(5):
        out[row] = jnp.concatenate(slots[4 * row : 4 * row + 4], axis=-1)
    out[5:] = jnp.zeros((3, 64, 128), bf16)


def fill_taps(core, own, other, out):
    for blocks, side in ((own, core), (other, 1 - core)):
        for half in range(2):
            rows = pl.ds(pl.multiple_of(half * 128 + side * 64, 64), 64)
            lanes = slice(half * 64, half * 64 + 64)
            for group in range(4):
                w = [
                    jnp.concatenate(
                        [blocks[2 * group][t][:, lanes], blocks[2 * group + 1][t][:, lanes]],
                        axis=-1,
                    ).astype(f32)
                    for t in range(9)
                ]
                down = {
                    (0, 0): w[0:3],
                    (0, 1): [w[3 + s] + w[6 + s] for s in range(3)],
                    (1, 0): [w[s] + w[3 + s] for s in range(3)],
                    (1, 1): w[6:9],
                }
                for a in range(2):
                    for u in range(2):
                        d = down[(a, u)]
                        across = {
                            (0, 0): d[0],
                            (0, 1): d[1] + d[2],
                            (1, 0): d[0] + d[1],
                            (1, 1): d[2],
                        }
                        for b in range(2):
                            for v in range(2):
                                out[
                                    a * 8 + b * 4 + u * 2 + v,
                                    rows,
                                    group * 128 : group * 128 + 128,
                                ] = across[(b, v)].astype(bf16)


def refiner_select(chip):
    r, q = iota((1024, 1024), 0), iota((1024, 1024), 1)
    channel = (r // 128) * 32 + r % 32
    return onehot((((r // 32) % 4) == (q // 256)) & ((channel ^ (chip * 128)) == (q % 256)))


def refiner_body(idx, own, other, out, ex):
    core, chip = idx[1], idx[2]
    select = refiner_select(chip)
    for blocks, side in ((own, core), (other, 1 - core)):
        rows = pl.multiple_of(side * 64, 64)
        raw = jnp.concatenate([blocks[k, :5].reshape(320, 128) for k in range(8)], axis=-1)
        got = dot(raw, select).astype(bf16)
        for q in range(18):
            piece = got[(q // 4) * 64 : (q // 4) * 64 + 64, (q % 4) * 256 : (q % 4) * 256 + 256]
            out[q // 2, pl.ds(rows + (q % 2) * 128, 64), :] = piece
        ex[pl.ds(rows, 64), :] = got[256:320, 512:768]


def feature_select(place):
    r, q = iota((512, 512), 0), iota((512, 512), 1)
    kept = r % 256
    return onehot((((kept // 64) ^ place) * 64 + kept % 64) * 2 + r // 256 == q)


def feature_body(idx, b0, b1, b2, b3, out, turned):
    ident = eye(128)

    def turn(s, carry):
        x = jnp.concatenate([b0[s], b1[s], b2[s], b3[s]], axis=0)
        t = dot(ident, x, NT).astype(bf16)
        turned[s] = jnp.concatenate([t[:64], t[64:]], axis=-1)
        return carry

    lax.fori_loop(0, 16, turn, 0, unroll=4)
    swap = sixteen_swap()
    select = feature_select(idx[0])
    zero = jnp.zeros((10, 16, 512), bf16)
    out[0] = zero
    out[9] = zero
    out[:, 0] = zero
    out[:, 9] = zero
    for block in range(4):
        a = turned[:, block * 16 : block * 16 + 16, :].reshape(256, 512)
        c = dot(dot(swap, a).astype(bf16), select).astype(bf16)
        out[1 + 2 * block : 3 + 2 * block, 1:9] = c.reshape(2, 8, 16, 512)


def input_back_body(io, idx, d, w, b0, b1, b2, b3, turned):
    swap = sixteen_swap()
    select = feature_select(idx[0])

    io.need(1)
    acc = None
    for a in range(2):
        for b in range(2):
            lhs = jnp.concatenate(
                [
                    d[a, b, 2 - u - a : 10 - u - a, 2 - v - b : 10 - v - b].reshape(1024, 256)
                    for u in range(2)
                    for v in range(2)
                ],
                axis=-1,
            )
            first = a * 8 + b * 4
            term = dot(lhs, w[first : first + 4].reshape(1024, 512))
            acc = term if acc is None else acc + term
    x = dot(acc.astype(bf16), select, NT).astype(bf16)
    for block in range(4):
        t = dot(swap, x[block * 256 : block * 256 + 256]).astype(bf16)
        turned[:, block * 16 : block * 16 + 16, :] = t.reshape(16, 16, 512)
    ident = eye(256)

    def turn(s, carry):
        t = turned[s]
        t = jnp.concatenate([t[:, :256], t[:, 256:]], axis=0)
        o = dot(ident, t, NT).astype(bf16)
        b0[s] = o[0:64]
        b1[s] = o[64:128]
        b2[s] = o[128:192]
        b3[s] = o[192:256]
        return carry

    lax.fori_loop(0, 16, turn, 0, unroll=4)


def upstream_body(idx, own, other, out, turned):
    first = idx[1] == 0
    ident = eye(256)

    def turn(s, carry):
        p, q = own[s], other[s]
        lo = jnp.where(first, p, q)
        hi = jnp.where(first, q, p)
        turned[s] = dot(ident, jnp.concatenate([lo, hi], axis=0), NT).astype(bf16)
        return carry

    lax.fori_loop(0, 16, turn, 0, unroll=4)
    swap = sixteen_swap()

    def mix(y, carry):
        a = turned[:, pl.ds(pl.multiple_of(y * 16, 16), 16), :].reshape(256, 128)
        out[y] = dot(swap, a).astype(bf16).reshape(16, 16, 128)
        return carry

    lax.fori_loop(0, 16, mix, 0, unroll=4)


def over_samples(mask, values):
    return jnp.concatenate(
        [jnp.sum(mask[m] * values, axis=0, keepdims=True) for m in range(MB)], axis=0
    )


def per_sample(mask, rows):
    return sum(mask[m] * rows[m : m + 1] for m in range(MB))


def local_stats(mask, mean_s, squares_s):
    ones = jnp.ones_like(mean_s)
    n = over_samples(mask, ones) * 256.0
    mean = over_samples(mask, mean_s) * 256.0 / jnp.maximum(n, 1.0)
    gap = mean_s - per_sample(mask, mean)
    squares = over_samples(mask, squares_s + 256.0 * gap * gap)
    return n, mean, squares


def total_stats(messages, entries):
    parts = [(g[0:4], g[4:8], g[8:12]) for g in messages]
    mean = tree([n * m for n, m, _ in parts]) / entries
    squares = tree([q + n * (m - mean) * (m - mean) for n, m, q in parts])
    inverse = lax.rsqrt(squares / entries + epsilon)
    return mean, inverse


def message_list(refs):
    return [ref[c] for ref in refs for c in range(ref.shape[0])]


def conv_one_body(io, idx, own, other, x, mask, gap, logit, base, msg, w, glu):
    fill_taps(idx[1], own, other, w)
    io.send(4)
    io.need(2, 3)
    total = jnp.zeros((16, 128), f32)
    for a in range(2):
        for b in range(2):
            kept = []
            for u in range(2):
                for v in range(2):
                    kept.append(x[u + a : u + a + 8, v + b : v + b + 8].reshape(1024, 512))
            first = a * 8 + b * 4
            rhs = jnp.concatenate([w[first + n] for n in range(4)], axis=-1)
            c = dot(jnp.concatenate(kept, axis=-1), rhs, NT)
            g = (c[:, :128] * sigmoid(c[:, 128:])).reshape(8, 8, 16, 128)
            logit[:, a, :, b] = c[:, 128:].reshape(8, 8, 16, 128).astype(bf16)
            glu[a, b] = g
            total = total + jnp.sum(g, axis=(0, 1))
    io.send(1)
    mean_s = total * (1.0 / 256.0)
    base[...] = mean_s
    io.send(2)

    def spread(i, acc):
        for a in range(2):
            for b in range(2):
                d = glu[a, b, i] - mean_s[None]
                gap[i, a, :, b] = d.astype(bf16)
                acc = acc + jnp.sum(d * d, axis=0)
        io.send(0, i, 8)
        return acc

    squares = lax.fori_loop(0, 8, spread, jnp.zeros((16, 128), f32))
    n, mean, squares = local_stats(mask[...], mean_s, squares)
    msg[0:4] = n
    msg[4:8] = mean
    msg[8:12] = squares
    msg[12:16] = jnp.zeros((4, 128), f32)


def make_scale_body(entries):
    def body(mask, gains, base, messages, line, stat):
        mean, inverse = total_stats(message_list([messages]), entries)
        m = mask[...]
        mean_s, inverse_s = per_sample(m, mean), per_sample(m, inverse)
        stat[0] = base[...] - mean_s
        stat[1] = inverse_s
        scale = inverse_s * gains[0:1]
        line[0] = scale
        line[1] = (base[...] - mean_s) * scale + gains[1:2]

    return body


def conv_two_body(io, own, other, line, line_other, w, up, held, glu, logit, sums):
    zero = jnp.zeros((18, 16, 256), bf16)
    held[0] = zero
    held[17] = zero
    held[:, 0] = zero
    held[:, 17] = zero

    def fill(y, carry):
        for gap, scale, lanes in ((own, line, 0), (other, line_other, 128)):
            h = gap[y].astype(f32) * scale[0] + scale[1]
            held[y + 1, 1:17, :, lanes : lanes + 128] = h.astype(bf16)
        return carry

    lax.fori_loop(0, 16, fill, 0)
    io.send(0)
    io.need(4)

    def rows(step, total):
        y = step * 4
        lhs = jnp.concatenate(
            [
                held[pl.ds(y + t // 3, 4), t % 3 : t % 3 + 16].reshape(1024, 256)
                for t in range(9)
            ],
            axis=-1,
        )
        rhs = jnp.concatenate([w[t] for t in range(9)], axis=-1)
        c = dot(lhs, rhs, NT)
        g = (c[:, :128] * sigmoid(c[:, 128:])).reshape(4, 16, 16, 128)
        logit[pl.ds(y, 4)] = c[:, 128:].reshape(4, 16, 16, 128).astype(bf16)
        glu[pl.ds(y, 4)] = g
        io.send(1, step, 4)
        io.send(2, step, 4)
        return total + jnp.sum(g, axis=(0, 1))

    total = lax.fori_loop(0, 4, rows, jnp.zeros((16, 128), f32))
    mean_s = total * (1.0 / 256.0)

    io.need(5)

    def spread(y, acc):
        gap = glu[y] - mean_s[None]
        u = up[y].astype(f32)
        return (
            acc[0] + jnp.sum(gap * gap, axis=0),
            acc[1] + jnp.sum(u, axis=0),
            acc[2] + jnp.sum(u * gap, axis=0),
        )

    none = jnp.zeros((16, 128), f32)
    squares, plain, cross = lax.fori_loop(0, 16, spread, (none, none, none))
    sums[0] = mean_s
    sums[1] = plain
    sums[2] = cross
    sums[3] = squares


def make_back_two_body(entries):
    def body(io, glu, logit, up, mask, pull, gains, sums, w, gap, gap_other, messages, *outs):
        grad, own, other, small, stat, mine = outs
        messages = message_list([messages])
        mean, inverse = total_stats(messages, entries)
        plain = tree([g[12:16] for g in messages])
        cross = inverse * tree([g[16:20] + g[12:16] * (g[4:8] - mean) for g in messages])
        m = mask[...]
        mean_s, inverse_s = per_sample(m, mean), per_sample(m, inverse)
        gain, shift = gains[2:3], gains[3:4]
        stat[0] = mean_s
        stat[1] = inverse_s
        weight, gate = pull[0], pull[1]
        centred = sums[2] + sums[1] * (sums[0] - mean_s)
        small[2] = weight * (gain * inverse_s * centred + shift * sums[1])
        mine[2, 0:1] = jnp.sum(cross, axis=0, keepdims=True)
        mine[2, 1:2] = jnp.sum(plain, axis=0, keepdims=True)
        mine[2, 2:] = jnp.zeros((14, 128), f32)
        plain_s = per_sample(m, plain) * (1.0 / entries)
        cross_s = per_sample(m, cross) * (1.0 / entries)
        scale = inverse_s * gain
        factor = weight * gate
        io.need(0, 1, 2)
        zero = jnp.zeros((18, 16, 256), bf16)
        grad[0] = zero
        grad[17] = zero
        grad[:, 0] = zero
        grad[:, 17] = zero

        def step(y, carry):
            g = glu[y]
            s = sigmoid(logit[y].astype(f32))
            hat = (g - mean_s) * inverse_s
            d = scale * (up[y].astype(f32) * factor - plain_s - hat * cross_s)
            grad[y + 1, 1:17, :, 0:128] = (d * s).astype(bf16)
            grad[y + 1, 1:17, :, 128:256] = (d * g * (1.0 - s)).astype(bf16)
            return carry

        lax.fori_loop(0, 16, step, 0)
        io.send(0)
        io.need(7, 8, 9)

        def rows(step, acc):
            y = step * 4
            lhs = jnp.concatenate(
                [
                    grad[pl.ds(y + 2 - t // 3, 4), 2 - t % 3 : 18 - t % 3].reshape(1024, 256)
                    for t in range(9)
                ],
                axis=-1,
            )
            c = dot(lhs, w[...].reshape(2304, 256)).astype(bf16)
            out = []
            for ref, at, lanes in ((own, gap, 0), (other, gap_other, 128)):
                d = c[:, lanes : lanes + 128].reshape(4, 16, 16, 128)
                ref[pl.ds(y, 4)] = d
                io.send(1 if lanes == 0 else 2, step, 4)
                d = d.astype(f32)
                out.append(jnp.sum(d, axis=(0, 1)))
                out.append(jnp.sum(d * at[pl.ds(y, 4)].astype(f32), axis=(0, 1)))
            return tuple(p + q for p, q in zip(acc, out))

        none = jnp.zeros((16, 128), f32)
        mine[0], mine[1], small[0], small[1] = lax.fori_loop(0, 4, rows, (none,) * 4)

    return body


def output_part(idx, glu, stat, pull, gains, own, other, turned):
    swap = sixteen_swap()
    mean_s, inverse_s = stat[0], stat[1]
    gain, shift = gains[2:3], gains[3:4]
    gate = pull[1]

    def step(y, carry):
        o = (((glu[y] - mean_s) * inverse_s) * gain + shift) * gate
        o = dot(swap, o.astype(bf16).reshape(256, 128)).astype(bf16)
        turned[:, pl.ds(pl.multiple_of(y * 16, 16), 16), :] = o.reshape(16, 16, 128)
        return carry

    lax.fori_loop(0, 16, step, 0, unroll=4)
    ident = eye(128)
    first = idx[1] == 0

    def turn(s, carry):
        t = dot(ident, turned[s], NT).astype(bf16)
        own[s] = jnp.where(first, t[:64], t[64:])
        other[s] = jnp.where(first, t[64:], t[:64])
        return carry

    lax.fori_loop(0, 16, turn, 0, unroll=4)


def refiner_grad_body(
    io, idx, grad, held, glu, stat, pull, gains, own, other, out_own, out_other, work, turned
):
    core, chip = idx[1], idx[2]

    def tap(t, carry):
        d = grad[1:17, 1:17].reshape(4096, 256)
        h = held[pl.ds(t // 3, 16), pl.ds(t % 3, 16)].reshape(4096, 256)
        work[t] = dot(d, h, TN).astype(bf16)
        return carry

    lax.fori_loop(0, 9, tap, 0)
    select = refiner_select(chip)
    for out, side in ((own, core), (other, 1 - core)):
        start = pl.multiple_of(side * 64, 64)
        rows = []
        for row in range(5):
            pieces = []
            for q in range(4 * row, 4 * row + 4):
                if q < 18:
                    pieces.append(work[q // 2, pl.ds(start + (q % 2) * 128, 64), :])
                else:
                    pieces.append(jnp.zeros((64, 256), bf16))
            rows.append(jnp.concatenate(pieces, axis=-1))
        got = dot(jnp.concatenate(rows, axis=0), select, NT).astype(bf16)
        for k in range(8):
            out[k] = got[:, k * 128 : k * 128 + 128].reshape(5, 64, 128)
    io.send(0)
    io.send(1)
    io.need(2, 3, 4, 5)
    output_part(idx, glu, stat, pull, gains, out_own, out_other, turned)


def refiner_sum_body(parts, out):
    total = tree([parts[k, :320].astype(f32) for k in range(8)])
    for q in range(18):
        rows = slice((q // 4) * 64, (q // 4) * 64 + 64)
        out[q // 2, q % 2] = total[rows, (q % 4) * 32 : (q % 4) * 32 + 32]


def first_sums_body(mine, theirs, mask, stat, msg):
    m = mask[...]
    plain = mine[0] + theirs[0]
    cross = mine[1] + theirs[1] + stat[0] * plain
    msg[0:4] = over_samples(m, plain)
    msg[4:8] = over_samples(m, cross * stat[1])


def make_back_one_body(entries):
    def body(
        io,
        idx,
        gap,
        logit,
        base,
        own,
        other,
        mask,
        stat,
        gains,
        messages,
        x,
        grad,
        small,
        keep,
        send,
        work,
    ):
        messages = message_list([messages])
        plain = tree([g[0:4] for g in messages])
        cross = tree([g[4:8] for g in messages])
        small[0:1] = jnp.sum(cross, axis=0, keepdims=True)
        small[1:2] = jnp.sum(plain, axis=0, keepdims=True)
        small[2:8] = jnp.zeros((6, 128), f32)
        io.send(1)
        m = mask[...]
        plain_s = per_sample(m, plain) * (1.0 / entries)
        cross_s = per_sample(m, cross) * (1.0 / entries)
        shift_s, inverse_s = stat[0], stat[1]
        mean = base[...]
        scale = inverse_s * gains[0:1]
        zero = jnp.zeros((10, 16, 256), bf16)
        for a in range(2):
            for b in range(2):
                grad[a, b, 0] = zero
                grad[a, b, 9] = zero
                grad[a, b, :, 0] = zero
                grad[a, b, :, 9] = zero

        def step(i, carry):
            for a in range(2):
                for b in range(2):
                    g = gap[i, a, :, b].astype(f32)
                    s = sigmoid(logit[i, a, :, b].astype(f32))
                    hat = (g + shift_s) * inverse_s
                    g = g + mean
                    d = own[i, a, :, b].astype(f32) + other[i, a, :, b].astype(f32)
                    d = scale * (d - plain_s - hat * cross_s)
                    grad[a, b, i + 1, 1:9, :, 0:128] = (d * s).astype(bf16)
                    grad[a, b, i + 1, 1:9, :, 128:256] = (d * g * (1.0 - s)).astype(bf16)
            return carry

        lax.fori_loop(0, 8, step, 0)
        io.send(0)
        io.need(9)
        widener_grad(idx[1], grad, x, keep, send, work)

    return body


def widener_grad(core, grad, x, own, other, work):
    def phase(n, carry):
        a, b = n // 2, n % 2
        d = grad[a, b, 1:9, 1:9].reshape(1024, 256)
        for u in range(2):
            for v in range(2):
                f = x[pl.ds(u + a, 8), pl.ds(v + b, 8)].reshape(1024, 512)
                work[n, 2 * u + v] = dot(d, f, TN)
        return carry

    lax.fori_loop(0, 4, phase, 0)
    source = {0: (0, 0), 1: (1, 0), 2: (1, 1)}
    for out, side in ((own, core), (other, 1 - core)):
        start = pl.multiple_of(side * 64, 64)
        for pair in range(4):
            lanes = slice(pair * 128, pair * 128 + 128)
            for r in range(3):
                for s in range(3):
                    both = []
                    for half in range(2):
                        rows = pl.ds(start + half * 128, 64)
                        both.append(
                            sum(
                                work[2 * a + b, 2 * source[r][a] + source[s][b], rows, lanes]
                                for a in range(2)
                                for b in range(2)
                            )
                        )
                    first, second = both
                    out[2 * pair, 3 * r + s] = jnp.concatenate(
                        [first[:, :64], second[:, :64]], axis=-1
                    ).astype(bf16)
                    out[2 * pair + 1, 3 * r + s] = jnp.concatenate(
                        [first[:, 64:], second[:, 64:]], axis=-1
                    ).astype(bf16)


def pair_sum_body(own, other, out):
    out[...] = (own[...].astype(f32) + other[...].astype(f32)).astype(bf16)


def widener_sum_body(parts, out):
    for t in range(9):
        total = tree([parts[k, t].astype(f32) for k in range(8)])
        out[t, 0] = total[:, :64]
        out[t, 1] = total[:, 64:]


def skip_quarter_body(idx, skip, out):
    rows = pl.ds(pl.multiple_of(idx[0] * 8, 8), 8)
    for i in range(8):
        out[i] = skip[rows, i * 16 : i * 16 + 16, :]


def squeeze_body(skip, kernels, msg, kept, out, rows):
    rows[...] = skip[...].astype(f32).reshape(1024, 128)
    for k in range(16):
        kept[:, k * 128 : k * 128 + 128] = rows[pl.ds(k, 64, stride=16), :].astype(bf16)
    part = dot(kept[...], kernels[...], NT)
    for i in range(8):
        for c in range(2):
            out[2 * i + c, 0:16] = msg[...]
            out[2 * i + c, 16:24] = part[i * 8 : i * 8 + 8, :128]
            out[2 * i + c, 24:32] = part[i * 8 : i * 8 + 8, 128:]


def part_sum_body(idx, parts, out):
    core = idx[1]
    out[:, :128] = tree([parts[2 * k + core, 16:24] for k in range(8)])
    out[:, 128:] = tree([parts[2 * k + core, 24:32] for k in range(8)])


def own_first(v, chip):
    return jnp.where(chip == 0, v, jnp.concatenate([v[:, 128:], v[:, :128]], axis=-1))


def gate_body(idx, s0, s1, s2, s3, ex, weight, out, squeezed):
    j, core, chip = idx[0], idx[1], idx[2]
    for n, part in enumerate((s0, s1, s2, s3)):
        squeezed[pl.ds(pl.multiple_of((j ^ n) * 8, 8), 8), :] = part[...]
    mine = squeezed[pl.ds(pl.multiple_of(core * 16, 16), 16), :]
    excited = dot(own_first(mine * sigmoid(mine), chip).astype(bf16), ex[...], NT)
    out[0] = weight[...]
    out[1] = sigmoid(excited)


def message_two_body(mask, pull, sums, msg):
    mean_s, plain, cross = sums[0], sums[1], sums[2]
    m = mask[...]
    n, mean, squares = local_stats(m, mean_s, sums[3])
    factor = pull[0] * pull[1]
    msg[0:4] = n
    msg[4:8] = mean
    msg[8:12] = squares
    msg[12:16] = over_samples(m, factor * plain)
    msg[16:20] = over_samples(m, factor * (cross + plain * (mean_s - per_sample(m, mean))))
    msg[20:24] = jnp.zeros((4, 128), f32)


def excite_back_body(idx, g0, g1, squeezed, ex_own, ex_other, fine, recv, vectors, out):
    chip = idx[2]
    s = squeezed[...]
    sigm = sigmoid(s)
    swish = (s * sigm).astype(bf16)
    mine = own_first(ex_own[...].astype(f32), chip)
    theirs = own_first(ex_other[...].astype(f32), 1 - chip)
    ex = jnp.where(
        chip == 0, jnp.concatenate([mine, theirs], axis=0), jnp.concatenate([theirs, mine], axis=0)
    ).astype(bf16)
    gate = sigmoid(dot(swish, ex, NT))
    core = idx[1]
    rows = []
    for half in range(2):
        own = jnp.where(core == half, g0[0], g1[0])
        other = jnp.where(core == half, g0[1], g1[1])
        lo, hi = jnp.where(chip == 0, own, other), jnp.where(chip == 0, other, own)
        rows.append(jnp.concatenate([lo, hi], axis=-1))
    grad_gate = jnp.concatenate(rows, axis=0)
    d_excited = (grad_gate * gate * (1.0 - gate)).astype(bf16)
    d_swish = dot(d_excited, ex)
    d_squeezed = d_swish * (sigm * (1.0 + s * (1.0 - sigm)))
    j = idx[0]
    pick_out = onehot(iota((256, 64), 0) == iota((256, 64), 1) + j * 64)
    both = jnp.concatenate(
        [dot(d_squeezed.astype(bf16), pick_out), dot(d_excited, pick_out)], axis=-1
    ).astype(bf16)
    vectors[...] = both
    pick_in = onehot((iota((256, 1024), 0) // 32 == iota((256, 1024), 1) // 128)
                     & (iota((256, 1024), 0) % 32 == iota((256, 1024), 1) % 128))
    picked = dot(swish, pick_in).astype(bf16)
    total = (fine[...].astype(f32) + recv[...].astype(f32)).astype(bf16)
    out[:, :320] = total.reshape(8, 320, 128)
    for k in range(8):
        out[k, 320:352] = both
        out[k, 352:384] = picked[:, k * 128 : k * 128 + 128]


def quarters_first(v):
    v = v.astype(f32)
    return jnp.concatenate(
        [v[i * 32 + q * 8 : i * 32 + q * 8 + 8] for q in range(4) for i in range(8)], axis=0
    )


def squeeze_back_body(parts, skips, ex_grad, sq_grad):
    vectors = jnp.concatenate([parts[k, 320:352] for k in range(8)], axis=0)
    swish = jnp.concatenate([parts[k, 352:384] for k in range(8)], axis=0)
    ex_grad[...] = dot(vectors, swish, TN)[64:, :32]
    sq_grad[...] = dot(quarters_first(vectors).astype(bf16), skips[...], TN)[:64]


def skip_back_body(idx, vectors, kernels, keep, send, rows):
    d = vectors[:, :64]
    for i in range(8):
        pooled = dot(d, kernels[i * 64 : i * 64 + 64, :])
        for k in range(16):
            rows[:, i * 16 + k, :] = pooled[:, k * 128 : k * 128 + 128]
    at = idx[2] * 64
    keep[...] = rows[:, pl.ds(pl.multiple_of(at, 64), 64), :].astype(bf16)
    send[...] = rows[:, pl.ds(pl.multiple_of(64 - at, 64), 64), :].astype(bf16)


def skip_add_body(idx, own, other, keep, send):
    first = idx[1] == 0
    total = own[...].astype(f32) + other[...].astype(f32)
    lo, hi = total[:, :32], total[:, 32:]
    keep[...] = jnp.where(first, lo, hi)
    send[...] = jnp.where(first, hi, lo).astype(bf16)


def skip_last_body(own, other, out):
    out[...] = own[...] + other[...].astype(f32)


def swap_with(v, axis, k):
    return lax.ppermute(v, axis, [(n, n ^ k) for n in range(lax.axis_size(axis))])


def on_device(
    features,
    skip_feature,
    section_ids,
    micro_ids,
    widener,
    refiner,
    squeezer,
    exciter,
    gain_one,
    bias_one,
    gain_two,
    bias_two,
    upstream,
):
    nb = lax.axis_size("batch")
    eight = nb == 8
    samples = features.shape[0]
    entries = float(samples * nb // MB * 256)
    i = lax.axis_index("batch")
    j = lax.axis_index("chan")
    core, chip = j % 2, j // 2
    idx = jnp.stack([j, core, chip, i]).astype(jnp.int32)

    def half(v, which):
        return lax.dynamic_slice_in_dim(v, which * 16, 16, axis=0)

    def natural(own, other, axis):
        return jnp.where(
            core == 0,
            jnp.concatenate([own, other], axis=axis),
            jnp.concatenate([other, own], axis=axis),
        )

    def over_batch(v):
        return lax.all_to_all(v, "batch", 0, 0, tiled=True)

    f_keep, f_send = half(features, core), half(features, 1 - core)
    f_blocks = [f_keep] + [
        swap_with(f_send if k % 2 else f_keep, "chan", k) for k in range(1, 4)
    ]
    if eight:
        (wide,) = call(
            pack_wide_body, [((8, 9, 64, 128), bf16)], (widener,), "pack_wide", smem=0, plain=True
        )
        wide_own = over_batch(wide)
    else:
        w_all = lax.all_gather(widener, "batch", axis=3, tiled=True)
        wide_own = w_all.reshape(9, 2, 64, 8, 64).transpose(3, 0, 2, 1, 4).reshape(8, 9, 64, 128)

    gains = jnp.stack([gain_one, bias_one, gain_two, bias_two], axis=0)
    gains = natural(gains, swap_with(gains, "chan", 1), 1)
    ids = half(micro_ids, core)
    mask = jnp.broadcast_to(
        (ids[None, :, None] == jnp.arange(MB, dtype=jnp.int32)[:, None, None]).astype(f32),
        (MB, 16, 128),
    )
    weight_of = jnp.where(section_ids == 0, 1.0, jnp.where(section_ids == 1, 2.0, 4.0)).astype(f32)
    weight = jnp.broadcast_to(half(weight_of, core)[:, None], (16, 128))

    groups = [[n * 4 + 2 * x + c for n in range(nb) for c in range(2)] for x in range(2)]

    def exchange(copies):
        return lax.all_to_all(
            copies, ("batch", "chan"), 0, 0, tiled=True, axis_index_groups=groups
        )

    def share(msg):
        if eight:
            return exchange(jnp.broadcast_to(msg, (16,) + msg.shape))
        pair = jnp.stack([msg, swap_with(msg, "chan", 1)], axis=0)
        return lax.all_gather(pair, "batch").reshape((-1,) + msg.shape)

    u_keep = half(upstream, core)
    u_other = swap_with(half(upstream, 1 - core), "chan", 1)
    (up,) = call(
        upstream_body,
        [((16, 16, 16, 128), bf16)],
        (idx, u_keep, u_other),
        "upstream_turned",
        scratch=[pltpu.VMEM((16, 256, 128), bf16)],
    )
    (field,) = call(
        feature_body,
        [((10, 10, 16, 512), bf16)],
        (idx, *f_blocks),
        "features_turned",
        scratch=[pltpu.VMEM((16, 64, 512), bf16)],
        deps=(up,),
    )
    if eight:
        skip_full = lax.all_gather(skip_feature, "chan", axis=1, tiled=True)
        flat = squeezer.reshape(16, 64, 16, 8).transpose(1, 2, 3, 0).reshape(64, 2048)
        squeezer_whole = lax.all_gather(flat, "chan", axis=0, tiled=True)
        wide_own = after(wide_own, field, skip_full)

        (quarter,) = call(
            skip_quarter_body,
            [((8, 8, 16, 128), bf16)],
            (idx, skip_full),
            "skip_quarter", plain=True,
            deps=(wide_own,),
        )
        quarter = over_batch(quarter)
        (fine,) = call(
            pack_fine_body,
            [((8, 64, 128), bf16)],
            (refiner, exciter),
            "pack_fine",
            smem=0, plain=True,
            deps=(wide_own,),
        )
        fine_own = lax.all_gather(fine, "batch")
    else:
        r_all = lax.all_gather(refiner, "batch", axis=3, tiled=True)
        e_all = lax.all_gather(exciter, "batch", axis=1, tiled=True)
        r_all = jnp.concatenate(
            [r_all.reshape(18, 64, 256), e_all[None], jnp.zeros((1, 64, 256), bf16)], axis=0
        )
        r_all = r_all.reshape(5, 4, 64, 8, 32).transpose(3, 0, 2, 1, 4).reshape(8, 5, 64, 128)
        fine_own = jnp.pad(r_all, ((0, 0), (0, 3), (0, 0), (0, 0)))

    wide_other = swap_with(wide_own, "chan", 1)
    gap, logit_one, base, msg_one, wide_w = call(
        conv_one_body,
        [
            ((8, 2, 8, 2, 16, 128), bf16),
            ((8, 2, 8, 2, 16, 128), bf16),
            ((16, 128), f32),
            ((16, 128), f32),
            ((16, 256, 512), bf16),
        ],
        (idx, wide_own, wide_other, field, mask),
        "conv_one",
        scratch=[pltpu.VMEM((2, 2, 8, 8, 16, 128), f32)],
        late=(2, 3),
    )
    flat_field = (16, 16, 16, 128)
    gap_other = swap_with(gap, "chan", 2).reshape(flat_field)

    if eight:
        skips, payload = call(
            squeeze_body,
            [((64, 2048), bf16), ((16, 32, 128), f32)],
            (quarter, squeezer_whole, msg_one),
            "squeeze",
            scratch=[pltpu.VMEM((1024, 128), f32)],
            smem=0,
            plain=True,
        )
        shared_one = exchange(payload)
    else:
        shared_one = share(msg_one)
    shared_one = after(shared_one, gap_other)
    if eight:
        (part,) = call(
            part_sum_body, [((8, 256), f32)], (idx, shared_one), "part_sum", plain=True
        )
    line, stat_one = call(
        make_scale_body(entries),
        [((2, 16, 128), f32), ((2, 16, 128), f32)],
        (mask, gains, base, shared_one),
        "scale", plain=True,
        smem=0,
    )
    fine_own = after(fine_own, shared_one)
    fine_other = swap_with(fine_own, "chan", 1)
    fine_w, exciter_own = call(
        refiner_body,
        [((9, 256, 256), bf16), ((128, 256), bf16)],
        (idx, fine_own, fine_other),
        "refiner_taps", plain=True,
    )
    if eight:
        line_other, part_other = swap_with(line, "chan", 2), swap_with(part, "chan", 2)
        squeezed = (part, swap_with(part, "chan", 1), part_other, swap_with(part_other, "chan", 1))
    else:
        line_other = swap_with(line, "chan", 2)

    held, glu_two, logit_two, sums_two = call(
        conv_two_body,
        [
            ((18, 18, 16, 256), bf16),
            ((16, 16, 16, 128), f32),
            ((16, 16, 16, 128), bf16),
            ((4, 16, 128), f32),
        ],
        (gap.reshape(flat_field), gap_other, line, line_other, fine_w, up),
        "conv_two",
        smem=0,
        late=(4, 5),
    )
    if eight:
        pull, squeezed = call(
            gate_body,
            [((2, 16, 128), f32), ((32, 256), f32)],
            (idx, *squeezed, exciter_own, weight),
            "gate", plain=True,
        )
    else:
        skip_full = lax.all_gather(skip_feature, "chan", axis=1, tiled=True)
        squeezer_full = lax.all_gather(squeezer, "batch", axis=2, tiled=True)
        pooled = skip_full.reshape(samples, -1, 16)
        squeezed = jnp.einsum("toc,bct->bo", squeezer_full, pooled, preferred_element_type=f32)
        squeeze_sig = jax.nn.sigmoid(squeezed)
        swish = (squeezed * squeeze_sig).astype(bf16)
        swish_full = lax.all_gather(swish, "chan", axis=1, tiled=True)
        exciter_full = lax.all_gather(exciter, "batch", axis=1, tiled=True)
        excited = jnp.einsum("oc,bc->bo", exciter_full, swish_full, preferred_element_type=f32)
        gate = jax.nn.sigmoid(excited)
        gate_mine = natural(half(gate, core), swap_with(half(gate, 1 - core), "chan", 1), 1)
        pull = jnp.stack([weight, gate_mine], axis=0)
    (msg_two,) = call(
        message_two_body, [((24, 128), f32)], (mask, pull, sums_two), "message_two", plain=True, smem=0
    )
    shared_two = share(msg_two)
    if eight:
        flats = lax.all_gather(after(flat, shared_two), "batch", axis=0, tiled=True)
    grad_two, dh_own, dh_send, small, stat_two, mine = call(
        make_back_two_body(entries),
        [
            ((18, 18, 16, 256), bf16),
            ((16, 16, 16, 128), bf16),
            ((16, 16, 16, 128), bf16),
            ((3, 16, 128), f32),
            ((2, 16, 128), f32),
            ((3, 16, 128), f32),
        ],
        (
            glu_two,
            logit_two,
            up,
            mask,
            pull,
            gains,
            sums_two,
            fine_w,
            gap.reshape(flat_field),
            gap_other,
            shared_two,
        ),
        "back_two",
        smem=0,
        late=(0, 1, 2, 7, 8, 9),
    )
    theirs = swap_with(small, "chan", 2)
    dh_other = swap_with(after(dh_send, theirs), "chan", 2)
    (msg_three,) = call(
        first_sums_body, [((8, 128), f32)], (mine, theirs, mask, stat_one), "first_sums", plain=True, smem=0
    )
    shared_three = share(msg_three)
    fine_keep, fine_send, out_own, out_send = call(
        refiner_grad_body,
        [
            ((8, 5, 64, 128), bf16),
            ((8, 5, 64, 128), bf16),
            ((16, 64, 256), bf16),
            ((16, 64, 256), bf16),
        ],
        (idx, grad_two, held, glu_two, stat_two, pull, gains),
        "refiner_grad",
        scratch=[pltpu.VMEM((9, 256, 256), bf16), pltpu.VMEM((16, 256, 128), bf16)],
        late=(2, 3, 4, 5),
    )
    output = natural(out_own, swap_with(out_send, "chan", 1), 0)
    fine_recv = swap_with(after(fine_send, shared_three), "chan", 1)

    def pair(keep, recv, name):
        return call(pair_sum_body, [(keep.shape, bf16)], (keep, recv), name, smem=0)[0]

    if eight:
        both = jnp.stack([small[2], theirs[2]], axis=0)
        vectors, combined = call(
            excite_back_body,
            [((32, 128), bf16), ((8, 384, 128), bf16)],
            (
                idx,
                both,
                swap_with(both, "chan", 1),
                squeezed,
                exciter_own,
                swap_with(exciter_own, "chan", 2),
                fine_keep,
                fine_recv,
            ),
            "excite_back",
            deps=(shared_three,),
        )
        parts = over_batch(combined)
        ready = (combined, out_own)
    else:
        refiner_pair = pair(fine_keep, fine_recv, "refiner_pair")
        ready = (refiner_pair, out_own)
        v = refiner_pair.reshape(8, 5, 64, 4, 32).transpose(1, 3, 2, 0, 4).reshape(20, 64, 256)
        v = v[:18].reshape(9, 2, 64, 256).astype(f32)
        refiner_sum = lax.psum_scatter(v, "batch", scatter_dimension=3, tiled=True)

    by_phase = (8, 2, 8, 2, 16, 128)
    grad_one, small_one, wide_keep, wide_send = call(
        make_back_one_body(entries),
        [
            ((2, 2, 10, 10, 16, 256), bf16),
            ((8, 128), f32),
            ((8, 9, 64, 128), bf16),
            ((8, 9, 64, 128), bf16),
        ],
        (
            idx,
            gap,
            logit_one,
            base,
            dh_own.reshape(by_phase),
            dh_other.reshape(by_phase),
            mask,
            stat_one,
            gains,
            shared_three,
            field,
        ),
        "back_one",
        scratch=[pltpu.VMEM((4, 4, 256, 512), f32)],
        deps=ready,
        late=(9,),
    )
    widener_pair = pair(wide_keep, swap_with(wide_send, "chan", 1), "widener_pair")
    if eight:
        widener_pair = after(widener_pair, parts)
        widener_parts = over_batch(widener_pair)
    else:
        v = widener_pair.reshape(8, 9, 64, 2, 64).transpose(1, 3, 2, 0, 4).reshape(9, 2, 64, 512)
        widener_sum = lax.psum_scatter(v.astype(f32), "batch", scatter_dimension=3, tiled=True)
    if eight:
        skip_keep, skip_send = call(
            skip_back_body,
            [((32, 64, 128), bf16), ((32, 64, 128), bf16)],
            (idx, vectors, flats),
            "skip_back",
            scratch=[pltpu.VMEM((32, 128, 128), f32)],
            deps=(widener_pair,),
        )
    blocks = call(
        input_back_body,
        [((16, 64, 128), bf16)] * 4,
        (idx, grad_one, wide_w),
        "input_back",
        scratch=[pltpu.VMEM((16, 64, 512), bf16)],
        deps=(skip_send,) if eight else (widener_pair,),
        late=(1,),
    )
    got = [blocks[0]] + [swap_with(blocks[k], "chan", k) for k in range(1, 4)]
    input_grad = natural(
        got[0].astype(f32) + got[2].astype(f32), got[1].astype(f32) + got[3].astype(f32), 0
    )

    if eight:
        (refiner_sum,) = call(
            refiner_sum_body,
            [(refiner.shape, f32)],
            (parts,),
            "refiner_sum",
            smem=0, plain=True,
            deps=(widener_pair,),
        )
        skips = lax.all_gather(after(skips, dh_other), "chan", axis=0, tiled=True)
        exciter_sum, squeezer_sum = call(
            squeeze_back_body,
            [((64, 32), f32), ((64, 2048), f32)],
            (parts, skips),
            "squeeze_back",
            smem=0,
            plain=True,
            deps=(widener_pair,),
        )
        squeezer_sum = (
            squeezer_sum.reshape(64, 16, 8, 16).transpose(3, 0, 1, 2).reshape(16, 64, 128)
        )
        skip_own, skip_other = call(
            skip_add_body,
            [((32, 32, 128), f32), ((32, 32, 128), bf16)],
            (idx, skip_keep, swap_with(skip_send, "chan", 2)),
            "skip_add", plain=True,
        )
        (skip_grad,) = call(
            skip_last_body,
            [((32, 32, 128), f32)],
            (skip_own, swap_with(skip_other, "chan", 1)),
            "skip_last", plain=True,
            smem=0,
        )
        (widener_sum,) = call(
            widener_sum_body,
            [(widener.shape, f32)],
            (widener_parts,),
            "widener_sum",
            smem=0, plain=True,
            deps=(input_grad, skip_grad, output, squeezer_sum, refiner_sum),
        )
    else:
        lo, hi = small[2, :, :64], small[2, :, 64:]
        keep, send = jnp.where(core == 0, lo, hi), jnp.where(core == 0, hi, lo)
        grad_gate = natural(keep, swap_with(send, "chan", 1), 0)
        grad_excited = (grad_gate * gate * (1.0 - gate)).astype(bf16)
        exciter_grad = jnp.einsum(
            "bo,bc->oc", grad_excited, swish_full, preferred_element_type=f32
        )
        partial_swish = jnp.einsum(
            "bo,oc->bc", grad_excited, exciter_full, preferred_element_type=f32
        )
        grad_swish = lax.psum_scatter(
            partial_swish.astype(bf16), "chan", scatter_dimension=1, tiled=True
        ).astype(f32)
        grad_squeezed = grad_swish * squeeze_sig * (1.0 + squeezed * (1.0 - squeeze_sig))
        grad_squeezed = grad_squeezed.astype(bf16)
        squeezer_grad = jnp.einsum(
            "bo,bct->toc", grad_squeezed, pooled, preferred_element_type=f32
        )
        partial_pooled = jnp.einsum(
            "bo,toc->bct", grad_squeezed, squeezer_full, preferred_element_type=f32
        ).reshape(samples, -1, 128)
        skip_grad = lax.psum_scatter(
            partial_pooled.astype(bf16), "chan", scatter_dimension=1, tiled=True
        ).astype(f32)
        squeezer_sum = lax.psum_scatter(squeezer_grad, "batch", scatter_dimension=2, tiled=True)
        exciter_sum = lax.psum_scatter(exciter_grad, "batch", scatter_dimension=1, tiled=True)

    norms = jnp.concatenate([small_one[0:2], mine[2, 0:2]], axis=0)
    norm_grads = jnp.where(core == 0, norms[:, :64], norms[:, 64:])
    return (
        output,
        input_grad,
        skip_grad,
        widener_sum,
        refiner_sum,
        squeezer_sum,
        exciter_sum,
        norm_grads,
    )


def solution(mesh):
    placed = (
        P("batch", "chan", None),
        P("batch", "chan", None),
        P("batch"),
        P("batch"),
        P(None, None, "chan", "batch"),
        P(None, None, "chan", "batch"),
        P(None, "chan", "batch"),
        P("chan", "batch"),
        P("chan"),
        P("chan"),
        P("chan"),
        P("chan"),
        P("batch", "chan", None),
    )
    return jax.shard_map(
        on_device,
        mesh=mesh,
        in_specs=placed,
        out_specs=(
            P("batch", "chan", None),
            P("batch", "chan", None),
            P("batch", "chan", None),
            P(None, None, "chan", "batch"),
            P(None, None, "chan", "batch"),
            P(None, "chan", "batch"),
            P("chan", "batch"),
            P(None, "chan"),
        ),
        check_vma=False,
    )
```

```python
import jax
import jax.numpy as jnp
from jax import lax
from jax.experimental import pallas as pl
from jax.experimental.pallas import tpu as pltpu
from jax.sharding import PartitionSpec as P

MB = 4
epsilon = 1e-05
f32 = jnp.float32
bf16 = jnp.bfloat16
MIB = 2**20
LIMIT = 58

NT = (((1,), (1,)), ((), ()))
TN = (((0,), (0,)), ((), ()))


def dot(a, b, dims=None):
    if dims is None:
        return jnp.dot(a, b, preferred_element_type=f32)
    return lax.dot_general(a, b, dims, preferred_element_type=f32)


class Traffic:
    def __init__(self, ins, outs, in_sems, out_sems, late, cuts):
        self.ins, self.outs, self.out_sems = [], outs, out_sems
        self.sent = {}
        count = 0
        for k, (pieces, held) in enumerate(ins):
            copies, at = [], 0
            parts = cuts.get(k, 1)
            for piece in pieces:
                rows = piece.shape[0] // parts
                for n in range(parts):
                    src = piece.at[pl.ds(n * rows, rows)]
                    dst = held.at[pl.ds(at, rows)]
                    copies.append(pltpu.make_async_copy(src, dst, in_sems.at[count]))
                    count += 1
                    at += rows
            self.ins.append(copies)
        for copies in self.ins:
            for copy in copies:
                copy.start()
        self.need(*[k for k in range(len(ins)) if k not in late])

    def need(self, *which):
        for k in which:
            for copy in self.ins[k]:
                copy.wait()

    def need_part(self, k, n):
        self.ins[k][n].wait()

    def part(self, k, n, count):
        made, pieces = self.outs[k]
        rows = made.shape[0] // count
        if len(pieces) == 1:
            dst = pieces[0].at[pl.ds(n * rows, rows)]
        else:
            each = pieces[0].shape[0]
            dst = pieces[n * rows // each].at[pl.ds(n * rows % each, rows)]
        return pltpu.make_async_copy(
            made.at[pl.ds(n * rows, rows)], dst, self.out_sems.at[k, n]
        )

    def send(self, k, n=0, count=1):
        self.sent[k] = count
        self.part(k, n, count).start()

    def finish(self):
        for k in range(len(self.outs)):
            if k not in self.sent:
                for n in range(len(self.outs[k][1])):
                    self.send(k, n, len(self.outs[k][1]))
        for k, count in self.sent.items():
            for n in range(count):
                self.part(k, n, count).wait()


def grouped(refs, sizes):
    out, at = [], 0
    for size in sizes:
        out.append(refs[at : at + size])
        at += size
    return out


def call(body, outs, args, name, scratch=(), smem=1, deps=(), late=(), cuts={}, plain=False):
    scalars, args, deps = list(args[:smem]), list(args[smem:]), list(deps)
    args = [a if isinstance(a, tuple) else (a,) for a in args]
    outs = [o if len(o) == 3 else (*o, 1) for o in outs]
    in_sizes, out_sizes = [len(a) for a in args], [o[2] for o in outs]
    n_in, n_out = sum(in_sizes), sum(out_sizes)
    results = [
        jax.ShapeDtypeStruct((shape[0] // count, *shape[1:]), dtype)
        for shape, dtype, count in outs
        for _ in range(count)
    ]
    anywhere, inside = pl.BlockSpec(memory_space=pl.ANY), pl.BlockSpec(memory_space=pltpu.VMEM)

    def kernel(*refs):
        refs = list(refs)
        numbers, refs = refs[:smem], refs[smem:]
        ins, refs = refs[:n_in], refs[n_in + len(deps) :]
        made, refs = refs[:n_out], refs[n_out:]
        if plain:
            body(*numbers, *ins, *made, *refs)
            return
        held, refs = refs[: len(args)], refs[len(args) :]
        work, refs = refs[: len(outs)], refs[len(outs) :]
        traffic = Traffic(
            list(zip(grouped(ins, in_sizes), held)),
            list(zip(work, grouped(made, out_sizes))),
            refs[0],
            refs[1],
            late,
            cuts,
        )
        extra = (traffic,) if late else ()
        body(*extra, *numbers, *held, *work, *refs[2:])
        traffic.finish()

    own = []
    if not plain:
        own = [
            pltpu.VMEM((sum(p.shape[0] for p in a), *a[0].shape[1:]), a[0].dtype) for a in args
        ]
        own += [pltpu.VMEM(shape, dtype) for shape, dtype, _ in outs]
        own += [pltpu.SemaphoreType.DMA((n_in * max([1, *cuts.values()]),)), pltpu.SemaphoreType.DMA((len(outs), 8))]
    got = pl.pallas_call(
        kernel,
        out_shape=results,
        in_specs=[pl.BlockSpec(memory_space=pltpu.SMEM)] * smem
        + [inside if plain else anywhere] * n_in
        + [anywhere] * len(deps),
        out_specs=[inside if plain else anywhere] * n_out,
        scratch_shapes=own + list(scratch),
        compiler_params=pltpu.CompilerParams(
            vmem_limit_bytes=(16 if plain else LIMIT) * MIB
        ),
        cost_estimate=pl.CostEstimate(flops=0, bytes_accessed=0, transcendentals=0),
        name=name,
    )(*scalars, *[p for a in args for p in a], *deps)
    return [p[0] if len(p) == 1 else tuple(p) for p in grouped(list(got), out_sizes)]


def after(value, *deps):
    return pl.pallas_call(
        lambda *refs: None,
        out_shape=jax.ShapeDtypeStruct(value.shape, value.dtype),
        in_specs=[pl.BlockSpec(memory_space=pl.ANY)] * (1 + len(deps)),
        out_specs=pl.BlockSpec(memory_space=pl.ANY),
        input_output_aliases={0: 0},
        name="after",
    )(value, *deps)


def iota(shape, dim):
    return lax.broadcasted_iota(jnp.int32, shape, dim)


def onehot(cond):
    return jnp.where(cond, 1.0, 0.0).astype(f32).astype(bf16)


def eye(n):
    return onehot(iota((n, n), 0) == iota((n, n), 1))


def sixteen_swap():
    r, q = iota((256, 256), 0), iota((256, 256), 1)
    return onehot(((r % 16) == (q // 16)) & ((r // 16) == (q % 16)))


def tree(parts):
    parts = list(parts)
    while len(parts) > 1:
        parts = [parts[n] + parts[n + 1] for n in range(0, len(parts), 2)]
    return parts[0]


def sigmoid(v):
    return 1.0 / (1.0 + jnp.exp(-v))


def pack_wide_body(w, out):
    packed = jnp.concatenate([w[:, 0], w[:, 1]], axis=-1)
    for k in range(8):
        out[k] = packed


def pack_fine_body(r, e, e_other, out):
    slots = [r[q // 2, q % 2] for q in range(18)] + [e[...], e_other[...]]
    for row in range(5):
        out[row] = jnp.concatenate(slots[4 * row : 4 * row + 4], axis=-1)
    out[5:] = jnp.zeros((3, 64, 128), bf16)


def fill_taps(core, own, other, out):
    for blocks, side in ((own, core), (other, 1 - core)):
        for half in range(2):
            rows = pl.ds(pl.multiple_of(half * 128 + side * 64, 64), 64)
            lanes = slice(half * 64, half * 64 + 64)
            for group in range(4):
                w = [
                    jnp.concatenate(
                        [blocks[2 * group][t][:, lanes], blocks[2 * group + 1][t][:, lanes]],
                        axis=-1,
                    ).astype(f32)
                    for t in range(9)
                ]
                down = {
                    (0, 0): w[0:3],
                    (0, 1): [w[3 + s] + w[6 + s] for s in range(3)],
                    (1, 0): [w[s] + w[3 + s] for s in range(3)],
                    (1, 1): w[6:9],
                }
                for a in range(2):
                    for u in range(2):
                        d = down[(a, u)]
                        across = {
                            (0, 0): d[0],
                            (0, 1): d[1] + d[2],
                            (1, 0): d[0] + d[1],
                            (1, 1): d[2],
                        }
                        for b in range(2):
                            for v in range(2):
                                out[
                                    a * 8 + b * 4 + u * 2 + v,
                                    rows,
                                    group * 128 : group * 128 + 128,
                                ] = across[(b, v)].astype(bf16)


def refiner_body(idx, own, other, out, ex, ex_other):
    core = idx[1]
    for blocks, side in ((own, core), (other, 1 - core)):
        rows = pl.multiple_of(side * 64, 64)
        for q in range(20):
            lanes = slice((q % 4) * 32, (q % 4) * 32 + 32)
            piece = jnp.concatenate([blocks[k, q // 4][:, lanes] for k in range(8)], axis=-1)
            if q < 18:
                out[q // 2, pl.ds(rows + (q % 2) * 128, 64), :] = piece
            else:
                (ex, ex_other)[q - 18][pl.ds(rows, 64), :] = piece


def feature_select(place):
    r, q = iota((512, 512), 0), iota((512, 512), 1)
    kept = r % 256
    return onehot((((kept // 64) ^ place) * 64 + kept % 64) * 2 + r // 256 == q)


def feature_body(idx, b0, b1, b2, b3, out, turned):
    ident = eye(128)

    def turn(s, carry):
        x = jnp.concatenate([b0[s], b1[s], b2[s], b3[s]], axis=0)
        t = dot(ident, x, NT).astype(bf16)
        turned[s] = jnp.concatenate([t[:64], t[64:]], axis=-1)
        return carry

    lax.fori_loop(0, 16, turn, 0, unroll=4)
    swap = sixteen_swap()
    select = feature_select(idx[0])
    zero = jnp.zeros((10, 16, 512), bf16)
    out[0] = zero
    out[9] = zero
    out[:, 0] = zero
    out[:, 9] = zero
    for block in range(4):
        a = turned[:, block * 16 : block * 16 + 16, :].reshape(256, 512)
        c = dot(dot(swap, a).astype(bf16), select).astype(bf16)
        out[1 + 2 * block : 3 + 2 * block, 1:9] = c.reshape(2, 8, 16, 512)


def input_back_body(io, idx, d, w, b0, b1, b2, b3, turned):
    swap = sixteen_swap()
    select = feature_select(idx[0])

    acc = None
    for a in range(2):
        io.need_part(0, a)
        for b in range(2):
            io.need_part(1, 2 * a + b)
            lhs = jnp.concatenate(
                [
                    d[a, b, 2 - u - a : 10 - u - a, 2 - v - b : 10 - v - b].reshape(1024, 256)
                    for u in range(2)
                    for v in range(2)
                ],
                axis=-1,
            )
            first = a * 8 + b * 4
            term = dot(lhs, w[first : first + 4].reshape(1024, 512))
            acc = term if acc is None else acc + term
    x = dot(acc.astype(bf16), select, NT).astype(bf16)
    for block in range(4):
        t = dot(swap, x[block * 256 : block * 256 + 256]).astype(bf16)
        turned[:, block * 16 : block * 16 + 16, :] = t.reshape(16, 16, 512)
    ident = eye(256)

    def turn(s, carry):
        t = turned[s]
        t = jnp.concatenate([t[:, :256], t[:, 256:]], axis=0)
        o = dot(ident, t, NT).astype(bf16)
        b0[s] = o[0:64]
        b1[s] = o[64:128]
        b2[s] = o[128:192]
        b3[s] = o[192:256]
        return carry

    lax.fori_loop(0, 16, turn, 0, unroll=4)


def input_join_body(idx, b0, b1, b2, b3, out):
    at = pl.multiple_of(idx[1] * 16, 16)
    out[pl.ds(at, 16)] = b0[...].astype(f32) + b2[...].astype(f32)
    out[pl.ds(16 - at, 16)] = b1[...].astype(f32) + b3[...].astype(f32)


def upstream_body(idx, own, other, out, turned):
    first = idx[1] == 0
    ident = eye(256)

    def turn(s, carry):
        p, q = own[s], other[s]
        lo = jnp.where(first, p, q)
        hi = jnp.where(first, q, p)
        turned[s] = dot(ident, jnp.concatenate([lo, hi], axis=0), NT).astype(bf16)
        return carry

    lax.fori_loop(0, 16, turn, 0, unroll=4)
    swap = sixteen_swap()

    def mix(y, carry):
        a = turned[:, pl.ds(pl.multiple_of(y * 16, 16), 16), :].reshape(256, 128)
        out[y] = dot(swap, a).astype(bf16).reshape(16, 16, 128)
        return carry

    lax.fori_loop(0, 16, mix, 0, unroll=4)


def over_samples(mask, values):
    return jnp.concatenate(
        [jnp.sum(mask[m] * values, axis=0, keepdims=True) for m in range(MB)], axis=0
    )


def per_sample(mask, rows):
    return sum(mask[m] * rows[m : m + 1] for m in range(MB))


def local_stats(mask, mean_s, squares_s):
    ones = jnp.ones_like(mean_s)
    n = over_samples(mask, ones) * 256.0
    mean = over_samples(mask, mean_s) * 256.0 / jnp.maximum(n, 1.0)
    gap = mean_s - per_sample(mask, mean)
    squares = over_samples(mask, squares_s + 256.0 * gap * gap)
    return n, mean, squares


def total_stats(messages, entries):
    parts = [(g[0:4], g[4:8], g[8:12]) for g in messages]
    mean = tree([n * m for n, m, _ in parts]) / entries
    squares = tree([q + n * (m - mean) * (m - mean) for n, m, q in parts])
    inverse = lax.rsqrt(squares / entries + epsilon)
    return mean, inverse


def message_list(refs):
    return [ref[c] for ref in refs for c in range(ref.shape[0])]


def conv_one_body(io, idx, own, other, x, mask, gap, logit, base, msg, w, glu):
    fill_taps(idx[1], own, other, w)
    io.send(4)
    io.need(2, 3)
    total = jnp.zeros((16, 128), f32)
    for a in range(2):
        for b in range(2):
            kept = []
            for u in range(2):
                for v in range(2):
                    kept.append(x[u + a : u + a + 8, v + b : v + b + 8].reshape(1024, 512))
            first = a * 8 + b * 4
            rhs = jnp.concatenate([w[first + n] for n in range(4)], axis=-1)
            c = dot(jnp.concatenate(kept, axis=-1), rhs, NT)
            g = (c[:, :128] * sigmoid(c[:, 128:])).reshape(8, 8, 16, 128)
            logit[:, a, :, b] = c[:, 128:].reshape(8, 8, 16, 128).astype(bf16)
            glu[a, b] = g
            total = total + jnp.sum(g, axis=(0, 1))
    io.send(1)
    mean_s = total * (1.0 / 256.0)
    base[...] = mean_s
    io.send(2)

    squares = jnp.zeros((16, 128), f32)
    for i in range(8):
        for a in range(2):
            for b in range(2):
                d = glu[a, b, i] - mean_s[None]
                gap[i, a, :, b] = d.astype(bf16)
                squares = squares + jnp.sum(d * d, axis=0)
        io.send(0, i, 8)
    n, mean, squares = local_stats(mask[...], mean_s, squares)
    msg[0:4] = n
    msg[4:8] = mean
    msg[8:12] = squares
    msg[12:16] = jnp.zeros((4, 128), f32)


def make_scale_body(entries):
    def body(idx, mask, gains, base, messages, line, stat):
        mean, inverse = total_stats(message_list([messages]), entries)
        m = mask[...]
        mean_s, inverse_s = per_sample(m, mean), per_sample(m, inverse)
        stat[0] = base[...] - mean_s
        stat[1] = inverse_s
        scale = inverse_s * gains[0:1]
        line[0] = scale
        line[1] = (base[...] - mean_s) * scale + gains[1:2]
        if messages.shape[0] == 16 and messages.shape[1] == 32:
            core = idx[1]
            line[2, 0:8] = tree([messages[2 * k + core, 16:24] for k in range(8)])
            line[2, 8:16] = tree([messages[2 * k + core, 24:32] for k in range(8)])
        else:
            line[2] = jnp.zeros((16, 128), f32)

    return body


def conv_two_body(io, idx, own, other, line, line_other, w, up, held, glu, logit, sums):
    zero = jnp.zeros((18, 16, 256), bf16)
    held[0] = zero
    held[17] = zero
    held[:, 0] = zero
    held[:, 17] = zero

    def fill(y, carry):
        for gap, scale, side in ((own, line, idx[2]), (other, line_other, 1 - idx[2])):
            h = gap[y].astype(f32) * scale[0] + scale[1]
            lanes = pl.ds(pl.multiple_of(side * 128, 128), 128)
            held[y + 1, 1:17, :, lanes] = h.astype(bf16)
        return carry

    lax.fori_loop(0, 16, fill, 0, unroll=2)
    io.send(0)
    io.need(4)

    def rows(step, total):
        y = step * 4
        lhs = jnp.concatenate(
            [
                held[pl.ds(y + t // 3, 4), t % 3 : t % 3 + 16].reshape(1024, 256)
                for t in range(9)
            ],
            axis=-1,
        )
        rhs = jnp.concatenate([w[t] for t in range(9)], axis=-1)
        c = dot(lhs, rhs, NT)
        g = (c[:, :128] * sigmoid(c[:, 128:])).reshape(4, 16, 16, 128)
        logit[pl.ds(y, 4)] = c[:, 128:].reshape(4, 16, 16, 128).astype(bf16)
        glu[pl.ds(y, 4)] = g
        io.send(1, step, 4)
        io.send(2, step, 4)
        return total + jnp.sum(g, axis=(0, 1))

    total = lax.fori_loop(0, 4, rows, jnp.zeros((16, 128), f32), unroll=True)
    mean_s = total * (1.0 / 256.0)

    io.need(5)

    def spread(y, acc):
        gap = glu[y] - mean_s[None]
        u = up[y].astype(f32)
        return (
            acc[0] + jnp.sum(gap * gap, axis=0),
            acc[1] + jnp.sum(u, axis=0),
            acc[2] + jnp.sum(u * gap, axis=0),
        )

    none = jnp.zeros((16, 128), f32)
    squares, plain, cross = lax.fori_loop(0, 16, spread, (none, none, none))
    sums[0] = mean_s
    sums[1] = plain
    sums[2] = cross
    sums[3] = squares


def make_back_two_body(entries):
    def body(io, idx, glu, logit, up, mask, pull, gains, sums, w, gap, gap_other, messages, *outs):
        grad, own, other, small, stat, mine = outs
        messages = message_list([messages])
        mean, inverse = total_stats(messages, entries)
        plain = tree([g[12:16] for g in messages])
        cross = inverse * tree([g[16:20] + g[12:16] * (g[4:8] - mean) for g in messages])
        m = mask[...]
        mean_s, inverse_s = per_sample(m, mean), per_sample(m, inverse)
        gain, shift = gains[2:3], gains[3:4]
        stat[0] = mean_s
        stat[1] = inverse_s
        weight, gate = pull[0], pull[1]
        centred = sums[2] + sums[1] * (sums[0] - mean_s)
        small[2] = weight * (gain * inverse_s * centred + shift * sums[1])
        mine[2, 0:1] = jnp.sum(cross, axis=0, keepdims=True)
        mine[2, 1:2] = jnp.sum(plain, axis=0, keepdims=True)
        mine[2, 2:] = jnp.zeros((14, 128), f32)
        plain_s = per_sample(m, plain) * (1.0 / entries)
        cross_s = per_sample(m, cross) * (1.0 / entries)
        scale = inverse_s * gain
        factor = weight * gate
        io.need(0, 1, 2)
        zero = jnp.zeros((18, 16, 256), bf16)
        grad[0] = zero
        grad[17] = zero
        grad[:, 0] = zero
        grad[:, 17] = zero

        def step(y, carry):
            g = glu[y]
            s = sigmoid(logit[y].astype(f32))
            hat = (g - mean_s) * inverse_s
            d = scale * (up[y].astype(f32) * factor - plain_s - hat * cross_s)
            grad[y + 1, 1:17, :, 0:128] = (d * s).astype(bf16)
            grad[y + 1, 1:17, :, 128:256] = (d * g * (1.0 - s)).astype(bf16)
            return carry

        lax.fori_loop(0, 16, step, 0, unroll=2)
        io.send(0)
        io.need(7, 8, 9)

        def rows(step, acc):
            y = step * 4
            lhs = jnp.concatenate(
                [
                    grad[pl.ds(y + 2 - t // 3, 4), 2 - t % 3 : 18 - t % 3].reshape(1024, 256)
                    for t in range(9)
                ],
                axis=-1,
            )
            c = dot(lhs, w[...].reshape(2304, 256)).astype(bf16)
            out = []
            first = idx[2] == 0
            mine_c = jnp.where(first, c[:, :128], c[:, 128:])
            their_c = jnp.where(first, c[:, 128:], c[:, :128])
            for k, ref, at, d in ((1, own, gap, mine_c), (2, other, gap_other, their_c)):
                d = d.reshape(4, 16, 16, 128)
                ref[pl.ds(y, 4)] = d
                io.send(k, step, 4)
                d = d.astype(f32)
                out.append(jnp.sum(d, axis=(0, 1)))
                out.append(jnp.sum(d * at[pl.ds(y, 4)].astype(f32), axis=(0, 1)))
            return tuple(p + q for p, q in zip(acc, out))

        none = jnp.zeros((16, 128), f32)
        mine[0], mine[1], small[0], small[1] = lax.fori_loop(
            0, 4, rows, (none,) * 4, unroll=True
        )

    return body


def output_part(idx, glu, stat, pull, gains, own, other, turned):
    swap = sixteen_swap()
    mean_s, inverse_s = stat[0], stat[1]
    gain, shift = gains[2:3], gains[3:4]
    gate = pull[1]

    def step(y, carry):
        o = (((glu[y] - mean_s) * inverse_s) * gain + shift) * gate
        o = dot(swap, o.astype(bf16).reshape(256, 128)).astype(bf16)
        turned[:, pl.ds(pl.multiple_of(y * 16, 16), 16), :] = o.reshape(16, 16, 128)
        return carry

    lax.fori_loop(0, 16, step, 0, unroll=4)
    ident = eye(128)
    first = idx[1] == 0

    def turn(s, carry):
        t = dot(ident, turned[s], NT).astype(bf16)
        own[s] = jnp.where(first, t[:64], t[64:])
        other[s] = jnp.where(first, t[64:], t[:64])
        return carry

    lax.fori_loop(0, 16, turn, 0, unroll=4)


def refiner_grad_body(
    io, idx, grad, held, glu, stat, pull, gains, own, other, out_own, out_other, work, turned
):
    core = idx[1]

    def tap(t, carry):
        d = grad[1:17, 1:17].reshape(4096, 256)
        h = held[pl.ds(t // 3, 16), pl.ds(t % 3, 16)].reshape(4096, 256)
        work[t] = dot(d, h, TN).astype(bf16)
        return carry

    lax.fori_loop(0, 9, tap, 0, unroll=3)
    for out, side in ((own, core), (other, 1 - core)):
        start = pl.multiple_of(side * 64, 64)
        for row in range(5):
            pieces = [
                work[q // 2, pl.ds(start + (q % 2) * 128, 64), :]
                for q in range(4 * row, min(4 * row + 4, 18))
            ]
            pieces += [jnp.zeros((64, 256), bf16)] * (4 - len(pieces))
            for k in range(8):
                lanes = slice(k * 32, k * 32 + 32)
                out[k, row] = jnp.concatenate([p[:, lanes] for p in pieces], axis=-1)
    io.send(0)
    io.send(1)
    io.need(2, 3, 4, 5)
    output_part(idx, glu, stat, pull, gains, out_own, out_other, turned)


def refiner_sum_body(parts, out):
    total = tree([parts[k, :320].astype(f32) for k in range(8)])
    for q in range(18):
        rows = slice((q // 4) * 64, (q // 4) * 64 + 64)
        out[q // 2, q % 2] = total[rows, (q % 4) * 32 : (q % 4) * 32 + 32]


def first_sums_body(mine, theirs, mask, stat, payload):
    m = mask[...]
    plain = mine[0] + theirs[0]
    cross = mine[1] + theirs[1] + stat[0] * plain
    msg = jnp.concatenate([over_samples(m, plain), over_samples(m, cross * stat[1])], axis=0)
    for k in range(payload.shape[0]):
        payload[k] = msg


def make_back_one_body(entries):
    def body(
        io,
        idx,
        gap,
        logit,
        base,
        own,
        other,
        mask,
        stat,
        gains,
        messages,
        x,
        grad,
        small,
        keep,
        send,
        work,
    ):
        messages = message_list([messages])
        plain = tree([g[0:4] for g in messages])
        cross = tree([g[4:8] for g in messages])
        small[0:1] = jnp.sum(cross, axis=0, keepdims=True)
        small[1:2] = jnp.sum(plain, axis=0, keepdims=True)
        small[2:8] = jnp.zeros((6, 128), f32)
        io.send(1)
        m = mask[...]
        plain_s = per_sample(m, plain) * (1.0 / entries)
        cross_s = per_sample(m, cross) * (1.0 / entries)
        shift_s, inverse_s = stat[0], stat[1]
        mean = base[...]
        scale = inverse_s * gains[0:1]
        zero = jnp.zeros((10, 16, 256), bf16)
        for a in range(2):
            for b in range(2):
                grad[a, b, 0] = zero
                grad[a, b, 9] = zero
                grad[a, b, :, 0] = zero
                grad[a, b, :, 9] = zero

        def step(i, carry):
            for a in range(2):
                for b in range(2):
                    g = gap[i, a, :, b].astype(f32)
                    s = sigmoid(logit[i, a, :, b].astype(f32))
                    hat = (g + shift_s) * inverse_s
                    g = g + mean
                    d = own[i, a, :, b].astype(f32) + other[i, a, :, b].astype(f32)
                    d = scale * (d - plain_s - hat * cross_s)
                    grad[a, b, i + 1, 1:9, :, 0:128] = (d * s).astype(bf16)
                    grad[a, b, i + 1, 1:9, :, 128:256] = (d * g * (1.0 - s)).astype(bf16)
            return carry

        lax.fori_loop(0, 8, step, 0)
        io.send(0)
        io.need(9)
        widener_grad(idx[1], grad, x, keep, send, work)

    return body


def widener_grad(core, grad, x, own, other, work):
    def phase(n, carry):
        a, b = n // 2, n % 2
        d = grad[a, b, 1:9, 1:9].reshape(1024, 256)
        for u in range(2):
            for v in range(2):
                f = x[pl.ds(u + a, 8), pl.ds(v + b, 8)].reshape(1024, 512)
                work[n, 2 * u + v] = dot(d, f, TN)
        return carry

    lax.fori_loop(0, 4, phase, 0, unroll=2)
    source = {0: (0, 0), 1: (1, 0), 2: (1, 1)}
    for out, side in ((own, core), (other, 1 - core)):
        start = pl.multiple_of(side * 64, 64)
        for pair in range(4):
            lanes = slice(pair * 128, pair * 128 + 128)
            for r in range(3):
                for s in range(3):
                    both = []
                    for half in range(2):
                        rows = pl.ds(start + half * 128, 64)
                        both.append(
                            sum(
                                work[2 * a + b, 2 * source[r][a] + source[s][b], rows, lanes]
                                for a in range(2)
                                for b in range(2)
                            )
                        )
                    first, second = both
                    out[2 * pair, 3 * r + s] = jnp.concatenate(
                        [first[:, :64], second[:, :64]], axis=-1
                    ).astype(bf16)
                    out[2 * pair + 1, 3 * r + s] = jnp.concatenate(
                        [first[:, 64:], second[:, 64:]], axis=-1
                    ).astype(bf16)


def pair_sum_body(io, own, other, out):
    for k in range(8):
        io.need_part(0, k)
        io.need_part(1, k)
        out[k] = (own[k].astype(f32) + other[k].astype(f32)).astype(bf16)
        io.send(0, k, 8)


def widener_sum_body(parts, out):
    for t in range(9):
        total = tree([parts[k, t].astype(f32) for k in range(8)])
        out[t, 0] = total[:, :64]
        out[t, 1] = total[:, 64:]


def skip_quarter_body(idx, skip, out):
    rows = pl.ds(pl.multiple_of(idx[0] * 8, 8), 8)
    for i in range(8):
        out[i] = skip[rows, i * 16 : i * 16 + 16, :]


def squeeze_body(skip, kernels, msg, kept, out, rows):
    rows[...] = skip[...].astype(f32).reshape(1024, 128)
    for k in range(16):
        kept[:, k * 128 : k * 128 + 128] = rows[pl.ds(k, 64, stride=16), :].astype(bf16)
    part = dot(kept[...], kernels[...], NT)
    for i in range(8):
        for c in range(2):
            out[2 * i + c, 0:16] = msg[...]
            out[2 * i + c, 16:24] = part[i * 8 : i * 8 + 8, :128]
            out[2 * i + c, 24:32] = part[i * 8 : i * 8 + 8, 128:]


def gate_body(idx, s0, s1, s2, s3, ex, weight, out, squeezed):
    j, core = idx[0], idx[1]
    for n, part in enumerate((s0, s1, s2, s3)):
        rows = pl.ds(pl.multiple_of((j ^ n) * 8, 8), 8)
        squeezed[rows, :128] = part[2, 0:8]
        squeezed[rows, 128:] = part[2, 8:16]
    mine = squeezed[pl.ds(pl.multiple_of(core * 16, 16), 16), :]
    excited = dot((mine * sigmoid(mine)).astype(bf16), ex[...], NT)
    out[0] = weight[...]
    out[1] = sigmoid(excited)


def gate_message_body(idx, s0, s1, s2, s3, ex, weight, mask, sums, out, squeezed, payload):
    gate_body(idx, s0, s1, s2, s3, ex, weight, out, squeezed)
    message_two_body(mask, out, sums, payload)


def message_two_body(mask, pull, sums, payload):
    mean_s, plain, cross = sums[0], sums[1], sums[2]
    m = mask[...]
    n, mean, squares = local_stats(m, mean_s, sums[3])
    factor = pull[0] * pull[1]
    spread = over_samples(m, factor * (cross + plain * (mean_s - per_sample(m, mean))))
    rows = [n, mean, squares, over_samples(m, factor * plain), spread, jnp.zeros((4, 128), f32)]
    msg = jnp.concatenate(rows, axis=0)
    for k in range(payload.shape[0]):
        payload[k] = msg


def excite_back_body(idx, g0, g1, squeezed, ex_own, ex_other, fine, recv, vectors, out):
    chip = idx[2]
    s = squeezed[...]
    sigm = sigmoid(s)
    swish = (s * sigm).astype(bf16)
    mine, theirs = ex_own[...], ex_other[...]
    ex = jnp.where(
        chip == 0, jnp.concatenate([mine, theirs], axis=0), jnp.concatenate([theirs, mine], axis=0)
    )
    gate = sigmoid(dot(swish, ex, NT))
    core = idx[1]
    rows = []
    for half in range(2):
        own = jnp.where(core == half, g0[0], g1[0])
        other = jnp.where(core == half, g0[1], g1[1])
        lo, hi = jnp.where(chip == 0, own, other), jnp.where(chip == 0, other, own)
        rows.append(jnp.concatenate([lo, hi], axis=-1))
    grad_gate = jnp.concatenate(rows, axis=0)
    d_excited = (grad_gate * gate * (1.0 - gate)).astype(bf16)
    d_swish = dot(d_excited, ex)
    d_squeezed = d_swish * (sigm * (1.0 + s * (1.0 - sigm)))
    j = idx[0]
    pick_out = onehot(iota((256, 64), 0) == iota((256, 64), 1) + j * 64)
    both = jnp.concatenate(
        [dot(d_squeezed.astype(bf16), pick_out), dot(d_excited, pick_out)], axis=-1
    ).astype(bf16)
    vectors[...] = both
    pick_in = onehot((iota((256, 1024), 0) // 32 == iota((256, 1024), 1) // 128)
                     & (iota((256, 1024), 0) % 32 == iota((256, 1024), 1) % 128))
    picked = dot(swish, pick_in).astype(bf16)
    total = (fine[...].astype(f32) + recv[...].astype(f32)).astype(bf16)
    out[:, :320] = total.reshape(8, 320, 128)
    for k in range(8):
        out[k, 320:352] = both
        out[k, 352:384] = picked[:, k * 128 : k * 128 + 128]


def quarters_first(v):
    v = v.astype(f32)
    return jnp.concatenate(
        [v[i * 32 + q * 8 : i * 32 + q * 8 + 8] for q in range(4) for i in range(8)], axis=0
    )


def squeeze_back_body(parts, skips, ex_grad, sq_grad, refiner_out):
    refiner_sum_body(parts, refiner_out)
    vectors = jnp.concatenate([parts[k, 320:352] for k in range(8)], axis=0)
    swish = jnp.concatenate([parts[k, 352:384] for k in range(8)], axis=0)
    ex_grad[...] = dot(vectors, swish, TN)[64:, :32]
    grad = dot(quarters_first(vectors).astype(bf16), skips[...], TN)
    for t in range(16):
        sq_grad[t] = grad[:64, t * 128 : t * 128 + 128]


def skip_back_body(io, idx, vectors, kernels, keep, send):
    d = vectors[:, :64]
    for i in range(8):
        io.need_part(1, i)
        pooled = dot(d, kernels[i * 64 : i * 64 + 64, :]).astype(bf16)
        lanes = slice((i % 4) * 2048, (i % 4) * 2048 + 2048)
        mine = idx[2] == i // 4

        @pl.when(mine)
        def _():
            keep[:, lanes] = pooled

        @pl.when(jnp.logical_not(mine))
        def _():
            send[:, lanes] = pooled


def skip_add_body(idx, own, other, keep, send):
    first = idx[1] == 0
    total = own[...].astype(f32) + other[...].astype(f32)
    lo, hi = total[:, :4096], total[:, 4096:]
    keep[...] = jnp.where(first, lo, hi)
    send[...] = jnp.where(first, hi, lo).astype(bf16)


def last_join_body(idx, b0, b1, b2, b3, own, other, out, skip):
    input_join_body(idx, b0, b1, b2, b3, out)
    for r in range(32):
        lanes = slice(r * 128, r * 128 + 128)
        skip[:, r, :] = own[:, lanes] + other[:, lanes].astype(f32)


def swap_with(v, axis, k):
    return lax.ppermute(v, axis, [(n, n ^ k) for n in range(lax.axis_size(axis))])


def on_device(
    features,
    skip_feature,
    section_ids,
    micro_ids,
    widener,
    refiner,
    squeezer,
    exciter,
    gain_one,
    bias_one,
    gain_two,
    bias_two,
    upstream,
):
    nb = lax.axis_size("batch")
    eight = nb == 8
    samples = features.shape[0]
    entries = float(samples * nb // MB * 256)
    i = lax.axis_index("batch")
    j = lax.axis_index("chan")
    core, chip = j % 2, j // 2
    idx = jnp.stack([j, core, chip, i]).astype(jnp.int32)

    def half(v, which):
        return lax.dynamic_slice_in_dim(v, which * 16, 16, axis=0)

    def natural(own, other, axis):
        return jnp.where(
            core == 0,
            jnp.concatenate([own, other], axis=axis),
            jnp.concatenate([other, own], axis=axis),
        )

    def over_batch(v):
        return lax.all_to_all(v, "batch", 0, 0, tiled=True)

    f_keep, f_send = half(features, core), half(features, 1 - core)
    f_blocks = [f_keep] + [
        swap_with(f_send if k % 2 else f_keep, "chan", k) for k in range(1, 4)
    ]
    if eight:
        (wide,) = call(
            pack_wide_body, [((8, 9, 64, 128), bf16)], (widener,), "pack_wide", smem=0, plain=True
        )
        wide_own = over_batch(wide)
    else:
        w_all = lax.all_gather(widener, "batch", axis=3, tiled=True)
        wide_own = w_all.reshape(9, 2, 64, 8, 64).transpose(3, 0, 2, 1, 4).reshape(8, 9, 64, 128)

    gains = jnp.stack([gain_one, bias_one, gain_two, bias_two], axis=0)
    gains = natural(gains, swap_with(gains, "chan", 1), 1)
    ids = half(micro_ids, core)
    mask = jnp.broadcast_to(
        (ids[None, :, None] == jnp.arange(MB, dtype=jnp.int32)[:, None, None]).astype(f32),
        (MB, 16, 128),
    )
    weight_of = jnp.where(section_ids == 0, 1.0, jnp.where(section_ids == 1, 2.0, 4.0)).astype(f32)
    weight = jnp.broadcast_to(half(weight_of, core)[:, None], (16, 128))

    groups = [[n * 4 + 2 * x + c for n in range(nb) for c in range(2)] for x in range(2)]

    def exchange(copies):
        return lax.all_to_all(
            copies, ("batch", "chan"), 0, 0, tiled=True, axis_index_groups=groups
        )

    def share(msg):
        if eight:
            return exchange(jnp.broadcast_to(msg, (16,) + msg.shape))
        pair = jnp.stack([msg, swap_with(msg, "chan", 1)], axis=0)
        return lax.all_gather(pair, "batch").reshape((-1,) + msg.shape)

    u_keep = half(upstream, core)
    u_other = swap_with(half(upstream, 1 - core), "chan", 1)
    (up,) = call(
        upstream_body,
        [((16, 16, 16, 128), bf16)],
        (idx, u_keep, u_other),
        "upstream_turned",
        scratch=[pltpu.VMEM((16, 256, 128), bf16)],
    )
    (field,) = call(
        feature_body,
        [((10, 10, 16, 512), bf16)],
        (idx, *f_blocks),
        "features_turned",
        scratch=[pltpu.VMEM((16, 64, 512), bf16)],
        deps=(up, gains),
    )
    if eight:
        by_tap = skip_feature.reshape(32, 2, 16, 8, 16).transpose(0, 1, 4, 2, 3)
        skip_full = lax.all_gather(by_tap.reshape(32, 32, 128), "chan", axis=1, tiled=True)
        flat = squeezer.reshape(16, 64, 16, 8).transpose(1, 2, 3, 0).reshape(64, 2048)
        squeezer_whole = lax.all_gather(
            squeezer.transpose(1, 0, 2).reshape(64, 2048), "chan", axis=0, tiled=True
        )
        (quarter,) = call(
            skip_quarter_body,
            [((8, 8, 16, 128), bf16)],
            (idx, skip_full),
            "skip_quarter", plain=True,
        )
        wide_own = after(wide_own, field, quarter)
        quarter = over_batch(after(quarter, wide_own))

        (fine,) = call(
            pack_fine_body,
            [((8, 64, 128), bf16)],
            (refiner, exciter, swap_with(exciter, "chan", 2)),
            "pack_fine",
            smem=0, plain=True,
            deps=(field,),
        )
        fine_own = lax.all_gather(fine, "batch")
    else:
        r_all = lax.all_gather(refiner, "batch", axis=3, tiled=True)
        e_all = lax.all_gather(exciter, "batch", axis=1, tiled=True)
        r_all = jnp.concatenate(
            [r_all.reshape(18, 64, 256), e_all[None], jnp.zeros((1, 64, 256), bf16)], axis=0
        )
        r_all = r_all.reshape(5, 4, 64, 8, 32).transpose(3, 0, 2, 1, 4).reshape(8, 5, 64, 128)
        fine_own = jnp.pad(r_all, ((0, 0), (0, 3), (0, 0), (0, 0)))

    wide_other = swap_with(wide_own, "chan", 1)
    gap, logit_one, base, msg_one, wide_w = call(
        conv_one_body,
        [
            ((8, 2, 8, 2, 16, 128), bf16, 2),
            ((8, 2, 8, 2, 16, 128), bf16),
            ((16, 128), f32),
            ((16, 128), f32),
            ((16, 256, 512), bf16),
        ],
        (idx, wide_own, wide_other, field, mask),
        "conv_one",
        scratch=[pltpu.VMEM((2, 2, 8, 8, 16, 128), f32)],
        late=(2, 3),
    )
    gap_other = tuple(swap_with(v, "chan", 2).reshape(8, 16, 16, 128) for v in gap)
    gap_flat = tuple(v.reshape(8, 16, 16, 128) for v in gap)

    if eight:
        skips, payload = call(
            squeeze_body,
            [((64, 2048), bf16), ((16, 32, 128), f32)],
            (quarter, squeezer_whole, msg_one),
            "squeeze",
            scratch=[pltpu.VMEM((1024, 128), f32)],
            smem=0,
        )
        shared_one = exchange(payload)
    else:
        shared_one = share(msg_one)
    shared_one = after(shared_one, *gap_other)
    line, stat_one = call(
        make_scale_body(entries),
        [((3, 16, 128), f32), ((2, 16, 128), f32)],
        (idx, mask, gains, base, shared_one),
        "scale",
        plain=True,
    )
    fine_own = after(fine_own, shared_one)
    fine_other = swap_with(fine_own, "chan", 1)
    fine_w, exciter_own, exciter_other = call(
        refiner_body,
        [((9, 256, 256), bf16), ((128, 256), bf16), ((128, 256), bf16)],
        (idx, fine_own, fine_other),
        "refiner_taps", plain=True,
    )
    line_other = swap_with(line, "chan", 2)
    if eight:
        squeezed = (line, swap_with(line, "chan", 1), line_other, swap_with(line_other, "chan", 1))
        skips_all = lax.all_gather(after(skips, line_other), "chan", axis=0, tiled=True)

    held, glu_two, logit_two, sums_two = call(
        conv_two_body,
        [
            ((18, 18, 16, 256), bf16),
            ((16, 16, 16, 128), f32),
            ((16, 16, 16, 128), bf16),
            ((4, 16, 128), f32),
        ],
        (idx, gap_flat, gap_other, line, line_other, fine_w, up),
        "conv_two",
        late=(4, 5),
    )
    if eight:
        pull, squeezed, payload_two = call(
            gate_message_body,
            [((2, 16, 128), f32), ((32, 256), f32), ((16, 24, 128), f32)],
            (idx, *squeezed, exciter_own, weight, mask, sums_two),
            "gate",
        )
        shared_two = exchange(payload_two)
    else:
        skip_full = lax.all_gather(skip_feature, "chan", axis=1, tiled=True)
        squeezer_full = lax.all_gather(squeezer, "batch", axis=2, tiled=True)
        pooled = skip_full.reshape(samples, -1, 16)
        squeezed = jnp.einsum("toc,bct->bo", squeezer_full, pooled, preferred_element_type=f32)
        squeeze_sig = jax.nn.sigmoid(squeezed)
        swish = (squeezed * squeeze_sig).astype(bf16)
        swish_full = lax.all_gather(swish, "chan", axis=1, tiled=True)
        exciter_full = lax.all_gather(exciter, "batch", axis=1, tiled=True)
        excited = jnp.einsum("oc,bc->bo", exciter_full, swish_full, preferred_element_type=f32)
        gate = jax.nn.sigmoid(excited)
        gate_mine = natural(half(gate, core), swap_with(half(gate, 1 - core), "chan", 1), 1)
        pull = jnp.stack([weight, gate_mine], axis=0)
        (msg_two,) = call(
            message_two_body, [((1, 24, 128), f32)], (mask, pull, sums_two), "message", smem=0
        )
        shared_two = share(msg_two[0])
    if eight:
        flats = lax.all_gather(after(flat, shared_two), "batch", axis=0, tiled=True)
    grad_two, dh_own, dh_send, small, stat_two, mine = call(
        make_back_two_body(entries),
        [
            ((18, 18, 16, 256), bf16),
            ((16, 16, 16, 128), bf16),
            ((16, 16, 16, 128), bf16),
            ((3, 16, 128), f32),
            ((2, 16, 128), f32),
            ((3, 16, 128), f32),
        ],
        (
            idx,
            glu_two,
            logit_two,
            up,
            mask,
            pull,
            gains,
            sums_two,
            fine_w,
            gap_flat,
            gap_other,
            shared_two,
        ),
        "back_two",
        deps=(skips_all,) if eight else (),
        late=(0, 1, 2, 7, 8, 9),
    )
    theirs = swap_with(small, "chan", 2)
    dh_other = swap_with(after(dh_send, theirs), "chan", 2)
    (payload_three,) = call(
        first_sums_body,
        [((16 if eight else 1, 8, 128), f32)],
        (mine, theirs, mask, stat_one),
        "first_sums",
        smem=0,
        plain=True,
    )
    shared_three = exchange(payload_three) if eight else share(payload_three[0])
    fine_keep, fine_send, out_own, out_send = call(
        refiner_grad_body,
        [
            ((8, 5, 64, 128), bf16),
            ((8, 5, 64, 128), bf16),
            ((16, 64, 256), bf16),
            ((16, 64, 256), bf16),
        ],
        (idx, grad_two, held, glu_two, stat_two, pull, gains),
        "refiner_grad",
        scratch=[pltpu.VMEM((9, 256, 256), bf16), pltpu.VMEM((16, 256, 128), bf16)],
        late=(2, 3, 4, 5),
    )
    output = natural(out_own, swap_with(out_send, "chan", 1), 0)
    fine_recv = swap_with(after(fine_send, shared_three), "chan", 1)

    def pair(keep, recv, name):
        return call(
            pair_sum_body,
            [(keep.shape, bf16)],
            (keep, recv),
            name,
            smem=0,
            late=(0, 1),
            cuts={0: 8, 1: 8},
        )[0]

    if eight:
        both = jnp.stack([small[2], theirs[2]], axis=0)
        vectors, combined = call(
            excite_back_body,
            [((32, 128), bf16), ((8, 384, 128), bf16)],
            (
                idx,
                both,
                swap_with(both, "chan", 1),
                squeezed,
                exciter_own,
                exciter_other,
                fine_keep,
                fine_recv,
            ),
            "excite_back",
            deps=(shared_three,),
        )
        parts = over_batch(combined)
        ready = (combined, out_own)
    else:
        refiner_pair = pair(fine_keep, fine_recv, "refiner_pair")
        ready = (refiner_pair, out_own)
        v = refiner_pair.reshape(8, 5, 64, 4, 32).transpose(1, 3, 2, 0, 4).reshape(20, 64, 256)
        v = v[:18].reshape(9, 2, 64, 256).astype(f32)
        refiner_sum = lax.psum_scatter(v, "batch", scatter_dimension=3, tiled=True)

    by_phase = (8, 2, 8, 2, 16, 128)
    grad_one, small_one, wide_keep, wide_send = call(
        make_back_one_body(entries),
        [
            ((2, 2, 10, 10, 16, 256), bf16),
            ((8, 128), f32),
            ((8, 9, 64, 128), bf16),
            ((8, 9, 64, 128), bf16),
        ],
        (
            idx,
            gap,
            logit_one,
            base,
            dh_own.reshape(by_phase),
            dh_other.reshape(by_phase),
            mask,
            stat_one,
            gains,
            shared_three,
            field,
        ),
        "back_one",
        scratch=[pltpu.VMEM((4, 4, 256, 512), f32)],
        deps=ready,
        late=(9,),
    )
    widener_pair = pair(wide_keep, swap_with(wide_send, "chan", 1), "widener_pair")
    if eight:
        widener_pair = after(widener_pair, parts)
        widener_parts = over_batch(widener_pair)
    else:
        v = widener_pair.reshape(8, 9, 64, 2, 64).transpose(1, 3, 2, 0, 4).reshape(9, 2, 64, 512)
        widener_sum = lax.psum_scatter(v.astype(f32), "batch", scatter_dimension=3, tiled=True)
    if eight:
        skip_keep, skip_send = call(
            skip_back_body,
            [((32, 8192), bf16), ((32, 8192), bf16)],
            (idx, vectors, flats),
            "skip_back",
            deps=(widener_pair,),
            late=(1,),
            cuts={1: 8},
        )
    blocks = call(
        input_back_body,
        [((16, 64, 128), bf16)] * 4,
        (idx, grad_one, wide_w),
        "input_back",
        scratch=[pltpu.VMEM((16, 64, 512), bf16)],
        deps=(skip_send,) if eight else (widener_pair,),
        late=(0, 1),
        cuts={0: 2, 1: 4},
    )
    if eight:
        skip_own, skip_other = call(
            skip_add_body,
            [((32, 4096), f32), ((32, 4096), bf16)],
            (idx, skip_keep, swap_with(skip_send, "chan", 2)),
            "skip_add", plain=True,
        )
        blocks = [blocks[0]] + [after(b, skip_other) for b in blocks[1:]]
    got = [blocks[0]] + [swap_with(blocks[k], "chan", k) for k in range(1, 4)]
    if eight:
        exciter_sum, squeezer_sum, refiner_sum = call(
            squeeze_back_body,
            [((64, 32), f32), ((16, 64, 128), f32), (refiner.shape, f32)],
            (parts, skips_all),
            "squeeze_back",
            smem=0,
            deps=(widener_pair,),
        )
        (widener_sum,) = call(
            widener_sum_body,
            [(widener.shape, f32)],
            (widener_parts,),
            "widener_sum",
            smem=0,
        )
        input_grad, skip_grad = call(
            last_join_body,
            [(features.shape, f32), (skip_feature.shape, f32)],
            (idx, *got, skip_own, swap_with(skip_other, "chan", 1)),
            "last_join",
            deps=(widener_sum, squeezer_sum, output),
        )
    else:
        (input_grad,) = call(input_join_body, [(features.shape, f32)], (idx, *got), "input_join")
        lo, hi = small[2, :, :64], small[2, :, 64:]
        keep, send = jnp.where(core == 0, lo, hi), jnp.where(core == 0, hi, lo)
        grad_gate = natural(keep, swap_with(send, "chan", 1), 0)
        grad_excited = (grad_gate * gate * (1.0 - gate)).astype(bf16)
        exciter_grad = jnp.einsum(
            "bo,bc->oc", grad_excited, swish_full, preferred_element_type=f32
        )
        partial_swish = jnp.einsum(
            "bo,oc->bc", grad_excited, exciter_full, preferred_element_type=f32
        )
        grad_swish = lax.psum_scatter(
            partial_swish.astype(bf16), "chan", scatter_dimension=1, tiled=True
        ).astype(f32)
        grad_squeezed = grad_swish * squeeze_sig * (1.0 + squeezed * (1.0 - squeeze_sig))
        grad_squeezed = grad_squeezed.astype(bf16)
        squeezer_grad = jnp.einsum(
            "bo,bct->toc", grad_squeezed, pooled, preferred_element_type=f32
        )
        partial_pooled = jnp.einsum(
            "bo,toc->bct", grad_squeezed, squeezer_full, preferred_element_type=f32
        ).reshape(samples, -1, 128)
        skip_grad = lax.psum_scatter(
            partial_pooled.astype(bf16), "chan", scatter_dimension=1, tiled=True
        ).astype(f32)
        squeezer_sum = lax.psum_scatter(squeezer_grad, "batch", scatter_dimension=2, tiled=True)
        exciter_sum = lax.psum_scatter(exciter_grad, "batch", scatter_dimension=1, tiled=True)

    norms = jnp.concatenate([small_one[0:2], mine[2, 0:2]], axis=0)
    norm_grads = jnp.where(core == 0, norms[:, :64], norms[:, 64:])
    return (
        output,
        input_grad,
        skip_grad,
        widener_sum,
        refiner_sum,
        squeezer_sum,
        exciter_sum,
        norm_grads,
    )


def solution(mesh):
    placed = (
        P("batch", "chan", None),
        P("batch", "chan", None),
        P("batch"),
        P("batch"),
        P(None, None, "chan", "batch"),
        P(None, None, "chan", "batch"),
        P(None, "chan", "batch"),
        P("chan", "batch"),
        P("chan"),
        P("chan"),
        P("chan"),
        P("chan"),
        P("batch", "chan", None),
    )
    return jax.shard_map(
        on_device,
        mesh=mesh,
        in_specs=placed,
        out_specs=(
            P("batch", "chan", None),
            P("batch", "chan", None),
            P("batch", "chan", None),
            P(None, None, "chan", "batch"),
            P(None, None, "chan", "batch"),
            P(None, "chan", "batch"),
            P("chan", "batch"),
            P(None, "chan"),
        ),
        check_vma=False,
    )
```

```python
import jax
import jax.numpy as jnp
from jax import lax
from jax.experimental import pallas as pl
from jax.experimental.pallas import tpu as pltpu
from jax.sharding import PartitionSpec as P

MB = 4
epsilon = 1e-05
f32 = jnp.float32
bf16 = jnp.bfloat16
MIB = 2**20
LIMIT = 58

NT = (((1,), (1,)), ((), ()))
TN = (((0,), (0,)), ((), ()))


def dot(a, b, dims=None):
    if dims is None:
        return jnp.dot(a, b, preferred_element_type=f32)
    return lax.dot_general(a, b, dims, preferred_element_type=f32)


class Traffic:
    def __init__(self, ins, outs, in_sems, out_sems, late, cuts):
        self.ins, self.outs, self.out_sems = [], outs, out_sems
        self.sent = {}
        count = 0
        for k, (pieces, held) in enumerate(ins):
            copies, at = [], 0
            parts = cuts.get(k, 1)
            for piece in pieces:
                rows = piece.shape[0] // parts
                for n in range(parts):
                    src = piece.at[pl.ds(n * rows, rows)]
                    dst = held.at[pl.ds(at, rows)]
                    copies.append(pltpu.make_async_copy(src, dst, in_sems.at[count]))
                    count += 1
                    at += rows
            self.ins.append(copies)
        for copies in self.ins:
            for copy in copies:
                copy.start()
        self.need(*[k for k in range(len(ins)) if k not in late])

    def need(self, *which):
        for k in which:
            for copy in self.ins[k]:
                copy.wait()

    def need_part(self, k, n):
        self.ins[k][n].wait()

    def part(self, k, n, count):
        made, pieces = self.outs[k]
        rows = made.shape[0] // count
        if len(pieces) == 1:
            dst = pieces[0].at[pl.ds(n * rows, rows)]
        else:
            each = pieces[0].shape[0]
            dst = pieces[n * rows // each].at[pl.ds(n * rows % each, rows)]
        return pltpu.make_async_copy(
            made.at[pl.ds(n * rows, rows)], dst, self.out_sems.at[k, n]
        )

    def send(self, k, n=0, count=1):
        self.sent[k] = count
        self.part(k, n, count).start()

    def finish(self):
        for k in range(len(self.outs)):
            if k not in self.sent:
                for n in range(len(self.outs[k][1])):
                    self.send(k, n, len(self.outs[k][1]))
        for k, count in self.sent.items():
            for n in range(count):
                self.part(k, n, count).wait()


def grouped(refs, sizes):
    out, at = [], 0
    for size in sizes:
        out.append(refs[at : at + size])
        at += size
    return out


def call(body, outs, args, name, scratch=(), smem=1, deps=(), late=(), cuts={}, plain=False):
    scalars, args, deps = list(args[:smem]), list(args[smem:]), list(deps)
    args = [a if isinstance(a, tuple) else (a,) for a in args]
    outs = [o if len(o) == 3 else (*o, 1) for o in outs]
    in_sizes, out_sizes = [len(a) for a in args], [o[2] for o in outs]
    n_in, n_out = sum(in_sizes), sum(out_sizes)
    results = [
        jax.ShapeDtypeStruct((shape[0] // count, *shape[1:]), dtype)
        for shape, dtype, count in outs
        for _ in range(count)
    ]
    anywhere, inside = pl.BlockSpec(memory_space=pl.ANY), pl.BlockSpec(memory_space=pltpu.VMEM)

    def kernel(*refs):
        refs = list(refs)
        numbers, refs = refs[:smem], refs[smem:]
        ins, refs = refs[:n_in], refs[n_in + len(deps) :]
        made, refs = refs[:n_out], refs[n_out:]
        if plain:
            body(*numbers, *ins, *made, *refs)
            return
        held, refs = refs[: len(args)], refs[len(args) :]
        work, refs = refs[: len(outs)], refs[len(outs) :]
        traffic = Traffic(
            list(zip(grouped(ins, in_sizes), held)),
            list(zip(work, grouped(made, out_sizes))),
            refs[0],
            refs[1],
            late,
            cuts,
        )
        extra = (traffic,) if late else ()
        body(*extra, *numbers, *held, *work, *refs[2:])
        traffic.finish()

    own = []
    if not plain:
        own = [
            pltpu.VMEM((sum(p.shape[0] for p in a), *a[0].shape[1:]), a[0].dtype) for a in args
        ]
        own += [pltpu.VMEM(shape, dtype) for shape, dtype, _ in outs]
        own += [pltpu.SemaphoreType.DMA((n_in * max([1, *cuts.values()]),)), pltpu.SemaphoreType.DMA((len(outs), 8))]
    got = pl.pallas_call(
        kernel,
        out_shape=results,
        in_specs=[pl.BlockSpec(memory_space=pltpu.SMEM)] * smem
        + [inside if plain else anywhere] * n_in
        + [anywhere] * len(deps),
        out_specs=[inside if plain else anywhere] * n_out,
        scratch_shapes=own + list(scratch),
        compiler_params=pltpu.CompilerParams(
            vmem_limit_bytes=(16 if plain else LIMIT) * MIB
        ),
        cost_estimate=pl.CostEstimate(flops=0, bytes_accessed=0, transcendentals=0),
        name=name,
    )(*scalars, *[p for a in args for p in a], *deps)
    return [p[0] if len(p) == 1 else tuple(p) for p in grouped(list(got), out_sizes)]


def after(value, *deps):
    return pl.pallas_call(
        lambda *refs: None,
        out_shape=jax.ShapeDtypeStruct(value.shape, value.dtype),
        in_specs=[pl.BlockSpec(memory_space=pl.ANY)] * (1 + len(deps)),
        out_specs=pl.BlockSpec(memory_space=pl.ANY),
        input_output_aliases={0: 0},
        name="after",
    )(value, *deps)


def iota(shape, dim):
    return lax.broadcasted_iota(jnp.int32, shape, dim)


def onehot(cond):
    return jnp.where(cond, 1.0, 0.0).astype(f32).astype(bf16)


def eye(n):
    return onehot(iota((n, n), 0) == iota((n, n), 1))


def sixteen_swap():
    r, q = iota((256, 256), 0), iota((256, 256), 1)
    return onehot(((r % 16) == (q // 16)) & ((r // 16) == (q % 16)))


def tree(parts):
    parts = list(parts)
    while len(parts) > 1:
        parts = [parts[n] + parts[n + 1] for n in range(0, len(parts), 2)]
    return parts[0]


def sigmoid(v):
    return 1.0 / (1.0 + jnp.exp(-v))


def pack_wide_body(w, out):
    packed = jnp.concatenate([w[:, 0], w[:, 1]], axis=-1)
    for k in range(8):
        out[k] = packed


def pack_fine_body(r, e, e_other, out):
    slots = [r[q // 2, q % 2] for q in range(18)] + [e[...], e_other[...]]
    for row in range(5):
        out[row] = jnp.concatenate(slots[4 * row : 4 * row + 4], axis=-1)
    out[5:] = jnp.zeros((3, 64, 128), bf16)


def fill_taps(core, own, other, out):
    for blocks, side in ((own, core), (other, 1 - core)):
        for half in range(2):
            rows = pl.ds(pl.multiple_of(half * 128 + side * 64, 64), 64)
            lanes = slice(half * 64, half * 64 + 64)
            for group in range(4):
                w = [
                    jnp.concatenate(
                        [blocks[2 * group][t][:, lanes], blocks[2 * group + 1][t][:, lanes]],
                        axis=-1,
                    ).astype(f32)
                    for t in range(9)
                ]
                down = {
                    (0, 0): w[0:3],
                    (0, 1): [w[3 + s] + w[6 + s] for s in range(3)],
                    (1, 0): [w[s] + w[3 + s] for s in range(3)],
                    (1, 1): w[6:9],
                }
                for a in range(2):
                    for u in range(2):
                        d = down[(a, u)]
                        across = {
                            (0, 0): d[0],
                            (0, 1): d[1] + d[2],
                            (1, 0): d[0] + d[1],
                            (1, 1): d[2],
                        }
                        for b in range(2):
                            for v in range(2):
                                out[
                                    a * 8 + b * 4 + u * 2 + v,
                                    rows,
                                    group * 128 : group * 128 + 128,
                                ] = across[(b, v)].astype(bf16)


def refiner_body(idx, own, other, out, ex, ex_other):
    core = idx[1]
    for blocks, side in ((own, core), (other, 1 - core)):
        rows = pl.multiple_of(side * 64, 64)
        for q in range(20):
            lanes = slice((q % 4) * 32, (q % 4) * 32 + 32)
            piece = jnp.concatenate([blocks[k, q // 4][:, lanes] for k in range(8)], axis=-1)
            if q < 18:
                out[q // 2, pl.ds(rows + (q % 2) * 128, 64), :] = piece
            else:
                (ex, ex_other)[q - 18][pl.ds(rows, 64), :] = piece


def feature_select(place):
    r, q = iota((512, 512), 0), iota((512, 512), 1)
    kept = r % 256
    return onehot((((kept // 64) ^ place) * 64 + kept % 64) * 2 + r // 256 == q)


def feature_body(idx, b0, b1, b2, b3, out, turned):
    ident = eye(128)

    def turn(s, carry):
        x = jnp.concatenate([b0[s], b1[s], b2[s], b3[s]], axis=0)
        t = dot(ident, x, NT).astype(bf16)
        turned[s] = jnp.concatenate([t[:64], t[64:]], axis=-1)
        return carry

    lax.fori_loop(0, 16, turn, 0, unroll=4)
    swap = sixteen_swap()
    select = feature_select(idx[0])
    zero = jnp.zeros((10, 16, 512), bf16)
    out[0] = zero
    out[9] = zero
    out[:, 0] = zero
    out[:, 9] = zero
    for block in range(4):
        a = turned[:, block * 16 : block * 16 + 16, :].reshape(256, 512)
        c = dot(dot(swap, a).astype(bf16), select).astype(bf16)
        out[1 + 2 * block : 3 + 2 * block, 1:9] = c.reshape(2, 8, 16, 512)


def input_back_body(io, idx, d, w, b0, b1, b2, b3, turned):
    swap = sixteen_swap()
    select = feature_select(idx[0])

    acc = None
    for a in range(2):
        io.need_part(0, a)
        for b in range(2):
            io.need_part(1, 2 * a + b)
            lhs = jnp.concatenate(
                [
                    d[a, b, 2 - u - a : 10 - u - a, 2 - v - b : 10 - v - b].reshape(1024, 256)
                    for u in range(2)
                    for v in range(2)
                ],
                axis=-1,
            )
            first = a * 8 + b * 4
            term = dot(lhs, w[first : first + 4].reshape(1024, 512))
            acc = term if acc is None else acc + term
    x = dot(acc.astype(bf16), select, NT).astype(bf16)
    for block in range(4):
        t = dot(swap, x[block * 256 : block * 256 + 256]).astype(bf16)
        turned[:, block * 16 : block * 16 + 16, :] = t.reshape(16, 16, 512)
    ident = eye(256)

    def turn(s, carry):
        t = turned[s]
        t = jnp.concatenate([t[:, :256], t[:, 256:]], axis=0)
        o = dot(ident, t, NT).astype(bf16)
        b0[s] = o[0:64]
        b1[s] = o[64:128]
        b2[s] = o[128:192]
        b3[s] = o[192:256]
        return carry

    lax.fori_loop(0, 16, turn, 0, unroll=4)


def input_join_body(idx, b0, b1, b2, b3, out):
    at = pl.multiple_of(idx[1] * 16, 16)
    out[pl.ds(at, 16)] = b0[...].astype(f32) + b2[...].astype(f32)
    out[pl.ds(16 - at, 16)] = b1[...].astype(f32) + b3[...].astype(f32)


def upstream_body(idx, own, other, out, turned):
    first = idx[1] == 0
    ident = eye(256)

    def turn(s, carry):
        p, q = own[s], other[s]
        lo = jnp.where(first, p, q)
        hi = jnp.where(first, q, p)
        turned[s] = dot(ident, jnp.concatenate([lo, hi], axis=0), NT).astype(bf16)
        return carry

    lax.fori_loop(0, 16, turn, 0, unroll=4)
    swap = sixteen_swap()

    def mix(y, carry):
        a = turned[:, pl.ds(pl.multiple_of(y * 16, 16), 16), :].reshape(256, 128)
        out[y] = dot(swap, a).astype(bf16).reshape(16, 16, 128)
        return carry

    lax.fori_loop(0, 16, mix, 0, unroll=4)


def over_samples(mask, values):
    return jnp.concatenate(
        [jnp.sum(mask[m] * values, axis=0, keepdims=True) for m in range(MB)], axis=0
    )


def per_sample(mask, rows):
    return sum(mask[m] * rows[m : m + 1] for m in range(MB))


def local_stats(mask, mean_s, squares_s):
    ones = jnp.ones_like(mean_s)
    n = over_samples(mask, ones) * 256.0
    mean = over_samples(mask, mean_s) * 256.0 / jnp.maximum(n, 1.0)
    gap = mean_s - per_sample(mask, mean)
    squares = over_samples(mask, squares_s + 256.0 * gap * gap)
    return n, mean, squares


def total_stats(messages, entries):
    parts = [(g[0:4], g[4:8], g[8:12]) for g in messages]
    mean = tree([n * m for n, m, _ in parts]) / entries
    squares = tree([q + n * (m - mean) * (m - mean) for n, m, q in parts])
    inverse = lax.rsqrt(squares / entries + epsilon)
    return mean, inverse


def message_list(refs):
    return [ref[c] for ref in refs for c in range(ref.shape[0])]


def conv_one_body(io, idx, own, other, x, mask, gap, logit, base, msg, w, glu):
    fill_taps(idx[1], own, other, w)
    io.send(4)
    io.need(2, 3)
    total = jnp.zeros((16, 128), f32)
    for a in range(2):
        for b in range(2):
            kept = []
            for u in range(2):
                for v in range(2):
                    kept.append(x[u + a : u + a + 8, v + b : v + b + 8].reshape(1024, 512))
            first = a * 8 + b * 4
            rhs = jnp.concatenate([w[first + n] for n in range(4)], axis=-1)
            c = dot(jnp.concatenate(kept, axis=-1), rhs, NT)
            g = (c[:, :128] * sigmoid(c[:, 128:])).reshape(8, 8, 16, 128)
            logit[:, a, :, b] = c[:, 128:].reshape(8, 8, 16, 128).astype(bf16)
            glu[a, b] = g
            total = total + jnp.sum(g, axis=(0, 1))
    io.send(1)
    mean_s = total * (1.0 / 256.0)
    base[...] = mean_s
    io.send(2)

    squares = jnp.zeros((16, 128), f32)
    for i in range(8):
        for a in range(2):
            for b in range(2):
                d = glu[a, b, i] - mean_s[None]
                gap[i, a, :, b] = d.astype(bf16)
                squares = squares + jnp.sum(d * d, axis=0)
        io.send(0, i, 8)
    n, mean, squares = local_stats(mask[...], mean_s, squares)
    msg[0:4] = n
    msg[4:8] = mean
    msg[8:12] = squares
    msg[12:16] = jnp.zeros((4, 128), f32)


def make_scale_body(entries):
    def body(idx, mask, gains, base, messages, line, stat):
        mean, inverse = total_stats(message_list([messages]), entries)
        m = mask[...]
        mean_s, inverse_s = per_sample(m, mean), per_sample(m, inverse)
        stat[0] = base[...] - mean_s
        stat[1] = inverse_s
        scale = inverse_s * gains[0:1]
        line[0] = scale
        line[1] = (base[...] - mean_s) * scale + gains[1:2]
        if messages.shape[0] == 16 and messages.shape[1] == 32:
            core = idx[1]
            line[2, 0:8] = tree([messages[2 * k + core, 16:24] for k in range(8)])
            line[2, 8:16] = tree([messages[2 * k + core, 24:32] for k in range(8)])
        else:
            line[2] = jnp.zeros((16, 128), f32)

    return body


def conv_two_body(io, idx, own, other, line, line_other, w, up, held, glu, logit, sums):
    zero = jnp.zeros((18, 16, 256), bf16)
    held[0] = zero
    held[17] = zero
    held[:, 0] = zero
    held[:, 17] = zero

    def fill(y, carry):
        for gap, scale, side in ((own, line, idx[2]), (other, line_other, 1 - idx[2])):
            h = gap[y].astype(f32) * scale[0] + scale[1]
            lanes = pl.ds(pl.multiple_of(side * 128, 128), 128)
            held[y + 1, 1:17, :, lanes] = h.astype(bf16)
        return carry

    lax.fori_loop(0, 16, fill, 0, unroll=2)
    io.send(0)
    io.need(4)

    def rows(step, total):
        y = step * 4
        lhs = jnp.concatenate(
            [
                held[pl.ds(y + t // 3, 4), t % 3 : t % 3 + 16].reshape(1024, 256)
                for t in range(9)
            ],
            axis=-1,
        )
        rhs = jnp.concatenate([w[t] for t in range(9)], axis=-1)
        c = dot(lhs, rhs, NT)
        g = (c[:, :128] * sigmoid(c[:, 128:])).reshape(4, 16, 16, 128)
        logit[pl.ds(y, 4)] = c[:, 128:].reshape(4, 16, 16, 128).astype(bf16)
        glu[pl.ds(y, 4)] = g
        io.send(1, step, 4)
        io.send(2, step, 4)
        return total + jnp.sum(g, axis=(0, 1))

    total = lax.fori_loop(0, 4, rows, jnp.zeros((16, 128), f32), unroll=True)
    mean_s = total * (1.0 / 256.0)

    io.need(5)

    def spread(y, acc):
        gap = glu[y] - mean_s[None]
        u = up[y].astype(f32)
        return (
            acc[0] + jnp.sum(gap * gap, axis=0),
            acc[1] + jnp.sum(u, axis=0),
            acc[2] + jnp.sum(u * gap, axis=0),
        )

    none = jnp.zeros((16, 128), f32)
    squares, plain, cross = lax.fori_loop(0, 16, spread, (none, none, none))
    sums[0] = mean_s
    sums[1] = plain
    sums[2] = cross
    sums[3] = squares


def make_back_two_body(entries):
    def body(io, idx, glu, logit, up, mask, pull, gains, sums, w, gap, gap_other, messages, *outs):
        grad, own, other, small, stat, mine = outs
        messages = message_list([messages])
        mean, inverse = total_stats(messages, entries)
        plain = tree([g[12:16] for g in messages])
        cross = inverse * tree([g[16:20] + g[12:16] * (g[4:8] - mean) for g in messages])
        m = mask[...]
        mean_s, inverse_s = per_sample(m, mean), per_sample(m, inverse)
        gain, shift = gains[2:3], gains[3:4]
        stat[0] = mean_s
        stat[1] = inverse_s
        weight, gate = pull[0], pull[1]
        centred = sums[2] + sums[1] * (sums[0] - mean_s)
        small[2] = weight * (gain * inverse_s * centred + shift * sums[1])
        mine[2, 0:1] = jnp.sum(cross, axis=0, keepdims=True)
        mine[2, 1:2] = jnp.sum(plain, axis=0, keepdims=True)
        mine[2, 2:] = jnp.zeros((14, 128), f32)
        plain_s = per_sample(m, plain) * (1.0 / entries)
        cross_s = per_sample(m, cross) * (1.0 / entries)
        scale = inverse_s * gain
        factor = weight * gate
        io.need(0, 1, 2)
        zero = jnp.zeros((18, 16, 256), bf16)
        grad[0] = zero
        grad[17] = zero
        grad[:, 0] = zero
        grad[:, 17] = zero

        def step(y, carry):
            g = glu[y]
            s = sigmoid(logit[y].astype(f32))
            hat = (g - mean_s) * inverse_s
            d = scale * (up[y].astype(f32) * factor - plain_s - hat * cross_s)
            grad[y + 1, 1:17, :, 0:128] = (d * s).astype(bf16)
            grad[y + 1, 1:17, :, 128:256] = (d * g * (1.0 - s)).astype(bf16)
            return carry

        lax.fori_loop(0, 16, step, 0, unroll=2)
        io.send(0)
        io.need(7, 8, 9)

        def rows(step, acc):
            y = step * 4
            lhs = jnp.concatenate(
                [
                    grad[pl.ds(y + 2 - t // 3, 4), 2 - t % 3 : 18 - t % 3].reshape(1024, 256)
                    for t in range(9)
                ],
                axis=-1,
            )
            c = dot(lhs, w[...].reshape(2304, 256)).astype(bf16)
            out = []
            first = idx[2] == 0
            mine_c = jnp.where(first, c[:, :128], c[:, 128:])
            their_c = jnp.where(first, c[:, 128:], c[:, :128])
            for k, ref, at, d in ((1, own, gap, mine_c), (2, other, gap_other, their_c)):
                d = d.reshape(4, 16, 16, 128)
                ref[pl.ds(y, 4)] = d
                io.send(k, step, 4)
                d = d.astype(f32)
                out.append(jnp.sum(d, axis=(0, 1)))
                out.append(jnp.sum(d * at[pl.ds(y, 4)].astype(f32), axis=(0, 1)))
            return tuple(p + q for p, q in zip(acc, out))

        none = jnp.zeros((16, 128), f32)
        mine[0], mine[1], small[0], small[1] = lax.fori_loop(
            0, 4, rows, (none,) * 4, unroll=True
        )

    return body


def output_part(idx, glu, stat, pull, gains, own, other, turned):
    swap = sixteen_swap()
    mean_s, inverse_s = stat[0], stat[1]
    gain, shift = gains[2:3], gains[3:4]
    gate = pull[1]

    def step(y, carry):
        o = (((glu[y] - mean_s) * inverse_s) * gain + shift) * gate
        o = dot(swap, o.astype(bf16).reshape(256, 128)).astype(bf16)
        turned[:, pl.ds(pl.multiple_of(y * 16, 16), 16), :] = o.reshape(16, 16, 128)
        return carry

    lax.fori_loop(0, 16, step, 0, unroll=4)
    ident = eye(128)
    first = idx[1] == 0

    def turn(s, carry):
        t = dot(ident, turned[s], NT).astype(bf16)
        own[s] = jnp.where(first, t[:64], t[64:])
        other[s] = jnp.where(first, t[64:], t[:64])
        return carry

    lax.fori_loop(0, 16, turn, 0, unroll=4)


def refiner_grad_body(
    io, idx, grad, held, glu, stat, pull, gains, own, other, out_own, out_other, work, turned
):
    core = idx[1]

    def tap(t, carry):
        d = grad[1:17, 1:17].reshape(4096, 256)
        h = held[pl.ds(t // 3, 16), pl.ds(t % 3, 16)].reshape(4096, 256)
        work[t] = dot(d, h, TN).astype(bf16)
        return carry

    lax.fori_loop(0, 9, tap, 0, unroll=3)
    for out, side in ((own, core), (other, 1 - core)):
        start = pl.multiple_of(side * 64, 64)
        for row in range(5):
            pieces = [
                work[q // 2, pl.ds(start + (q % 2) * 128, 64), :]
                for q in range(4 * row, min(4 * row + 4, 18))
            ]
            pieces += [jnp.zeros((64, 256), bf16)] * (4 - len(pieces))
            for k in range(8):
                lanes = slice(k * 32, k * 32 + 32)
                out[k, row] = jnp.concatenate([p[:, lanes] for p in pieces], axis=-1)
    io.send(0)
    io.send(1)
    io.need(2, 3, 4, 5)
    output_part(idx, glu, stat, pull, gains, out_own, out_other, turned)


def refiner_sum_body(parts, out):
    total = tree([parts[k, :320].astype(f32) for k in range(8)])
    for row in range(5):
        turned = total[row * 64 : row * 64 + 64].T
        for q in range(4 * row, min(4 * row + 4, 18)):
            out[q // 2, q % 2] = turned[(q % 4) * 32 : (q % 4) * 32 + 32]


def first_sums_body(mine, theirs, mask, stat, payload):
    m = mask[...]
    plain = mine[0] + theirs[0]
    cross = mine[1] + theirs[1] + stat[0] * plain
    msg = jnp.concatenate([over_samples(m, plain), over_samples(m, cross * stat[1])], axis=0)
    for k in range(payload.shape[0]):
        payload[k] = msg


def make_back_one_body(entries):
    def body(
        io,
        idx,
        gap,
        logit,
        base,
        own,
        other,
        mask,
        stat,
        gains,
        messages,
        x,
        grad,
        small,
        keep,
        send,
        work,
    ):
        messages = message_list([messages])
        plain = tree([g[0:4] for g in messages])
        cross = tree([g[4:8] for g in messages])
        small[0:1] = jnp.sum(cross, axis=0, keepdims=True)
        small[1:2] = jnp.sum(plain, axis=0, keepdims=True)
        small[2:8] = jnp.zeros((6, 128), f32)
        io.send(1)
        m = mask[...]
        plain_s = per_sample(m, plain) * (1.0 / entries)
        cross_s = per_sample(m, cross) * (1.0 / entries)
        shift_s, inverse_s = stat[0], stat[1]
        mean = base[...]
        scale = inverse_s * gains[0:1]
        zero = jnp.zeros((10, 16, 256), bf16)
        for a in range(2):
            for b in range(2):
                grad[a, b, 0] = zero
                grad[a, b, 9] = zero
                grad[a, b, :, 0] = zero
                grad[a, b, :, 9] = zero

        def step(i, carry):
            for a in range(2):
                for b in range(2):
                    g = gap[i, a, :, b].astype(f32)
                    s = sigmoid(logit[i, a, :, b].astype(f32))
                    hat = (g + shift_s) * inverse_s
                    g = g + mean
                    d = own[i, a, :, b].astype(f32) + other[i, a, :, b].astype(f32)
                    d = scale * (d - plain_s - hat * cross_s)
                    grad[a, b, i + 1, 1:9, :, 0:128] = (d * s).astype(bf16)
                    grad[a, b, i + 1, 1:9, :, 128:256] = (d * g * (1.0 - s)).astype(bf16)
            return carry

        lax.fori_loop(0, 8, step, 0)
        io.send(0)
        io.need(9)
        widener_grad(idx[1], grad, x, keep, send, work)

    return body


def widener_grad(core, grad, x, own, other, work):
    def phase(n, carry):
        a, b = n // 2, n % 2
        d = grad[a, b, 1:9, 1:9].reshape(1024, 256)
        for u in range(2):
            for v in range(2):
                f = x[pl.ds(u + a, 8), pl.ds(v + b, 8)].reshape(1024, 512)
                work[n, 2 * u + v] = dot(d, f, TN)
        return carry

    lax.fori_loop(0, 4, phase, 0, unroll=2)
    source = {0: (0, 0), 1: (1, 0), 2: (1, 1)}
    for out, side in ((own, core), (other, 1 - core)):
        start = pl.multiple_of(side * 64, 64)
        for pair in range(4):
            lanes = slice(pair * 128, pair * 128 + 128)
            for r in range(3):
                for s in range(3):
                    both = []
                    for half in range(2):
                        rows = pl.ds(start + half * 128, 64)
                        both.append(
                            sum(
                                work[2 * a + b, 2 * source[r][a] + source[s][b], rows, lanes]
                                for a in range(2)
                                for b in range(2)
                            )
                        )
                    first, second = both
                    out[2 * pair, 3 * r + s] = jnp.concatenate(
                        [first[:, :64], second[:, :64]], axis=-1
                    ).astype(bf16)
                    out[2 * pair + 1, 3 * r + s] = jnp.concatenate(
                        [first[:, 64:], second[:, 64:]], axis=-1
                    ).astype(bf16)


def pair_sum_body(io, own, other, out):
    for k in range(8):
        io.need_part(0, k)
        io.need_part(1, k)
        out[k] = (own[k].astype(f32) + other[k].astype(f32)).astype(bf16)
        io.send(0, k, 8)


def widener_sum_body(parts, out):
    for t in range(9):
        total = tree([parts[k, t].astype(f32) for k in range(8)])
        out[t, 0] = total[:, :64]
        out[t, 1] = total[:, 64:]


def skip_quarter_body(idx, skip, out):
    rows = pl.ds(pl.multiple_of(idx[0] * 8, 8), 8)
    for i in range(8):
        out[i] = skip[rows, i * 16 : i * 16 + 16, :]


def squeeze_body(skip, kernels, msg, kept, out, rows):
    rows[...] = skip[...].astype(f32).reshape(1024, 128)
    for k in range(16):
        kept[:, k * 128 : k * 128 + 128] = rows[pl.ds(k, 64, stride=16), :].astype(bf16)
    part = dot(kept[...], kernels[...], NT)
    for i in range(8):
        for c in range(2):
            out[2 * i + c, 0:16] = msg[...]
            out[2 * i + c, 16:24] = part[i * 8 : i * 8 + 8, :128]
            out[2 * i + c, 24:32] = part[i * 8 : i * 8 + 8, 128:]


def gate_body(idx, s0, s1, s2, s3, ex, weight, out, squeezed):
    j, core = idx[0], idx[1]
    for n, part in enumerate((s0, s1, s2, s3)):
        rows = pl.ds(pl.multiple_of((j ^ n) * 8, 8), 8)
        squeezed[rows, :128] = part[2, 0:8]
        squeezed[rows, 128:] = part[2, 8:16]
    mine = squeezed[pl.ds(pl.multiple_of(core * 16, 16), 16), :]
    excited = dot((mine * sigmoid(mine)).astype(bf16), ex[...], NT)
    out[0] = weight[...]
    out[1] = sigmoid(excited)


def gate_message_body(idx, s0, s1, s2, s3, ex, weight, mask, sums, out, squeezed, payload):
    gate_body(idx, s0, s1, s2, s3, ex, weight, out, squeezed)
    message_two_body(mask, out, sums, payload)


def message_two_body(mask, pull, sums, payload):
    mean_s, plain, cross = sums[0], sums[1], sums[2]
    m = mask[...]
    n, mean, squares = local_stats(m, mean_s, sums[3])
    factor = pull[0] * pull[1]
    spread = over_samples(m, factor * (cross + plain * (mean_s - per_sample(m, mean))))
    rows = [n, mean, squares, over_samples(m, factor * plain), spread, jnp.zeros((4, 128), f32)]
    msg = jnp.concatenate(rows, axis=0)
    for k in range(payload.shape[0]):
        payload[k] = msg


def excite_back_body(idx, g0, g1, squeezed, ex_own, ex_other, fine, recv, vectors, out):
    chip = idx[2]
    s = squeezed[...]
    sigm = sigmoid(s)
    swish = (s * sigm).astype(bf16)
    mine, theirs = ex_own[...], ex_other[...]
    ex = jnp.where(
        chip == 0, jnp.concatenate([mine, theirs], axis=0), jnp.concatenate([theirs, mine], axis=0)
    )
    gate = sigmoid(dot(swish, ex, NT))
    core = idx[1]
    rows = []
    for half in range(2):
        own = jnp.where(core == half, g0[0], g1[0])
        other = jnp.where(core == half, g0[1], g1[1])
        lo, hi = jnp.where(chip == 0, own, other), jnp.where(chip == 0, other, own)
        rows.append(jnp.concatenate([lo, hi], axis=-1))
    grad_gate = jnp.concatenate(rows, axis=0)
    d_excited = (grad_gate * gate * (1.0 - gate)).astype(bf16)
    d_swish = dot(d_excited, ex)
    d_squeezed = d_swish * (sigm * (1.0 + s * (1.0 - sigm)))
    j = idx[0]
    pick_out = onehot(iota((256, 64), 0) == iota((256, 64), 1) + j * 64)
    both = jnp.concatenate(
        [dot(d_squeezed.astype(bf16), pick_out), dot(d_excited, pick_out)], axis=-1
    ).astype(bf16)
    vectors[...] = both
    pick_in = onehot((iota((256, 1024), 0) // 32 == iota((256, 1024), 1) // 128)
                     & (iota((256, 1024), 0) % 32 == iota((256, 1024), 1) % 128))
    picked = dot(swish, pick_in).astype(bf16)
    total = (fine[...].astype(f32) + recv[...].astype(f32)).astype(bf16)
    out[:, :320] = total.reshape(8, 320, 128)
    for k in range(8):
        out[k, 320:352] = both
        out[k, 352:384] = picked[:, k * 128 : k * 128 + 128]


def quarters_first(v):
    v = v.astype(f32)
    return jnp.concatenate(
        [v[i * 32 + q * 8 : i * 32 + q * 8 + 8] for q in range(4) for i in range(8)], axis=0
    )


def squeeze_back_body(parts, skips, ex_grad, sq_grad, refiner_out):
    refiner_sum_body(parts, refiner_out)
    vectors = jnp.concatenate([parts[k, 320:352] for k in range(8)], axis=0)
    swish = jnp.concatenate([parts[k, 352:384] for k in range(8)], axis=0)
    ex_grad[...] = dot(swish, vectors, TN)[:32, 64:]
    grad = dot(quarters_first(vectors).astype(bf16), skips[...], TN)
    for t in range(16):
        sq_grad[t] = grad[:64, t * 128 : t * 128 + 128]


def skip_back_body(io, idx, vectors, kernels, keep, send):
    d = vectors[:, :64]
    for i in range(8):
        io.need_part(1, i)
        pooled = dot(d, kernels[i * 64 : i * 64 + 64, :]).astype(bf16)
        lanes = slice((i % 4) * 2048, (i % 4) * 2048 + 2048)
        mine = idx[2] == i // 4

        @pl.when(mine)
        def _():
            keep[:, lanes] = pooled

        @pl.when(jnp.logical_not(mine))
        def _():
            send[:, lanes] = pooled


def skip_add_body(idx, own, other, keep, send):
    first = idx[1] == 0
    total = own[...].astype(f32) + other[...].astype(f32)
    lo, hi = total[:, :4096], total[:, 4096:]
    keep[...] = jnp.where(first, lo, hi)
    send[...] = jnp.where(first, hi, lo).astype(bf16)


def last_join_body(idx, b0, b1, b2, b3, own, other, out, skip):
    input_join_body(idx, b0, b1, b2, b3, out)
    for r in range(32):
        lanes = slice(r * 128, r * 128 + 128)
        skip[:, r, :] = own[:, lanes] + other[:, lanes].astype(f32)


def swap_with(v, axis, k):
    return lax.ppermute(v, axis, [(n, n ^ k) for n in range(lax.axis_size(axis))])


def on_device(
    features,
    skip_feature,
    section_ids,
    micro_ids,
    widener,
    refiner,
    squeezer,
    exciter,
    gain_one,
    bias_one,
    gain_two,
    bias_two,
    upstream,
):
    nb = lax.axis_size("batch")
    eight = nb == 8
    samples = features.shape[0]
    entries = float(samples * nb // MB * 256)
    i = lax.axis_index("batch")
    j = lax.axis_index("chan")
    core, chip = j % 2, j // 2
    idx = jnp.stack([j, core, chip, i]).astype(jnp.int32)

    def half(v, which):
        return lax.dynamic_slice_in_dim(v, which * 16, 16, axis=0)

    def natural(own, other, axis):
        return jnp.where(
            core == 0,
            jnp.concatenate([own, other], axis=axis),
            jnp.concatenate([other, own], axis=axis),
        )

    def over_batch(v):
        return lax.all_to_all(v, "batch", 0, 0, tiled=True)

    f_keep, f_send = half(features, core), half(features, 1 - core)
    f_blocks = [f_keep] + [
        swap_with(f_send if k % 2 else f_keep, "chan", k) for k in range(1, 4)
    ]
    if eight:
        (wide,) = call(
            pack_wide_body, [((8, 9, 64, 128), bf16)], (widener,), "pack_wide", smem=0, plain=True
        )
        wide_own = over_batch(wide)
    else:
        w_all = lax.all_gather(widener, "batch", axis=3, tiled=True)
        wide_own = w_all.reshape(9, 2, 64, 8, 64).transpose(3, 0, 2, 1, 4).reshape(8, 9, 64, 128)

    gains = jnp.stack([gain_one, bias_one, gain_two, bias_two], axis=0)
    gains = natural(gains, swap_with(gains, "chan", 1), 1)
    ids = half(micro_ids, core)
    mask = jnp.broadcast_to(
        (ids[None, :, None] == jnp.arange(MB, dtype=jnp.int32)[:, None, None]).astype(f32),
        (MB, 16, 128),
    )
    weight_of = jnp.where(section_ids == 0, 1.0, jnp.where(section_ids == 1, 2.0, 4.0)).astype(f32)
    weight = jnp.broadcast_to(half(weight_of, core)[:, None], (16, 128))

    groups = [[n * 4 + 2 * x + c for n in range(nb) for c in range(2)] for x in range(2)]

    def exchange(copies):
        return lax.all_to_all(
            copies, ("batch", "chan"), 0, 0, tiled=True, axis_index_groups=groups
        )

    def share(msg):
        if eight:
            return exchange(jnp.broadcast_to(msg, (16,) + msg.shape))
        pair = jnp.stack([msg, swap_with(msg, "chan", 1)], axis=0)
        return lax.all_gather(pair, "batch").reshape((-1,) + msg.shape)

    u_keep = half(upstream, core)
    u_other = swap_with(half(upstream, 1 - core), "chan", 1)
    (up,) = call(
        upstream_body,
        [((16, 16, 16, 128), bf16)],
        (idx, u_keep, u_other),
        "upstream_turned",
        scratch=[pltpu.VMEM((16, 256, 128), bf16)],
    )
    (field,) = call(
        feature_body,
        [((10, 10, 16, 512), bf16)],
        (idx, *f_blocks),
        "features_turned",
        scratch=[pltpu.VMEM((16, 64, 512), bf16)],
        deps=(up, gains, mask, weight),
    )
    if eight:
        by_tap = skip_feature.reshape(32, 2, 16, 8, 16).transpose(0, 1, 4, 2, 3)
        skip_full = lax.all_gather(by_tap.reshape(32, 32, 128), "chan", axis=1, tiled=True)
        flat = squeezer.reshape(16, 64, 16, 8).transpose(1, 2, 3, 0).reshape(64, 2048)
        squeezer_whole = lax.all_gather(
            squeezer.transpose(1, 0, 2).reshape(64, 2048), "chan", axis=0, tiled=True
        )
        (quarter,) = call(
            skip_quarter_body,
            [((8, 8, 16, 128), bf16)],
            (idx, skip_full),
            "skip_quarter", plain=True,
        )
        wide_own = after(wide_own, field, quarter)
        quarter = over_batch(after(quarter, wide_own))

        (fine,) = call(
            pack_fine_body,
            [((8, 64, 128), bf16)],
            (refiner, exciter, swap_with(exciter, "chan", 2)),
            "pack_fine",
            smem=0, plain=True,
            deps=(field,),
        )
        fine_own = lax.all_gather(fine, "batch")
    else:
        r_all = lax.all_gather(refiner, "batch", axis=3, tiled=True)
        e_all = lax.all_gather(exciter, "batch", axis=1, tiled=True)
        r_all = jnp.concatenate(
            [r_all.reshape(18, 64, 256), e_all[None], jnp.zeros((1, 64, 256), bf16)], axis=0
        )
        r_all = r_all.reshape(5, 4, 64, 8, 32).transpose(3, 0, 2, 1, 4).reshape(8, 5, 64, 128)
        fine_own = jnp.pad(r_all, ((0, 0), (0, 3), (0, 0), (0, 0)))

    wide_other = swap_with(wide_own, "chan", 1)
    gap, logit_one, base, msg_one, wide_w = call(
        conv_one_body,
        [
            ((8, 2, 8, 2, 16, 128), bf16, 2),
            ((8, 2, 8, 2, 16, 128), bf16),
            ((16, 128), f32),
            ((16, 128), f32),
            ((16, 256, 512), bf16),
        ],
        (idx, wide_own, wide_other, field, mask),
        "conv_one",
        scratch=[pltpu.VMEM((2, 2, 8, 8, 16, 128), f32)],
        late=(2, 3),
    )
    gap_other = tuple(swap_with(v, "chan", 2).reshape(8, 16, 16, 128) for v in gap)
    gap_flat = tuple(v.reshape(8, 16, 16, 128) for v in gap)

    if eight:
        skips, payload = call(
            squeeze_body,
            [((64, 2048), bf16), ((16, 32, 128), f32)],
            (quarter, squeezer_whole, msg_one),
            "squeeze",
            scratch=[pltpu.VMEM((1024, 128), f32)],
            smem=0,
        )
        shared_one = exchange(payload)
    else:
        shared_one = share(msg_one)
    shared_one = after(shared_one, *gap_other)
    line, stat_one = call(
        make_scale_body(entries),
        [((3, 16, 128), f32), ((2, 16, 128), f32)],
        (idx, mask, gains, base, shared_one),
        "scale",
        plain=True,
    )
    fine_own = after(fine_own, shared_one)
    fine_other = swap_with(fine_own, "chan", 1)
    fine_w, exciter_own, exciter_other = call(
        refiner_body,
        [((9, 256, 256), bf16), ((128, 256), bf16), ((128, 256), bf16)],
        (idx, fine_own, fine_other),
        "refiner_taps", plain=True,
    )
    line_other = swap_with(line, "chan", 2)
    if eight:
        squeezed = (line, swap_with(line, "chan", 1), line_other, swap_with(line_other, "chan", 1))
        skips_all = lax.all_gather(after(skips, line_other), "chan", axis=0, tiled=True)

    held, glu_two, logit_two, sums_two = call(
        conv_two_body,
        [
            ((18, 18, 16, 256), bf16),
            ((16, 16, 16, 128), f32),
            ((16, 16, 16, 128), bf16),
            ((4, 16, 128), f32),
        ],
        (idx, gap_flat, gap_other, line, line_other, fine_w, up),
        "conv_two",
        late=(4, 5),
    )
    if eight:
        pull, squeezed, payload_two = call(
            gate_message_body,
            [((2, 16, 128), f32), ((32, 256), f32), ((16, 24, 128), f32)],
            (idx, *squeezed, exciter_own, weight, mask, sums_two),
            "gate",
        )
        shared_two = exchange(payload_two)
    else:
        skip_full = lax.all_gather(skip_feature, "chan", axis=1, tiled=True)
        squeezer_full = lax.all_gather(squeezer, "batch", axis=2, tiled=True)
        pooled = skip_full.reshape(samples, -1, 16)
        squeezed = jnp.einsum("toc,bct->bo", squeezer_full, pooled, preferred_element_type=f32)
        squeeze_sig = jax.nn.sigmoid(squeezed)
        swish = (squeezed * squeeze_sig).astype(bf16)
        swish_full = lax.all_gather(swish, "chan", axis=1, tiled=True)
        exciter_full = lax.all_gather(exciter, "batch", axis=1, tiled=True)
        excited = jnp.einsum("oc,bc->bo", exciter_full, swish_full, preferred_element_type=f32)
        gate = jax.nn.sigmoid(excited)
        gate_mine = natural(half(gate, core), swap_with(half(gate, 1 - core), "chan", 1), 1)
        pull = jnp.stack([weight, gate_mine], axis=0)
        (msg_two,) = call(
            message_two_body, [((1, 24, 128), f32)], (mask, pull, sums_two), "message", smem=0
        )
        shared_two = share(msg_two[0])
    if eight:
        flats = lax.all_gather(after(flat, shared_two), "batch", axis=0, tiled=True)
    grad_two, dh_own, dh_send, small, stat_two, mine = call(
        make_back_two_body(entries),
        [
            ((18, 18, 16, 256), bf16),
            ((16, 16, 16, 128), bf16),
            ((16, 16, 16, 128), bf16),
            ((3, 16, 128), f32),
            ((2, 16, 128), f32),
            ((3, 16, 128), f32),
        ],
        (
            idx,
            glu_two,
            logit_two,
            up,
            mask,
            pull,
            gains,
            sums_two,
            fine_w,
            gap_flat,
            gap_other,
            shared_two,
        ),
        "back_two",
        deps=(skips_all,) if eight else (),
        late=(0, 1, 2, 7, 8, 9),
    )
    theirs = swap_with(small, "chan", 2)
    dh_other = swap_with(after(dh_send, theirs), "chan", 2)
    (payload_three,) = call(
        first_sums_body,
        [((16 if eight else 1, 8, 128), f32)],
        (mine, theirs, mask, stat_one),
        "first_sums",
        smem=0,
        plain=True,
    )
    shared_three = exchange(payload_three) if eight else share(payload_three[0])
    fine_keep, fine_send, out_own, out_send = call(
        refiner_grad_body,
        [
            ((8, 5, 64, 128), bf16),
            ((8, 5, 64, 128), bf16),
            ((16, 64, 256), bf16),
            ((16, 64, 256), bf16),
        ],
        (idx, grad_two, held, glu_two, stat_two, pull, gains),
        "refiner_grad",
        scratch=[pltpu.VMEM((9, 256, 256), bf16), pltpu.VMEM((16, 256, 128), bf16)],
        late=(2, 3, 4, 5),
    )
    output = natural(out_own, swap_with(out_send, "chan", 1), 0)
    fine_recv = swap_with(after(fine_send, shared_three), "chan", 1)

    def pair(keep, recv, name):
        return call(
            pair_sum_body,
            [(keep.shape, bf16)],
            (keep, recv),
            name,
            smem=0,
            late=(0, 1),
            cuts={0: 8, 1: 8},
        )[0]

    if eight:
        both = jnp.stack([small[2], theirs[2]], axis=0)
        vectors, combined = call(
            excite_back_body,
            [((32, 128), bf16), ((8, 384, 128), bf16)],
            (
                idx,
                both,
                swap_with(both, "chan", 1),
                squeezed,
                exciter_own,
                exciter_other,
                fine_keep,
                fine_recv,
            ),
            "excite_back",
            deps=(shared_three,),
        )
        parts = over_batch(combined)
        ready = (combined, out_own)
    else:
        refiner_pair = pair(fine_keep, fine_recv, "refiner_pair")
        ready = (refiner_pair, out_own)
        v = refiner_pair.reshape(8, 5, 64, 4, 32).transpose(1, 3, 2, 0, 4).reshape(20, 64, 256)
        v = v[:18].reshape(9, 2, 64, 256).astype(f32)
        refiner_sum = lax.psum_scatter(v, "batch", scatter_dimension=3, tiled=True)

    by_phase = (8, 2, 8, 2, 16, 128)
    grad_one, small_one, wide_keep, wide_send = call(
        make_back_one_body(entries),
        [
            ((2, 2, 10, 10, 16, 256), bf16),
            ((8, 128), f32),
            ((8, 9, 64, 128), bf16),
            ((8, 9, 64, 128), bf16),
        ],
        (
            idx,
            gap,
            logit_one,
            base,
            dh_own.reshape(by_phase),
            dh_other.reshape(by_phase),
            mask,
            stat_one,
            gains,
            shared_three,
            field,
        ),
        "back_one",
        scratch=[pltpu.VMEM((4, 4, 256, 512), f32)],
        deps=ready,
        late=(9,),
    )
    widener_pair = pair(wide_keep, swap_with(wide_send, "chan", 1), "widener_pair")
    if eight:
        widener_pair = after(widener_pair, parts)
        widener_parts = over_batch(widener_pair)
    else:
        v = widener_pair.reshape(8, 9, 64, 2, 64).transpose(1, 3, 2, 0, 4).reshape(9, 2, 64, 512)
        widener_sum = lax.psum_scatter(v.astype(f32), "batch", scatter_dimension=3, tiled=True)
    if eight:
        skip_keep, skip_send = call(
            skip_back_body,
            [((32, 8192), bf16), ((32, 8192), bf16)],
            (idx, vectors, flats),
            "skip_back",
            deps=(widener_pair,),
            late=(1,),
            cuts={1: 8},
        )
    blocks = call(
        input_back_body,
        [((16, 64, 128), bf16)] * 4,
        (idx, grad_one, wide_w),
        "input_back",
        scratch=[pltpu.VMEM((16, 64, 512), bf16)],
        deps=(skip_send,) if eight else (widener_pair,),
        late=(0, 1),
        cuts={0: 2, 1: 4},
    )
    if eight:
        skip_recv = swap_with(skip_send, "chan", 2)
        skip_own, skip_other = call(
            skip_add_body,
            [((32, 4096), f32), ((32, 4096), bf16)],
            (idx, skip_keep, skip_recv),
            "skip_add", plain=True,
        )
        blocks = [blocks[0]] + [after(b, skip_recv) for b in blocks[1:]]
    got = [blocks[0]] + [swap_with(blocks[k], "chan", k) for k in range(1, 4)]
    if eight:
        exciter_sum, squeezer_sum, refiner_sum = call(
            squeeze_back_body,
            [((32, 64), f32), ((16, 64, 128), f32), ((9, 2, 32, 64), f32)],
            (parts, skips_all),
            "squeeze_back",
            smem=0,
            deps=(widener_pair,),
        )
        exciter_sum = exciter_sum.T
        refiner_sum = refiner_sum.transpose(0, 1, 3, 2)
        (widener_sum,) = call(
            widener_sum_body,
            [(widener.shape, f32)],
            (widener_parts,),
            "widener_sum",
            smem=0,
        )
        input_grad, skip_grad = call(
            last_join_body,
            [(features.shape, f32), (skip_feature.shape, f32)],
            (idx, *got, skip_own, swap_with(skip_other, "chan", 1)),
            "last_join",
            deps=(widener_sum, squeezer_sum, output),
        )
    else:
        (input_grad,) = call(input_join_body, [(features.shape, f32)], (idx, *got), "input_join")
        lo, hi = small[2, :, :64], small[2, :, 64:]
        keep, send = jnp.where(core == 0, lo, hi), jnp.where(core == 0, hi, lo)
        grad_gate = natural(keep, swap_with(send, "chan", 1), 0)
        grad_excited = (grad_gate * gate * (1.0 - gate)).astype(bf16)
        exciter_grad = jnp.einsum(
            "bo,bc->oc", grad_excited, swish_full, preferred_element_type=f32
        )
        partial_swish = jnp.einsum(
            "bo,oc->bc", grad_excited, exciter_full, preferred_element_type=f32
        )
        grad_swish = lax.psum_scatter(
            partial_swish.astype(bf16), "chan", scatter_dimension=1, tiled=True
        ).astype(f32)
        grad_squeezed = grad_swish * squeeze_sig * (1.0 + squeezed * (1.0 - squeeze_sig))
        grad_squeezed = grad_squeezed.astype(bf16)
        squeezer_grad = jnp.einsum(
            "bo,bct->toc", grad_squeezed, pooled, preferred_element_type=f32
        )
        partial_pooled = jnp.einsum(
            "bo,toc->bct", grad_squeezed, squeezer_full, preferred_element_type=f32
        ).reshape(samples, -1, 128)
        skip_grad = lax.psum_scatter(
            partial_pooled.astype(bf16), "chan", scatter_dimension=1, tiled=True
        ).astype(f32)
        squeezer_sum = lax.psum_scatter(squeezer_grad, "batch", scatter_dimension=2, tiled=True)
        exciter_sum = lax.psum_scatter(exciter_grad, "batch", scatter_dimension=1, tiled=True)

    norms = jnp.concatenate([small_one[0:2], mine[2, 0:2]], axis=0)
    norm_grads = jnp.where(core == 0, norms[:, :64], norms[:, 64:])
    return (
        output,
        input_grad,
        skip_grad,
        widener_sum,
        refiner_sum,
        squeezer_sum,
        exciter_sum,
        norm_grads,
    )


def solution(mesh):
    placed = (
        P("batch", "chan", None),
        P("batch", "chan", None),
        P("batch"),
        P("batch"),
        P(None, None, "chan", "batch"),
        P(None, None, "chan", "batch"),
        P(None, "chan", "batch"),
        P("chan", "batch"),
        P("chan"),
        P("chan"),
        P("chan"),
        P("chan"),
        P("batch", "chan", None),
    )
    return jax.shard_map(
        on_device,
        mesh=mesh,
        in_specs=placed,
        out_specs=(
            P("batch", "chan", None),
            P("batch", "chan", None),
            P("batch", "chan", None),
            P(None, None, "chan", "batch"),
            P(None, None, "chan", "batch"),
            P(None, "chan", "batch"),
            P("chan", "batch"),
            P(None, "chan"),
        ),
        check_vma=False,
    )
```

```python
import jax
import jax.numpy as jnp
from jax import lax
from jax.experimental import pallas as pl
from jax.experimental.pallas import tpu as pltpu
from jax.sharding import PartitionSpec as P

MB = 4
epsilon = 1e-05
f32 = jnp.float32
bf16 = jnp.bfloat16
MIB = 2**20
LIMIT = 58

NT = (((1,), (1,)), ((), ()))
TN = (((0,), (0,)), ((), ()))


def dot(a, b, dims=None):
    if dims is None:
        return jnp.dot(a, b, preferred_element_type=f32)
    return lax.dot_general(a, b, dims, preferred_element_type=f32)


class Traffic:
    def __init__(self, ins, outs, in_sems, out_sems, late, cuts):
        self.ins, self.outs, self.out_sems = [], outs, out_sems
        self.sent = {}
        count = 0
        for k, (pieces, held) in enumerate(ins):
            copies, at = [], 0
            parts = cuts.get(k, 1)
            for piece in pieces:
                rows = piece.shape[0] // parts
                for n in range(parts):
                    src = piece.at[pl.ds(n * rows, rows)]
                    dst = held.at[pl.ds(at, rows)]
                    copies.append(pltpu.make_async_copy(src, dst, in_sems.at[count]))
                    count += 1
                    at += rows
            self.ins.append(copies)
        for copies in self.ins:
            for copy in copies:
                copy.start()
        self.need(*[k for k in range(len(ins)) if k not in late])

    def need(self, *which):
        for k in which:
            for copy in self.ins[k]:
                copy.wait()

    def need_part(self, k, n):
        self.ins[k][n].wait()

    def part(self, k, n, count):
        made, pieces = self.outs[k]
        rows = made.shape[0] // count
        if len(pieces) == 1:
            dst = pieces[0].at[pl.ds(n * rows, rows)]
        else:
            each = pieces[0].shape[0]
            dst = pieces[n * rows // each].at[pl.ds(n * rows % each, rows)]
        return pltpu.make_async_copy(
            made.at[pl.ds(n * rows, rows)], dst, self.out_sems.at[k, n]
        )

    def send(self, k, n=0, count=1):
        self.sent[k] = count
        self.part(k, n, count).start()

    def finish(self):
        for k in range(len(self.outs)):
            if k not in self.sent:
                for n in range(len(self.outs[k][1])):
                    self.send(k, n, len(self.outs[k][1]))
        for k, count in self.sent.items():
            for n in range(count):
                self.part(k, n, count).wait()


def grouped(refs, sizes):
    out, at = [], 0
    for size in sizes:
        out.append(refs[at : at + size])
        at += size
    return out


def call(body, outs, args, name, scratch=(), smem=1, deps=(), late=(), cuts={}, plain=False):
    scalars, args, deps = list(args[:smem]), list(args[smem:]), list(deps)
    args = [a if isinstance(a, tuple) else (a,) for a in args]
    outs = [o if len(o) == 3 else (*o, 1) for o in outs]
    in_sizes, out_sizes = [len(a) for a in args], [o[2] for o in outs]
    n_in, n_out = sum(in_sizes), sum(out_sizes)
    results = [
        jax.ShapeDtypeStruct((shape[0] // count, *shape[1:]), dtype)
        for shape, dtype, count in outs
        for _ in range(count)
    ]
    anywhere, inside = pl.BlockSpec(memory_space=pl.ANY), pl.BlockSpec(memory_space=pltpu.VMEM)

    def kernel(*refs):
        refs = list(refs)
        numbers, refs = refs[:smem], refs[smem:]
        ins, refs = refs[:n_in], refs[n_in + len(deps) :]
        made, refs = refs[:n_out], refs[n_out:]
        if plain:
            body(*numbers, *ins, *made, *refs)
            return
        held, refs = refs[: len(args)], refs[len(args) :]
        work, refs = refs[: len(outs)], refs[len(outs) :]
        traffic = Traffic(
            list(zip(grouped(ins, in_sizes), held)),
            list(zip(work, grouped(made, out_sizes))),
            refs[0],
            refs[1],
            late,
            cuts,
        )
        extra = (traffic,) if late else ()
        body(*extra, *numbers, *held, *work, *refs[2:])
        traffic.finish()

    own = []
    if not plain:
        own = [
            pltpu.VMEM((sum(p.shape[0] for p in a), *a[0].shape[1:]), a[0].dtype) for a in args
        ]
        own += [pltpu.VMEM(shape, dtype) for shape, dtype, _ in outs]
        own += [pltpu.SemaphoreType.DMA((n_in * max([1, *cuts.values()]),)), pltpu.SemaphoreType.DMA((len(outs), 8))]
    got = pl.pallas_call(
        kernel,
        out_shape=results,
        in_specs=[pl.BlockSpec(memory_space=pltpu.SMEM)] * smem
        + [inside if plain else anywhere] * n_in
        + [anywhere] * len(deps),
        out_specs=[inside if plain else anywhere] * n_out,
        scratch_shapes=own + list(scratch),
        compiler_params=pltpu.CompilerParams(
            vmem_limit_bytes=(16 if plain else LIMIT) * MIB
        ),
        cost_estimate=pl.CostEstimate(flops=0, bytes_accessed=0, transcendentals=0),
        name=name,
    )(*scalars, *[p for a in args for p in a], *deps)
    return [p[0] if len(p) == 1 else tuple(p) for p in grouped(list(got), out_sizes)]


def after(value, *deps):
    return pl.pallas_call(
        lambda *refs: None,
        out_shape=jax.ShapeDtypeStruct(value.shape, value.dtype),
        in_specs=[pl.BlockSpec(memory_space=pl.ANY)] * (1 + len(deps)),
        out_specs=pl.BlockSpec(memory_space=pl.ANY),
        input_output_aliases={0: 0},
        name="after",
    )(value, *deps)


def iota(shape, dim):
    return lax.broadcasted_iota(jnp.int32, shape, dim)


def onehot(cond):
    return jnp.where(cond, 1.0, 0.0).astype(f32).astype(bf16)


def eye(n):
    return onehot(iota((n, n), 0) == iota((n, n), 1))


def sixteen_swap():
    r, q = iota((256, 256), 0), iota((256, 256), 1)
    return onehot(((r % 16) == (q // 16)) & ((r // 16) == (q % 16)))


def tree(parts):
    parts = list(parts)
    while len(parts) > 1:
        parts = [parts[n] + parts[n + 1] for n in range(0, len(parts), 2)]
    return parts[0]


def sigmoid(v):
    return 1.0 / (1.0 + jnp.exp(-v))


def pack_wide_body(w, out):
    packed = jnp.concatenate([w[:, 0], w[:, 1]], axis=-1)
    for k in range(8):
        out[k] = packed


def pack_fine_body(r, e, e_other, out):
    slots = [r[q // 2, q % 2] for q in range(18)] + [e[...], e_other[...]]
    for row in range(5):
        out[row] = jnp.concatenate(slots[4 * row : 4 * row + 4], axis=-1)
    out[5:] = jnp.zeros((3, 64, 128), bf16)


def fill_taps(core, own, other, out):
    for blocks, side in ((own, core), (other, 1 - core)):
        for half in range(2):
            rows = pl.ds(pl.multiple_of(half * 128 + side * 64, 64), 64)
            lanes = slice(half * 64, half * 64 + 64)
            for group in range(4):
                w = [
                    jnp.concatenate(
                        [blocks[2 * group][t][:, lanes], blocks[2 * group + 1][t][:, lanes]],
                        axis=-1,
                    ).astype(f32)
                    for t in range(9)
                ]
                down = {
                    (0, 0): w[0:3],
                    (0, 1): [w[3 + s] + w[6 + s] for s in range(3)],
                    (1, 0): [w[s] + w[3 + s] for s in range(3)],
                    (1, 1): w[6:9],
                }
                for a in range(2):
                    for u in range(2):
                        d = down[(a, u)]
                        across = {
                            (0, 0): d[0],
                            (0, 1): d[1] + d[2],
                            (1, 0): d[0] + d[1],
                            (1, 1): d[2],
                        }
                        for b in range(2):
                            for v in range(2):
                                out[
                                    a * 8 + b * 4 + u * 2 + v,
                                    rows,
                                    group * 128 : group * 128 + 128,
                                ] = across[(b, v)].astype(bf16)


def refiner_body(idx, own, other, out, ex, ex_other):
    core = idx[1]
    for blocks, side in ((own, core), (other, 1 - core)):
        rows = pl.multiple_of(side * 64, 64)
        for q in range(20):
            lanes = slice((q % 4) * 32, (q % 4) * 32 + 32)
            piece = jnp.concatenate([blocks[k, q // 4][:, lanes] for k in range(8)], axis=-1)
            if q < 18:
                out[q // 2, pl.ds(rows + (q % 2) * 128, 64), :] = piece
            else:
                (ex, ex_other)[q - 18][pl.ds(rows, 64), :] = piece


def feature_select(place):
    r, q = iota((512, 512), 0), iota((512, 512), 1)
    kept = r % 256
    return onehot((((kept // 64) ^ place) * 64 + kept % 64) * 2 + r // 256 == q)


def feature_body(idx, b0, b1, b2, b3, out, turned):
    ident = eye(128)

    def turn(s, carry):
        x = jnp.concatenate([b0[s], b1[s], b2[s], b3[s]], axis=0)
        t = dot(ident, x, NT).astype(bf16)
        turned[s] = jnp.concatenate([t[:64], t[64:]], axis=-1)
        return carry

    lax.fori_loop(0, 16, turn, 0, unroll=4)
    swap = sixteen_swap()
    select = feature_select(idx[0])
    zero = jnp.zeros((10, 16, 512), bf16)
    out[0] = zero
    out[9] = zero
    out[:, 0] = zero
    out[:, 9] = zero
    for block in range(4):
        a = turned[:, block * 16 : block * 16 + 16, :].reshape(256, 512)
        c = dot(dot(swap, a).astype(bf16), select).astype(bf16)
        out[1 + 2 * block : 3 + 2 * block, 1:9] = c.reshape(2, 8, 16, 512)


def input_back_body(io, idx, d, w, b0, b1, b2, b3, turned):
    swap = sixteen_swap()
    select = feature_select(idx[0])

    acc = None
    for a in range(2):
        io.need_part(0, a)
        for b in range(2):
            io.need_part(1, 2 * a + b)
            lhs = jnp.concatenate(
                [
                    d[a, b, 2 - u - a : 10 - u - a, 2 - v - b : 10 - v - b].reshape(1024, 256)
                    for u in range(2)
                    for v in range(2)
                ],
                axis=-1,
            )
            first = a * 8 + b * 4
            term = dot(lhs, w[first : first + 4].reshape(1024, 512))
            acc = term if acc is None else acc + term
    x = dot(acc.astype(bf16), select, NT).astype(bf16)
    for block in range(4):
        t = dot(swap, x[block * 256 : block * 256 + 256]).astype(bf16)
        turned[:, block * 16 : block * 16 + 16, :] = t.reshape(16, 16, 512)
    ident = eye(256)

    def turn(s, carry):
        t = turned[s]
        t = jnp.concatenate([t[:, :256], t[:, 256:]], axis=0)
        o = dot(ident, t, NT).astype(bf16)
        b0[s] = o[0:64]
        b1[s] = o[64:128]
        b2[s] = o[128:192]
        b3[s] = o[192:256]
        return carry

    lax.fori_loop(0, 16, turn, 0, unroll=4)


def input_join_body(idx, b0, b1, b2, b3, out):
    at = pl.multiple_of(idx[1] * 16, 16)
    out[pl.ds(at, 16)] = b0[...].astype(f32) + b2[...].astype(f32)
    out[pl.ds(16 - at, 16)] = b1[...].astype(f32) + b3[...].astype(f32)


def upstream_body(idx, own, other, out, turned):
    first = idx[1] == 0
    ident = eye(256)

    def turn(s, carry):
        p, q = own[s], other[s]
        lo = jnp.where(first, p, q)
        hi = jnp.where(first, q, p)
        turned[s] = dot(ident, jnp.concatenate([lo, hi], axis=0), NT).astype(bf16)
        return carry

    lax.fori_loop(0, 16, turn, 0, unroll=4)
    swap = sixteen_swap()

    def mix(y, carry):
        a = turned[:, pl.ds(pl.multiple_of(y * 16, 16), 16), :].reshape(256, 128)
        out[y] = dot(swap, a).astype(bf16).reshape(16, 16, 128)
        return carry

    lax.fori_loop(0, 16, mix, 0, unroll=4)


def over_samples(mask, values):
    return jnp.concatenate(
        [jnp.sum(mask[m] * values, axis=0, keepdims=True) for m in range(MB)], axis=0
    )


def per_sample(mask, rows):
    return sum(mask[m] * rows[m : m + 1] for m in range(MB))


def local_stats(mask, mean_s, squares_s):
    ones = jnp.ones_like(mean_s)
    n = over_samples(mask, ones) * 256.0
    mean = over_samples(mask, mean_s) * 256.0 / jnp.maximum(n, 1.0)
    gap = mean_s - per_sample(mask, mean)
    squares = over_samples(mask, squares_s + 256.0 * gap * gap)
    return n, mean, squares


def total_stats(messages, entries):
    parts = [(g[0:4], g[4:8], g[8:12]) for g in messages]
    mean = tree([n * m for n, m, _ in parts]) / entries
    squares = tree([q + n * (m - mean) * (m - mean) for n, m, q in parts])
    inverse = lax.rsqrt(squares / entries + epsilon)
    return mean, inverse


def message_list(refs):
    return [ref[c] for ref in refs for c in range(ref.shape[0])]


def conv_one_body(io, idx, own, other, x, mask, gap, logit, base, msg, w, glu):
    fill_taps(idx[1], own, other, w)
    io.send(4)
    io.need(2, 3)
    total = jnp.zeros((16, 128), f32)
    for a in range(2):
        for b in range(2):
            kept = []
            for u in range(2):
                for v in range(2):
                    kept.append(x[u + a : u + a + 8, v + b : v + b + 8].reshape(1024, 512))
            first = a * 8 + b * 4
            rhs = jnp.concatenate([w[first + n] for n in range(4)], axis=-1)
            c = dot(jnp.concatenate(kept, axis=-1), rhs, NT)
            g = (c[:, :128] * sigmoid(c[:, 128:])).reshape(8, 8, 16, 128)
            logit[:, a, :, b] = c[:, 128:].reshape(8, 8, 16, 128).astype(bf16)
            glu[a, b] = g
            total = total + jnp.sum(g, axis=(0, 1))
    io.send(1)
    mean_s = total * (1.0 / 256.0)
    base[...] = mean_s
    io.send(2)

    squares = jnp.zeros((16, 128), f32)
    for i in range(8):
        for a in range(2):
            for b in range(2):
                d = glu[a, b, i] - mean_s[None]
                gap[i, a, :, b] = d.astype(bf16)
                squares = squares + jnp.sum(d * d, axis=0)
        io.send(0, i, 8)
    n, mean, squares = local_stats(mask[...], mean_s, squares)
    msg[0:4] = n
    msg[4:8] = mean
    msg[8:12] = squares
    msg[12:16] = jnp.zeros((4, 128), f32)


def make_scale_body(entries):
    def body(idx, mask, gains, base, messages, line, stat):
        mean, inverse = total_stats(message_list([messages]), entries)
        m = mask[...]
        mean_s, inverse_s = per_sample(m, mean), per_sample(m, inverse)
        stat[0] = base[...] - mean_s
        stat[1] = inverse_s
        scale = inverse_s * gains[0:1]
        line[0] = scale
        line[1] = (base[...] - mean_s) * scale + gains[1:2]
        if messages.shape[0] == 16 and messages.shape[1] == 32:
            core = idx[1]
            line[2, 0:8] = tree([messages[2 * k + core, 16:24] for k in range(8)])
            line[2, 8:16] = tree([messages[2 * k + core, 24:32] for k in range(8)])
        else:
            line[2] = jnp.zeros((16, 128), f32)

    return body


def conv_two_body(io, idx, own, other, line, line_other, w, up, held, glu, logit, sums):
    zero = jnp.zeros((18, 16, 256), bf16)
    held[0] = zero
    held[17] = zero
    held[:, 0] = zero
    held[:, 17] = zero

    def fill(y, carry):
        for gap, scale, side in ((own, line, idx[2]), (other, line_other, 1 - idx[2])):
            h = gap[y].astype(f32) * scale[0] + scale[1]
            lanes = pl.ds(pl.multiple_of(side * 128, 128), 128)
            held[y + 1, 1:17, :, lanes] = h.astype(bf16)
        return carry

    lax.fori_loop(0, 16, fill, 0, unroll=2)
    io.send(0)
    io.need(4)

    def rows(step, total):
        y = step * 4
        lhs = jnp.concatenate(
            [
                held[pl.ds(y + t // 3, 4), t % 3 : t % 3 + 16].reshape(1024, 256)
                for t in range(9)
            ],
            axis=-1,
        )
        rhs = jnp.concatenate([w[t] for t in range(9)], axis=-1)
        c = dot(lhs, rhs, NT)
        g = (c[:, :128] * sigmoid(c[:, 128:])).reshape(4, 16, 16, 128)
        logit[pl.ds(y, 4)] = c[:, 128:].reshape(4, 16, 16, 128).astype(bf16)
        glu[pl.ds(y, 4)] = g
        io.send(1, step, 4)
        io.send(2, step, 4)
        return total + jnp.sum(g, axis=(0, 1))

    total = lax.fori_loop(0, 4, rows, jnp.zeros((16, 128), f32), unroll=True)
    mean_s = total * (1.0 / 256.0)

    io.need(5)

    def spread(y, acc):
        gap = glu[y] - mean_s[None]
        u = up[y].astype(f32)
        return (
            acc[0] + jnp.sum(gap * gap, axis=0),
            acc[1] + jnp.sum(u, axis=0),
            acc[2] + jnp.sum(u * gap, axis=0),
        )

    none = jnp.zeros((16, 128), f32)
    squares, plain, cross = lax.fori_loop(0, 16, spread, (none, none, none))
    sums[0] = mean_s
    sums[1] = plain
    sums[2] = cross
    sums[3] = squares


def make_back_two_body(entries):
    def body(io, idx, glu, logit, up, mask, pull, gains, sums, w, gap, gap_other, messages, *outs):
        grad, own, other, small, stat, mine = outs
        messages = message_list([messages])
        mean, inverse = total_stats(messages, entries)
        plain = tree([g[12:16] for g in messages])
        cross = inverse * tree([g[16:20] + g[12:16] * (g[4:8] - mean) for g in messages])
        m = mask[...]
        mean_s, inverse_s = per_sample(m, mean), per_sample(m, inverse)
        gain, shift = gains[2:3], gains[3:4]
        stat[0] = mean_s
        stat[1] = inverse_s
        weight, gate = pull[0], pull[1]
        centred = sums[2] + sums[1] * (sums[0] - mean_s)
        small[2] = weight * (gain * inverse_s * centred + shift * sums[1])
        mine[2, 0:1] = jnp.sum(cross, axis=0, keepdims=True)
        mine[2, 1:2] = jnp.sum(plain, axis=0, keepdims=True)
        mine[2, 2:] = jnp.zeros((14, 128), f32)
        plain_s = per_sample(m, plain) * (1.0 / entries)
        cross_s = per_sample(m, cross) * (1.0 / entries)
        scale = inverse_s * gain
        factor = weight * gate
        io.need(0, 1, 2)
        zero = jnp.zeros((18, 16, 256), bf16)
        grad[0] = zero
        grad[17] = zero
        grad[:, 0] = zero
        grad[:, 17] = zero

        def step(y, carry):
            g = glu[y]
            s = sigmoid(logit[y].astype(f32))
            hat = (g - mean_s) * inverse_s
            d = scale * (up[y].astype(f32) * factor - plain_s - hat * cross_s)
            grad[y + 1, 1:17, :, 0:128] = (d * s).astype(bf16)
            grad[y + 1, 1:17, :, 128:256] = (d * g * (1.0 - s)).astype(bf16)
            return carry

        lax.fori_loop(0, 16, step, 0, unroll=2)
        io.send(0)
        io.need(7, 8, 9)

        def rows(step, acc):
            y = step * 4
            lhs = jnp.concatenate(
                [
                    grad[pl.ds(y + 2 - t // 3, 4), 2 - t % 3 : 18 - t % 3].reshape(1024, 256)
                    for t in range(9)
                ],
                axis=-1,
            )
            c = dot(lhs, w[...].reshape(2304, 256)).astype(bf16)
            out = []
            first = idx[2] == 0
            mine_c = jnp.where(first, c[:, :128], c[:, 128:])
            their_c = jnp.where(first, c[:, 128:], c[:, :128])
            for k, ref, at, d in ((1, own, gap, mine_c), (2, other, gap_other, their_c)):
                d = d.reshape(4, 16, 16, 128)
                ref[pl.ds(y, 4)] = d
                io.send(k, step, 4)
                d = d.astype(f32)
                out.append(jnp.sum(d, axis=(0, 1)))
                out.append(jnp.sum(d * at[pl.ds(y, 4)].astype(f32), axis=(0, 1)))
            return tuple(p + q for p, q in zip(acc, out))

        none = jnp.zeros((16, 128), f32)
        mine[0], mine[1], small[0], small[1] = lax.fori_loop(
            0, 4, rows, (none,) * 4, unroll=True
        )

    return body


def output_part(idx, glu, stat, pull, gains, own, other, turned):
    swap = sixteen_swap()
    mean_s, inverse_s = stat[0], stat[1]
    gain, shift = gains[2:3], gains[3:4]
    gate = pull[1]

    def step(y, carry):
        o = (((glu[y] - mean_s) * inverse_s) * gain + shift) * gate
        o = dot(swap, o.astype(bf16).reshape(256, 128)).astype(bf16)
        turned[:, pl.ds(pl.multiple_of(y * 16, 16), 16), :] = o.reshape(16, 16, 128)
        return carry

    lax.fori_loop(0, 16, step, 0, unroll=4)
    ident = eye(128)
    first = idx[1] == 0

    def turn(s, carry):
        t = dot(ident, turned[s], NT).astype(bf16)
        own[s] = jnp.where(first, t[:64], t[64:])
        other[s] = jnp.where(first, t[64:], t[:64])
        return carry

    lax.fori_loop(0, 16, turn, 0, unroll=4)


def refiner_grad_body(
    io, idx, grad, held, glu, stat, pull, gains, own, other, out_own, out_other, work, turned
):
    core = idx[1]

    def tap(t, carry):
        d = grad[1:17, 1:17].reshape(4096, 256)
        h = held[pl.ds(t // 3, 16), pl.ds(t % 3, 16)].reshape(4096, 256)
        work[t] = dot(d, h, TN).astype(bf16)
        return carry

    lax.fori_loop(0, 9, tap, 0, unroll=3)
    for out, side in ((own, core), (other, 1 - core)):
        start = pl.multiple_of(side * 64, 64)
        for row in range(5):
            pieces = [
                work[q // 2, pl.ds(start + (q % 2) * 128, 64), :]
                for q in range(4 * row, min(4 * row + 4, 18))
            ]
            pieces += [jnp.zeros((64, 256), bf16)] * (4 - len(pieces))
            for k in range(8):
                lanes = slice(k * 32, k * 32 + 32)
                out[k, row] = jnp.concatenate([p[:, lanes] for p in pieces], axis=-1)
    io.send(0)
    io.send(1)
    io.need(2, 3, 4, 5)
    output_part(idx, glu, stat, pull, gains, out_own, out_other, turned)


def refiner_sum_body(parts, out):
    total = tree([parts[k, :320].astype(f32) for k in range(8)])
    for row in range(5):
        turned = total[row * 64 : row * 64 + 64].T
        for q in range(4 * row, min(4 * row + 4, 18)):
            out[q // 2, q % 2] = turned[(q % 4) * 32 : (q % 4) * 32 + 32]


def first_sums_body(mine, theirs, mask, stat, payload):
    m = mask[...]
    plain = mine[0] + theirs[0]
    cross = mine[1] + theirs[1] + stat[0] * plain
    msg = jnp.concatenate([over_samples(m, plain), over_samples(m, cross * stat[1])], axis=0)
    for k in range(payload.shape[0]):
        payload[k] = msg


def make_back_one_body(entries):
    def body(
        io,
        idx,
        gap,
        logit,
        base,
        own,
        other,
        mask,
        stat,
        gains,
        messages,
        x,
        grad,
        small,
        keep,
        send,
        work,
    ):
        messages = message_list([messages])
        plain = tree([g[0:4] for g in messages])
        cross = tree([g[4:8] for g in messages])
        small[0:1] = jnp.sum(cross, axis=0, keepdims=True)
        small[1:2] = jnp.sum(plain, axis=0, keepdims=True)
        small[2:8] = jnp.zeros((6, 128), f32)
        io.send(1)
        m = mask[...]
        plain_s = per_sample(m, plain) * (1.0 / entries)
        cross_s = per_sample(m, cross) * (1.0 / entries)
        shift_s, inverse_s = stat[0], stat[1]
        mean = base[...]
        scale = inverse_s * gains[0:1]
        zero = jnp.zeros((10, 16, 256), bf16)
        for a in range(2):
            for b in range(2):
                grad[a, b, 0] = zero
                grad[a, b, 9] = zero
                grad[a, b, :, 0] = zero
                grad[a, b, :, 9] = zero

        def step(i, carry):
            for a in range(2):
                for b in range(2):
                    g = gap[i, a, :, b].astype(f32)
                    s = sigmoid(logit[i, a, :, b].astype(f32))
                    hat = (g + shift_s) * inverse_s
                    g = g + mean
                    d = own[i, a, :, b].astype(f32) + other[i, a, :, b].astype(f32)
                    d = scale * (d - plain_s - hat * cross_s)
                    grad[a, b, i + 1, 1:9, :, 0:128] = (d * s).astype(bf16)
                    grad[a, b, i + 1, 1:9, :, 128:256] = (d * g * (1.0 - s)).astype(bf16)
            return carry

        lax.fori_loop(0, 8, step, 0)
        io.send(0)
        io.need(9)
        widener_grad(idx[1], grad, x, keep, send, work)

    return body


def widener_grad(core, grad, x, own, other, work):
    def phase(n, carry):
        a, b = n // 2, n % 2
        d = grad[a, b, 1:9, 1:9].reshape(1024, 256)
        for u in range(2):
            for v in range(2):
                f = x[pl.ds(u + a, 8), pl.ds(v + b, 8)].reshape(1024, 512)
                work[n, 2 * u + v] = dot(d, f, TN)
        return carry

    lax.fori_loop(0, 4, phase, 0, unroll=2)
    source = {0: (0, 0), 1: (1, 0), 2: (1, 1)}
    for out, side in ((own, core), (other, 1 - core)):
        start = pl.multiple_of(side * 64, 64)
        for pair in range(4):
            lanes = slice(pair * 128, pair * 128 + 128)
            for r in range(3):
                for s in range(3):
                    both = []
                    for half in range(2):
                        rows = pl.ds(start + half * 128, 64)
                        both.append(
                            sum(
                                work[2 * a + b, 2 * source[r][a] + source[s][b], rows, lanes]
                                for a in range(2)
                                for b in range(2)
                            )
                        )
                    first, second = both
                    out[2 * pair, 3 * r + s] = jnp.concatenate(
                        [first[:, :64], second[:, :64]], axis=-1
                    ).astype(bf16)
                    out[2 * pair + 1, 3 * r + s] = jnp.concatenate(
                        [first[:, 64:], second[:, 64:]], axis=-1
                    ).astype(bf16)


def pair_sum_body(io, own, other, out):
    for k in range(8):
        io.need_part(0, k)
        io.need_part(1, k)
        out[k] = (own[k].astype(f32) + other[k].astype(f32)).astype(bf16)
        io.send(0, k, 8)


def widener_sum_body(parts, out):
    for t in range(9):
        total = tree([parts[k, t].astype(f32) for k in range(8)])
        out[t, 0] = total[:, :64]
        out[t, 1] = total[:, 64:]


def skip_quarter_body(idx, skip, out):
    rows = pl.ds(pl.multiple_of(idx[0] * 8, 8), 8)
    for i in range(8):
        out[i] = skip[rows, i * 16 : i * 16 + 16, :]


def squeeze_body(skip, kernels, msg, kept, out, rows):
    rows[...] = skip[...].astype(f32).reshape(1024, 128)
    for k in range(16):
        kept[:, k * 128 : k * 128 + 128] = rows[pl.ds(k, 64, stride=16), :].astype(bf16)
    part = dot(kept[...], kernels[...], NT)
    for i in range(8):
        for c in range(2):
            out[2 * i + c, 0:16] = msg[...]
            out[2 * i + c, 16:24] = part[i * 8 : i * 8 + 8, :128]
            out[2 * i + c, 24:32] = part[i * 8 : i * 8 + 8, 128:]


def gate_body(idx, s0, s1, s2, s3, ex, weight, out, squeezed):
    j, core = idx[0], idx[1]
    for n, part in enumerate((s0, s1, s2, s3)):
        rows = pl.ds(pl.multiple_of((j ^ n) * 8, 8), 8)
        squeezed[rows, :128] = part[2, 0:8]
        squeezed[rows, 128:] = part[2, 8:16]
    mine = squeezed[pl.ds(pl.multiple_of(core * 16, 16), 16), :]
    excited = dot((mine * sigmoid(mine)).astype(bf16), ex[...], NT)
    out[0] = weight[...]
    out[1] = sigmoid(excited)


def gate_message_body(idx, s0, s1, s2, s3, ex, weight, mask, sums, out, squeezed, payload):
    gate_body(idx, s0, s1, s2, s3, ex, weight, out, squeezed)
    message_two_body(mask, out, sums, payload)


def message_two_body(mask, pull, sums, payload):
    mean_s, plain, cross = sums[0], sums[1], sums[2]
    m = mask[...]
    n, mean, squares = local_stats(m, mean_s, sums[3])
    factor = pull[0] * pull[1]
    spread = over_samples(m, factor * (cross + plain * (mean_s - per_sample(m, mean))))
    rows = [n, mean, squares, over_samples(m, factor * plain), spread, jnp.zeros((4, 128), f32)]
    msg = jnp.concatenate(rows, axis=0)
    for k in range(payload.shape[0]):
        payload[k] = msg


def excite_back_body(idx, g0, g1, squeezed, ex_own, ex_other, fine, recv, vectors, out):
    chip = idx[2]
    s = squeezed[...]
    sigm = sigmoid(s)
    swish = (s * sigm).astype(bf16)
    mine, theirs = ex_own[...], ex_other[...]
    ex = jnp.where(
        chip == 0, jnp.concatenate([mine, theirs], axis=0), jnp.concatenate([theirs, mine], axis=0)
    )
    gate = sigmoid(dot(swish, ex, NT))
    core = idx[1]
    rows = []
    for half in range(2):
        own = jnp.where(core == half, g0[0], g1[0])
        other = jnp.where(core == half, g0[1], g1[1])
        lo, hi = jnp.where(chip == 0, own, other), jnp.where(chip == 0, other, own)
        rows.append(jnp.concatenate([lo, hi], axis=-1))
    grad_gate = jnp.concatenate(rows, axis=0)
    d_excited = (grad_gate * gate * (1.0 - gate)).astype(bf16)
    d_swish = dot(d_excited, ex)
    d_squeezed = d_swish * (sigm * (1.0 + s * (1.0 - sigm)))
    j = idx[0]
    pick_out = onehot(iota((256, 64), 0) == iota((256, 64), 1) + j * 64)
    both = jnp.concatenate(
        [dot(d_squeezed.astype(bf16), pick_out), dot(d_excited, pick_out)], axis=-1
    ).astype(bf16)
    vectors[...] = both
    pick_in = onehot((iota((256, 1024), 0) // 32 == iota((256, 1024), 1) // 128)
                     & (iota((256, 1024), 0) % 32 == iota((256, 1024), 1) % 128))
    picked = dot(swish, pick_in).astype(bf16)
    total = (fine[...].astype(f32) + recv[...].astype(f32)).astype(bf16)
    out[:, :320] = total.reshape(8, 320, 128)
    for k in range(8):
        out[k, 320:352] = both
        out[k, 352:384] = picked[:, k * 128 : k * 128 + 128]


def quarters_first(v):
    v = v.astype(f32)
    return jnp.concatenate(
        [v[i * 32 + q * 8 : i * 32 + q * 8 + 8] for q in range(4) for i in range(8)], axis=0
    )


def squeeze_back_body(parts, skips, ex_grad, sq_grad, refiner_out):
    refiner_sum_body(parts, refiner_out)
    vectors = jnp.concatenate([parts[k, 320:352] for k in range(8)], axis=0)
    swish = jnp.concatenate([parts[k, 352:384] for k in range(8)], axis=0)
    ex_grad[...] = dot(swish, vectors, TN)[:32, 64:]
    grad = dot(quarters_first(vectors).astype(bf16), skips[...], TN)
    for t in range(16):
        sq_grad[t] = grad[:64, t * 128 : t * 128 + 128]


def skip_back_body(io, idx, vectors, kernels, keep, send):
    d = vectors[:, :64]
    for i in range(8):
        io.need_part(1, i)
        pooled = dot(d, kernels[i * 64 : i * 64 + 64, :]).astype(bf16)
        lanes = slice((i % 4) * 2048, (i % 4) * 2048 + 2048)
        mine = idx[2] == i // 4

        @pl.when(mine)
        def _():
            keep[:, lanes] = pooled

        @pl.when(jnp.logical_not(mine))
        def _():
            send[:, lanes] = pooled


def skip_add_body(idx, own, other, keep, send):
    first = idx[1] == 0
    total = own[...].astype(f32) + other[...].astype(f32)
    lo, hi = total[:, :4096], total[:, 4096:]
    keep[...] = jnp.where(first, lo, hi)
    send[...] = jnp.where(first, hi, lo).astype(bf16)


def last_join_body(idx, b0, b1, b2, b3, own, other, out, skip):
    input_join_body(idx, b0, b1, b2, b3, out)
    for r in range(32):
        lanes = slice(r * 128, r * 128 + 128)
        skip[:, r, :] = own[:, lanes] + other[:, lanes].astype(f32)


def swap_with(v, axis, k):
    return lax.ppermute(v, axis, [(n, n ^ k) for n in range(lax.axis_size(axis))])


def on_device(
    features,
    skip_feature,
    section_ids,
    micro_ids,
    widener,
    refiner,
    squeezer,
    exciter,
    gain_one,
    bias_one,
    gain_two,
    bias_two,
    upstream,
):
    nb = lax.axis_size("batch")
    eight = nb == 8
    samples = features.shape[0]
    entries = float(samples * nb // MB * 256)
    i = lax.axis_index("batch")
    j = lax.axis_index("chan")
    core, chip = j % 2, j // 2
    idx = jnp.stack([j, core, chip, i]).astype(jnp.int32)

    def half(v, which):
        return lax.dynamic_slice_in_dim(v, which * 16, 16, axis=0)

    def natural(own, other, axis):
        return jnp.where(
            core == 0,
            jnp.concatenate([own, other], axis=axis),
            jnp.concatenate([other, own], axis=axis),
        )

    def over_batch(v):
        return lax.all_to_all(v, "batch", 0, 0, tiled=True)

    f_keep, f_send = half(features, core), half(features, 1 - core)
    f_blocks = [f_keep] + [
        swap_with(f_send if k % 2 else f_keep, "chan", k) for k in range(1, 4)
    ]
    if eight:
        (wide,) = call(
            pack_wide_body, [((8, 9, 64, 128), bf16)], (widener,), "pack_wide", smem=0, plain=True
        )
        wide_own = over_batch(wide)
    else:
        w_all = lax.all_gather(widener, "batch", axis=3, tiled=True)
        wide_own = w_all.reshape(9, 2, 64, 8, 64).transpose(3, 0, 2, 1, 4).reshape(8, 9, 64, 128)

    gains = jnp.stack([gain_one, bias_one, gain_two, bias_two], axis=0)
    gains = natural(gains, swap_with(gains, "chan", 1), 1)
    ids = half(micro_ids, core)
    mask = jnp.broadcast_to(
        (ids[None, :, None] == jnp.arange(MB, dtype=jnp.int32)[:, None, None]).astype(f32),
        (MB, 16, 128),
    )
    weight_of = jnp.where(section_ids == 0, 1.0, jnp.where(section_ids == 1, 2.0, 4.0)).astype(f32)
    weight = jnp.broadcast_to(half(weight_of, core)[:, None], (16, 128))

    groups = [[n * 4 + 2 * x + c for n in range(nb) for c in range(2)] for x in range(2)]

    def exchange(copies):
        return lax.all_to_all(
            copies, ("batch", "chan"), 0, 0, tiled=True, axis_index_groups=groups
        )

    def share(msg):
        if eight:
            return exchange(jnp.broadcast_to(msg, (16,) + msg.shape))
        pair = jnp.stack([msg, swap_with(msg, "chan", 1)], axis=0)
        return lax.all_gather(pair, "batch").reshape((-1,) + msg.shape)

    u_keep = half(upstream, core)
    u_other = swap_with(half(upstream, 1 - core), "chan", 1)
    (up,) = call(
        upstream_body,
        [((16, 16, 16, 128), bf16)],
        (idx, u_keep, u_other),
        "upstream_turned",
        scratch=[pltpu.VMEM((16, 256, 128), bf16)],
    )
    (field,) = call(
        feature_body,
        [((10, 10, 16, 512), bf16)],
        (idx, *f_blocks),
        "features_turned",
        scratch=[pltpu.VMEM((16, 64, 512), bf16)],
        deps=(up, gains, mask, weight),
    )
    if eight:
        by_tap = skip_feature.reshape(32, 2, 16, 8, 16).transpose(0, 1, 4, 2, 3)
        skip_full = lax.all_gather(by_tap.reshape(32, 32, 128), "chan", axis=1, tiled=True)
        flat = squeezer.reshape(16, 64, 16, 8).transpose(1, 2, 3, 0).reshape(64, 2048)
        squeezer_whole = lax.all_gather(
            squeezer.transpose(1, 0, 2).reshape(64, 2048), "chan", axis=0, tiled=True
        )
        (quarter,) = call(
            skip_quarter_body,
            [((8, 8, 16, 128), bf16)],
            (idx, skip_full),
            "skip_quarter", plain=True,
        )
        wide_own = after(wide_own, field, quarter)
        quarter = over_batch(after(quarter, wide_own))

        (fine,) = call(
            pack_fine_body,
            [((8, 64, 128), bf16)],
            (refiner, exciter, swap_with(exciter, "chan", 2)),
            "pack_fine",
            smem=0, plain=True,
            deps=(field,),
        )
        fine_own = lax.all_gather(fine, "batch")
    else:
        r_all = lax.all_gather(refiner, "batch", axis=3, tiled=True)
        e_all = lax.all_gather(exciter, "batch", axis=1, tiled=True)
        r_all = jnp.concatenate(
            [r_all.reshape(18, 64, 256), e_all[None], jnp.zeros((1, 64, 256), bf16)], axis=0
        )
        r_all = r_all.reshape(5, 4, 64, 8, 32).transpose(3, 0, 2, 1, 4).reshape(8, 5, 64, 128)
        fine_own = jnp.pad(r_all, ((0, 0), (0, 3), (0, 0), (0, 0)))

    wide_other = swap_with(wide_own, "chan", 1)
    gap, logit_one, base, msg_one, wide_w = call(
        conv_one_body,
        [
            ((8, 2, 8, 2, 16, 128), bf16, 2),
            ((8, 2, 8, 2, 16, 128), bf16),
            ((16, 128), f32),
            ((16, 128), f32),
            ((16, 256, 512), bf16),
        ],
        (idx, wide_own, wide_other, field, mask),
        "conv_one",
        scratch=[pltpu.VMEM((2, 2, 8, 8, 16, 128), f32)],
        late=(2, 3),
    )
    gap_other = tuple(swap_with(v, "chan", 2).reshape(8, 16, 16, 128) for v in gap)
    gap_flat = tuple(v.reshape(8, 16, 16, 128) for v in gap)

    if eight:
        skips, payload = call(
            squeeze_body,
            [((64, 2048), bf16), ((16, 32, 128), f32)],
            (quarter, squeezer_whole, msg_one),
            "squeeze",
            scratch=[pltpu.VMEM((1024, 128), f32)],
            smem=0,
        )
        shared_one = exchange(payload)
    else:
        shared_one = share(msg_one)
    shared_one = after(shared_one, *gap_other)
    line, stat_one = call(
        make_scale_body(entries),
        [((3, 16, 128), f32), ((2, 16, 128), f32)],
        (idx, mask, gains, base, shared_one),
        "scale",
        plain=True,
    )
    fine_own = after(fine_own, shared_one)
    fine_other = swap_with(fine_own, "chan", 1)
    fine_w, exciter_own, exciter_other = call(
        refiner_body,
        [((9, 256, 256), bf16), ((128, 256), bf16), ((128, 256), bf16)],
        (idx, fine_own, fine_other),
        "refiner_taps", plain=True,
    )
    line_other = swap_with(line, "chan", 2)
    if eight:
        squeezed = (line, swap_with(line, "chan", 1), line_other, swap_with(line_other, "chan", 1))
        skips_all = lax.all_gather(after(skips, line_other), "chan", axis=0, tiled=True)

    held, glu_two, logit_two, sums_two = call(
        conv_two_body,
        [
            ((18, 18, 16, 256), bf16),
            ((16, 16, 16, 128), f32),
            ((16, 16, 16, 128), bf16),
            ((4, 16, 128), f32),
        ],
        (idx, gap_flat, gap_other, line, line_other, fine_w, up),
        "conv_two",
        late=(4, 5),
    )
    if eight:
        pull, squeezed, payload_two = call(
            gate_message_body,
            [((2, 16, 128), f32), ((32, 256), f32), ((16, 24, 128), f32)],
            (idx, *squeezed, exciter_own, weight, mask, sums_two),
            "gate",
        )
        shared_two = exchange(payload_two)
    else:
        skip_full = lax.all_gather(skip_feature, "chan", axis=1, tiled=True)
        squeezer_full = lax.all_gather(squeezer, "batch", axis=2, tiled=True)
        pooled = skip_full.reshape(samples, -1, 16)
        squeezed = jnp.einsum("toc,bct->bo", squeezer_full, pooled, preferred_element_type=f32)
        squeeze_sig = jax.nn.sigmoid(squeezed)
        swish = (squeezed * squeeze_sig).astype(bf16)
        swish_full = lax.all_gather(swish, "chan", axis=1, tiled=True)
        exciter_full = lax.all_gather(exciter, "batch", axis=1, tiled=True)
        excited = jnp.einsum("oc,bc->bo", exciter_full, swish_full, preferred_element_type=f32)
        gate = jax.nn.sigmoid(excited)
        gate_mine = natural(half(gate, core), swap_with(half(gate, 1 - core), "chan", 1), 1)
        pull = jnp.stack([weight, gate_mine], axis=0)
        (msg_two,) = call(
            message_two_body, [((1, 24, 128), f32)], (mask, pull, sums_two), "message", smem=0
        )
        shared_two = share(msg_two[0])
    if eight:
        flats = lax.all_gather(after(flat, shared_two), "batch", axis=0, tiled=True)
    grad_two, dh_own, dh_send, small, stat_two, mine = call(
        make_back_two_body(entries),
        [
            ((18, 18, 16, 256), bf16),
            ((16, 16, 16, 128), bf16),
            ((16, 16, 16, 128), bf16),
            ((3, 16, 128), f32),
            ((2, 16, 128), f32),
            ((3, 16, 128), f32),
        ],
        (
            idx,
            glu_two,
            logit_two,
            up,
            mask,
            pull,
            gains,
            sums_two,
            fine_w,
            gap_flat,
            gap_other,
            shared_two,
        ),
        "back_two",
        deps=(skips_all,) if eight else (),
        late=(0, 1, 2, 7, 8, 9),
    )
    theirs = swap_with(small, "chan", 2)
    dh_other = swap_with(after(dh_send, theirs), "chan", 2)
    (payload_three,) = call(
        first_sums_body,
        [((16 if eight else 1, 8, 128), f32)],
        (mine, theirs, mask, stat_one),
        "first_sums",
        smem=0,
        plain=True,
    )
    shared_three = exchange(payload_three) if eight else share(payload_three[0])
    fine_keep, fine_send, out_own, out_send = call(
        refiner_grad_body,
        [
            ((8, 5, 64, 128), bf16),
            ((8, 5, 64, 128), bf16),
            ((16, 64, 256), bf16),
            ((16, 64, 256), bf16),
        ],
        (idx, grad_two, held, glu_two, stat_two, pull, gains),
        "refiner_grad",
        scratch=[pltpu.VMEM((9, 256, 256), bf16), pltpu.VMEM((16, 256, 128), bf16)],
        late=(2, 3, 4, 5),
    )
    output = natural(out_own, swap_with(out_send, "chan", 1), 0)
    fine_recv = swap_with(after(fine_send, shared_three), "chan", 1)

    def pair(keep, recv, name):
        return call(
            pair_sum_body,
            [(keep.shape, bf16)],
            (keep, recv),
            name,
            smem=0,
            late=(0, 1),
            cuts={0: 8, 1: 8},
        )[0]

    if eight:
        both = jnp.stack([small[2], theirs[2]], axis=0)
        vectors, combined = call(
            excite_back_body,
            [((32, 128), bf16), ((8, 384, 128), bf16)],
            (
                idx,
                both,
                swap_with(both, "chan", 1),
                squeezed,
                exciter_own,
                exciter_other,
                fine_keep,
                fine_recv,
            ),
            "excite_back",
            deps=(shared_three,),
        )
        parts = over_batch(combined)
        ready = (combined, out_own)
    else:
        refiner_pair = pair(fine_keep, fine_recv, "refiner_pair")
        ready = (refiner_pair, out_own)
        v = refiner_pair.reshape(8, 5, 64, 4, 32).transpose(1, 3, 2, 0, 4).reshape(20, 64, 256)
        v = v[:18].reshape(9, 2, 64, 256).astype(f32)
        refiner_sum = lax.psum_scatter(v, "batch", scatter_dimension=3, tiled=True)

    by_phase = (8, 2, 8, 2, 16, 128)
    grad_one, small_one, wide_keep, wide_send = call(
        make_back_one_body(entries),
        [
            ((2, 2, 10, 10, 16, 256), bf16),
            ((8, 128), f32),
            ((8, 9, 64, 128), bf16),
            ((8, 9, 64, 128), bf16),
        ],
        (
            idx,
            gap,
            logit_one,
            base,
            dh_own.reshape(by_phase),
            dh_other.reshape(by_phase),
            mask,
            stat_one,
            gains,
            shared_three,
            field,
        ),
        "back_one",
        scratch=[pltpu.VMEM((4, 4, 256, 512), f32)],
        deps=ready,
        late=(9,),
    )
    widener_pair = pair(wide_keep, swap_with(wide_send, "chan", 1), "widener_pair")
    if eight:
        widener_pair = after(widener_pair, parts)
        widener_parts = over_batch(widener_pair)
    else:
        v = widener_pair.reshape(8, 9, 64, 2, 64).transpose(1, 3, 2, 0, 4).reshape(9, 2, 64, 512)
        widener_sum = lax.psum_scatter(v.astype(f32), "batch", scatter_dimension=3, tiled=True)
    if eight:
        skip_keep, skip_send = call(
            skip_back_body,
            [((32, 8192), bf16), ((32, 8192), bf16)],
            (idx, vectors, flats),
            "skip_back",
            deps=(widener_pair,),
            late=(1,),
            cuts={1: 8},
        )
    blocks = call(
        input_back_body,
        [((16, 64, 128), bf16)] * 4,
        (idx, grad_one, wide_w),
        "input_back",
        scratch=[pltpu.VMEM((16, 64, 512), bf16)],
        deps=(skip_send,) if eight else (widener_pair,),
        late=(0, 1),
        cuts={0: 2, 1: 4},
    )
    if eight:
        skip_recv = swap_with(skip_send, "chan", 2)
        blocks = [blocks[0]] + [after(b, skip_recv) for b in blocks[1:]]
    got = [blocks[0]] + [swap_with(blocks[k], "chan", k) for k in range(1, 4)]
    if eight:
        exciter_sum, squeezer_sum, refiner_sum = call(
            squeeze_back_body,
            [((32, 64), f32), ((16, 64, 128), f32), ((9, 2, 32, 64), f32)],
            (parts, skips_all),
            "squeeze_back",
            smem=0,
            deps=(widener_pair,),
        )
        exciter_sum = exciter_sum.T
        refiner_sum = refiner_sum.transpose(0, 1, 3, 2)
        skip_own, skip_other = call(
            skip_add_body,
            [((32, 4096), f32), ((32, 4096), bf16)],
            (idx, skip_keep, skip_recv),
            "skip_add",
            plain=True,
            deps=(squeezer_sum,),
        )
        (widener_sum,) = call(
            widener_sum_body,
            [(widener.shape, f32)],
            (widener_parts,),
            "widener_sum",
            smem=0,
        )
        input_grad, skip_grad = call(
            last_join_body,
            [(features.shape, f32), (skip_feature.shape, f32)],
            (idx, *got, skip_own, swap_with(skip_other, "chan", 1)),
            "last_join",
            deps=(widener_sum, squeezer_sum, output),
        )
    else:
        (input_grad,) = call(input_join_body, [(features.shape, f32)], (idx, *got), "input_join")
        lo, hi = small[2, :, :64], small[2, :, 64:]
        keep, send = jnp.where(core == 0, lo, hi), jnp.where(core == 0, hi, lo)
        grad_gate = natural(keep, swap_with(send, "chan", 1), 0)
        grad_excited = (grad_gate * gate * (1.0 - gate)).astype(bf16)
        exciter_grad = jnp.einsum(
            "bo,bc->oc", grad_excited, swish_full, preferred_element_type=f32
        )
        partial_swish = jnp.einsum(
            "bo,oc->bc", grad_excited, exciter_full, preferred_element_type=f32
        )
        grad_swish = lax.psum_scatter(
            partial_swish.astype(bf16), "chan", scatter_dimension=1, tiled=True
        ).astype(f32)
        grad_squeezed = grad_swish * squeeze_sig * (1.0 + squeezed * (1.0 - squeeze_sig))
        grad_squeezed = grad_squeezed.astype(bf16)
        squeezer_grad = jnp.einsum(
            "bo,bct->toc", grad_squeezed, pooled, preferred_element_type=f32
        )
        partial_pooled = jnp.einsum(
            "bo,toc->bct", grad_squeezed, squeezer_full, preferred_element_type=f32
        ).reshape(samples, -1, 128)
        skip_grad = lax.psum_scatter(
            partial_pooled.astype(bf16), "chan", scatter_dimension=1, tiled=True
        ).astype(f32)
        squeezer_sum = lax.psum_scatter(squeezer_grad, "batch", scatter_dimension=2, tiled=True)
        exciter_sum = lax.psum_scatter(exciter_grad, "batch", scatter_dimension=1, tiled=True)

    norms = jnp.concatenate([small_one[0:2], mine[2, 0:2]], axis=0)
    norm_grads = jnp.where(core == 0, norms[:, :64], norms[:, 64:])
    return (
        output,
        input_grad,
        skip_grad,
        widener_sum,
        refiner_sum,
        squeezer_sum,
        exciter_sum,
        norm_grads,
    )


def solution(mesh):
    placed = (
        P("batch", "chan", None),
        P("batch", "chan", None),
        P("batch"),
        P("batch"),
        P(None, None, "chan", "batch"),
        P(None, None, "chan", "batch"),
        P(None, "chan", "batch"),
        P("chan", "batch"),
        P("chan"),
        P("chan"),
        P("chan"),
        P("chan"),
        P("batch", "chan", None),
    )
    return jax.shard_map(
        on_device,
        mesh=mesh,
        in_specs=placed,
        out_specs=(
            P("batch", "chan", None),
            P("batch", "chan", None),
            P("batch", "chan", None),
            P(None, None, "chan", "batch"),
            P(None, None, "chan", "batch"),
            P(None, "chan", "batch"),
            P("chan", "batch"),
            P(None, "chan"),
        ),
        check_vma=False,
    )
```

```python
import jax
import jax.numpy as jnp
from jax import lax
from jax.experimental import pallas as pl
from jax.experimental.pallas import tpu as pltpu
from jax.sharding import PartitionSpec as P

MB = 4
epsilon = 1e-05
f32 = jnp.float32
bf16 = jnp.bfloat16
MIB = 2**20
LIMIT = 58

NT = (((1,), (1,)), ((), ()))
TN = (((0,), (0,)), ((), ()))


def dot(a, b, dims=None):
    if dims is None:
        return jnp.dot(a, b, preferred_element_type=f32)
    return lax.dot_general(a, b, dims, preferred_element_type=f32)


class Traffic:
    def __init__(self, ins, outs, in_sems, out_sems, late, cuts):
        self.ins, self.outs, self.out_sems = [], outs, out_sems
        self.sent = {}
        count = 0
        for k, (pieces, held) in enumerate(ins):
            copies, at = [], 0
            parts = cuts.get(k, 1)
            for piece in pieces:
                rows = piece.shape[0] // parts
                for n in range(parts):
                    src = piece.at[pl.ds(n * rows, rows)]
                    dst = held.at[pl.ds(at, rows)]
                    copies.append(pltpu.make_async_copy(src, dst, in_sems.at[count]))
                    count += 1
                    at += rows
            self.ins.append(copies)
        for copies in self.ins:
            for copy in copies:
                copy.start()
        self.need(*[k for k in range(len(ins)) if k not in late])

    def need(self, *which):
        for k in which:
            for copy in self.ins[k]:
                copy.wait()

    def need_part(self, k, n):
        self.ins[k][n].wait()

    def part(self, k, n, count):
        made, pieces = self.outs[k]
        rows = made.shape[0] // count
        if len(pieces) == 1:
            dst = pieces[0].at[pl.ds(n * rows, rows)]
        else:
            each = pieces[0].shape[0]
            dst = pieces[n * rows // each].at[pl.ds(n * rows % each, rows)]
        return pltpu.make_async_copy(
            made.at[pl.ds(n * rows, rows)], dst, self.out_sems.at[k, n]
        )

    def send(self, k, n=0, count=1):
        self.sent[k] = count
        self.part(k, n, count).start()

    def finish(self):
        for k in range(len(self.outs)):
            if k not in self.sent:
                for n in range(len(self.outs[k][1])):
                    self.send(k, n, len(self.outs[k][1]))
        for k, count in self.sent.items():
            for n in range(count):
                self.part(k, n, count).wait()


def grouped(refs, sizes):
    out, at = [], 0
    for size in sizes:
        out.append(refs[at : at + size])
        at += size
    return out


def call(body, outs, args, name, scratch=(), smem=1, deps=(), late=(), cuts={}, plain=False):
    scalars, args, deps = list(args[:smem]), list(args[smem:]), list(deps)
    args = [a if isinstance(a, tuple) else (a,) for a in args]
    outs = [o if len(o) == 3 else (*o, 1) for o in outs]
    in_sizes, out_sizes = [len(a) for a in args], [o[2] for o in outs]
    n_in, n_out = sum(in_sizes), sum(out_sizes)
    results = [
        jax.ShapeDtypeStruct((shape[0] // count, *shape[1:]), dtype)
        for shape, dtype, count in outs
        for _ in range(count)
    ]
    anywhere, inside = pl.BlockSpec(memory_space=pl.ANY), pl.BlockSpec(memory_space=pltpu.VMEM)

    def kernel(*refs):
        refs = list(refs)
        numbers, refs = refs[:smem], refs[smem:]
        ins, refs = refs[:n_in], refs[n_in + len(deps) :]
        made, refs = refs[:n_out], refs[n_out:]
        if plain:
            body(*numbers, *ins, *made, *refs)
            return
        held, refs = refs[: len(args)], refs[len(args) :]
        work, refs = refs[: len(outs)], refs[len(outs) :]
        traffic = Traffic(
            list(zip(grouped(ins, in_sizes), held)),
            list(zip(work, grouped(made, out_sizes))),
            refs[0],
            refs[1],
            late,
            cuts,
        )
        extra = (traffic,) if late else ()
        body(*extra, *numbers, *held, *work, *refs[2:])
        traffic.finish()

    own = []
    if not plain:
        own = [
            pltpu.VMEM((sum(p.shape[0] for p in a), *a[0].shape[1:]), a[0].dtype) for a in args
        ]
        own += [pltpu.VMEM(shape, dtype) for shape, dtype, _ in outs]
        own += [pltpu.SemaphoreType.DMA((n_in * max([1, *cuts.values()]),)), pltpu.SemaphoreType.DMA((len(outs), 8))]
    got = pl.pallas_call(
        kernel,
        out_shape=results,
        in_specs=[pl.BlockSpec(memory_space=pltpu.SMEM)] * smem
        + [inside if plain else anywhere] * n_in
        + [anywhere] * len(deps),
        out_specs=[inside if plain else anywhere] * n_out,
        scratch_shapes=own + list(scratch),
        compiler_params=pltpu.CompilerParams(
            vmem_limit_bytes=(16 if plain else LIMIT) * MIB
        ),
        cost_estimate=pl.CostEstimate(flops=0, bytes_accessed=0, transcendentals=0),
        name=name,
    )(*scalars, *[p for a in args for p in a], *deps)
    return [p[0] if len(p) == 1 else tuple(p) for p in grouped(list(got), out_sizes)]


def after(value, *deps):
    return pl.pallas_call(
        lambda *refs: None,
        out_shape=jax.ShapeDtypeStruct(value.shape, value.dtype),
        in_specs=[pl.BlockSpec(memory_space=pl.ANY)] * (1 + len(deps)),
        out_specs=pl.BlockSpec(memory_space=pl.ANY),
        input_output_aliases={0: 0},
        name="after",
    )(value, *deps)


def iota(shape, dim):
    return lax.broadcasted_iota(jnp.int32, shape, dim)


def onehot(cond):
    return jnp.where(cond, 1.0, 0.0).astype(f32).astype(bf16)


def eye(n):
    return onehot(iota((n, n), 0) == iota((n, n), 1))


def sixteen_swap():
    r, q = iota((256, 256), 0), iota((256, 256), 1)
    return onehot(((r % 16) == (q // 16)) & ((r // 16) == (q % 16)))


def tree(parts):
    parts = list(parts)
    while len(parts) > 1:
        parts = [parts[n] + parts[n + 1] for n in range(0, len(parts), 2)]
    return parts[0]


def sigmoid(v):
    return 1.0 / (1.0 + jnp.exp(-v))


def pack_wide_body(w, out):
    packed = jnp.concatenate([w[:, 0], w[:, 1]], axis=-1)
    for k in range(8):
        out[k] = packed


def pack_fine_body(r, e, e_other, out):
    slots = [r[q // 2, q % 2] for q in range(18)] + [e[...], e_other[...]]
    for row in range(5):
        out[row] = jnp.concatenate(slots[4 * row : 4 * row + 4], axis=-1)
    out[5:] = jnp.zeros((3, 64, 128), bf16)


def fill_taps(core, own, other, out):
    for blocks, side in ((own, core), (other, 1 - core)):
        for half in range(2):
            rows = pl.ds(pl.multiple_of(half * 128 + side * 64, 64), 64)
            lanes = slice(half * 64, half * 64 + 64)
            for group in range(4):
                w = [
                    jnp.concatenate(
                        [blocks[2 * group][t][:, lanes], blocks[2 * group + 1][t][:, lanes]],
                        axis=-1,
                    ).astype(f32)
                    for t in range(9)
                ]
                down = {
                    (0, 0): w[0:3],
                    (0, 1): [w[3 + s] + w[6 + s] for s in range(3)],
                    (1, 0): [w[s] + w[3 + s] for s in range(3)],
                    (1, 1): w[6:9],
                }
                for a in range(2):
                    for u in range(2):
                        d = down[(a, u)]
                        across = {
                            (0, 0): d[0],
                            (0, 1): d[1] + d[2],
                            (1, 0): d[0] + d[1],
                            (1, 1): d[2],
                        }
                        for b in range(2):
                            for v in range(2):
                                out[
                                    a * 8 + b * 4 + u * 2 + v,
                                    rows,
                                    group * 128 : group * 128 + 128,
                                ] = across[(b, v)].astype(bf16)


def refiner_body(idx, own, other, out, ex, ex_other):
    core = idx[1]
    for blocks, side in ((own, core), (other, 1 - core)):
        rows = pl.multiple_of(side * 64, 64)
        for q in range(20):
            lanes = slice((q % 4) * 32, (q % 4) * 32 + 32)
            piece = jnp.concatenate([blocks[k, q // 4][:, lanes] for k in range(8)], axis=-1)
            if q < 18:
                out[q // 2, pl.ds(rows + (q % 2) * 128, 64), :] = piece
            else:
                (ex, ex_other)[q - 18][pl.ds(rows, 64), :] = piece


def feature_select(place):
    r, q = iota((512, 512), 0), iota((512, 512), 1)
    kept = r % 256
    return onehot((((kept // 64) ^ place) * 64 + kept % 64) * 2 + r // 256 == q)


def feature_body(idx, b0, b1, b2, b3, out, turned):
    ident = eye(128)

    def turn(s, carry):
        x = jnp.concatenate([b0[s], b1[s], b2[s], b3[s]], axis=0)
        t = dot(ident, x, NT).astype(bf16)
        turned[s] = jnp.concatenate([t[:64], t[64:]], axis=-1)
        return carry

    lax.fori_loop(0, 16, turn, 0, unroll=4)
    swap = sixteen_swap()
    select = feature_select(idx[0])
    zero = jnp.zeros((10, 16, 512), bf16)
    out[0] = zero
    out[9] = zero
    out[:, 0] = zero
    out[:, 9] = zero
    for block in range(4):
        a = turned[:, block * 16 : block * 16 + 16, :].reshape(256, 512)
        c = dot(dot(swap, a).astype(bf16), select).astype(bf16)
        out[1 + 2 * block : 3 + 2 * block, 1:9] = c.reshape(2, 8, 16, 512)


def input_back_body(io, idx, d, w, b0, b1, b2, b3, turned):
    swap = sixteen_swap()
    select = feature_select(idx[0])

    acc = None
    for a in range(2):
        io.need_part(0, a)
        for b in range(2):
            io.need_part(1, 2 * a + b)
            lhs = jnp.concatenate(
                [
                    d[a, b, 2 - u - a : 10 - u - a, 2 - v - b : 10 - v - b].reshape(1024, 256)
                    for u in range(2)
                    for v in range(2)
                ],
                axis=-1,
            )
            first = a * 8 + b * 4
            term = dot(lhs, w[first : first + 4].reshape(1024, 512))
            acc = term if acc is None else acc + term
    x = dot(acc.astype(bf16), select, NT).astype(bf16)
    for block in range(4):
        t = dot(swap, x[block * 256 : block * 256 + 256]).astype(bf16)
        turned[:, block * 16 : block * 16 + 16, :] = t.reshape(16, 16, 512)
    ident = eye(256)

    def turn(s, carry):
        t = turned[s]
        t = jnp.concatenate([t[:, :256], t[:, 256:]], axis=0)
        o = dot(ident, t, NT).astype(bf16)
        b0[s] = o[0:64]
        b1[s] = o[64:128]
        b2[s] = o[128:192]
        b3[s] = o[192:256]
        return carry

    lax.fori_loop(0, 16, turn, 0, unroll=4)


def input_join_body(idx, b0, b1, b2, b3, out):
    at = pl.multiple_of(idx[1] * 16, 16)
    out[pl.ds(at, 16)] = b0[...].astype(f32) + b2[...].astype(f32)
    out[pl.ds(16 - at, 16)] = b1[...].astype(f32) + b3[...].astype(f32)


def upstream_body(idx, own, other, out, turned):
    first = idx[1] == 0
    ident = eye(256)

    def turn(s, carry):
        p, q = own[s], other[s]
        lo = jnp.where(first, p, q)
        hi = jnp.where(first, q, p)
        turned[s] = dot(ident, jnp.concatenate([lo, hi], axis=0), NT).astype(bf16)
        return carry

    lax.fori_loop(0, 16, turn, 0, unroll=4)
    swap = sixteen_swap()

    def mix(y, carry):
        a = turned[:, pl.ds(pl.multiple_of(y * 16, 16), 16), :].reshape(256, 128)
        out[y] = dot(swap, a).astype(bf16).reshape(16, 16, 128)
        return carry

    lax.fori_loop(0, 16, mix, 0, unroll=4)


def over_samples(mask, values):
    return jnp.concatenate(
        [jnp.sum(mask[m] * values, axis=0, keepdims=True) for m in range(MB)], axis=0
    )


def per_sample(mask, rows):
    return sum(mask[m] * rows[m : m + 1] for m in range(MB))


def local_stats(mask, mean_s, squares_s):
    ones = jnp.ones_like(mean_s)
    n = over_samples(mask, ones) * 256.0
    mean = over_samples(mask, mean_s) * 256.0 / jnp.maximum(n, 1.0)
    gap = mean_s - per_sample(mask, mean)
    squares = over_samples(mask, squares_s + 256.0 * gap * gap)
    return n, mean, squares


def total_stats(messages, entries):
    parts = [(g[0:4], g[4:8], g[8:12]) for g in messages]
    mean = tree([n * m for n, m, _ in parts]) / entries
    squares = tree([q + n * (m - mean) * (m - mean) for n, m, q in parts])
    inverse = lax.rsqrt(squares / entries + epsilon)
    return mean, inverse


def message_list(refs):
    return [ref[c] for ref in refs for c in range(ref.shape[0])]


def conv_one_body(io, idx, own, other, x, mask, gap, logit, base, msg, w, glu):
    fill_taps(idx[1], own, other, w)
    io.send(4)
    io.need(2, 3)
    total = jnp.zeros((16, 128), f32)
    for a in range(2):
        for b in range(2):
            kept = []
            for u in range(2):
                for v in range(2):
                    kept.append(x[u + a : u + a + 8, v + b : v + b + 8].reshape(1024, 512))
            first = a * 8 + b * 4
            rhs = jnp.concatenate([w[first + n] for n in range(4)], axis=-1)
            c = dot(jnp.concatenate(kept, axis=-1), rhs, NT)
            g = (c[:, :128] * sigmoid(c[:, 128:])).reshape(8, 8, 16, 128)
            logit[:, a, :, b] = c[:, 128:].reshape(8, 8, 16, 128).astype(bf16)
            glu[a, b] = g
            total = total + jnp.sum(g, axis=(0, 1))
    io.send(1)
    mean_s = total * (1.0 / 256.0)
    base[...] = mean_s
    io.send(2)

    squares = jnp.zeros((16, 128), f32)
    for i in range(8):
        for a in range(2):
            for b in range(2):
                d = glu[a, b, i] - mean_s[None]
                gap[i, a, :, b] = d.astype(bf16)
                squares = squares + jnp.sum(d * d, axis=0)
        io.send(0, i, 8)
    n, mean, squares = local_stats(mask[...], mean_s, squares)
    msg[0:4] = n
    msg[4:8] = mean
    msg[8:12] = squares
    msg[12:16] = jnp.zeros((4, 128), f32)


def make_scale_body(entries):
    def body(idx, mask, gains, base, messages, line, stat):
        mean, inverse = total_stats(message_list([messages]), entries)
        m = mask[...]
        mean_s, inverse_s = per_sample(m, mean), per_sample(m, inverse)
        stat[0] = base[...] - mean_s
        stat[1] = inverse_s
        scale = inverse_s * gains[0:1]
        line[0] = scale
        line[1] = (base[...] - mean_s) * scale + gains[1:2]
        if messages.shape[0] == 16 and messages.shape[1] == 32:
            core = idx[1]
            line[2, 0:8] = tree([messages[2 * k + core, 16:24] for k in range(8)])
            line[2, 8:16] = tree([messages[2 * k + core, 24:32] for k in range(8)])
        else:
            line[2] = jnp.zeros((16, 128), f32)

    return body


def conv_two_body(io, idx, own, other, line, line_other, w, up, held, glu, logit, sums):
    zero = jnp.zeros((18, 16, 256), bf16)
    held[0] = zero
    held[17] = zero
    held[:, 0] = zero
    held[:, 17] = zero

    def fill(y, carry):
        for gap, scale, side in ((own, line, idx[2]), (other, line_other, 1 - idx[2])):
            h = gap[y].astype(f32) * scale[0] + scale[1]
            lanes = pl.ds(pl.multiple_of(side * 128, 128), 128)
            held[y + 1, 1:17, :, lanes] = h.astype(bf16)
        return carry

    lax.fori_loop(0, 16, fill, 0, unroll=2)
    io.send(0)
    io.need(4)

    def rows(step, total):
        y = step * 4
        lhs = jnp.concatenate(
            [
                held[pl.ds(y + t // 3, 4), t % 3 : t % 3 + 16].reshape(1024, 256)
                for t in range(9)
            ],
            axis=-1,
        )
        rhs = jnp.concatenate([w[t] for t in range(9)], axis=-1)
        c = dot(lhs, rhs, NT)
        g = (c[:, :128] * sigmoid(c[:, 128:])).reshape(4, 16, 16, 128)
        logit[pl.ds(y, 4)] = c[:, 128:].reshape(4, 16, 16, 128).astype(bf16)
        glu[pl.ds(y, 4)] = g
        io.send(1, step, 4)
        io.send(2, step, 4)
        return total + jnp.sum(g, axis=(0, 1))

    total = lax.fori_loop(0, 4, rows, jnp.zeros((16, 128), f32), unroll=True)
    mean_s = total * (1.0 / 256.0)

    io.need(5)

    def spread(y, acc):
        gap = glu[y] - mean_s[None]
        u = up[y].astype(f32)
        return (
            acc[0] + jnp.sum(gap * gap, axis=0),
            acc[1] + jnp.sum(u, axis=0),
            acc[2] + jnp.sum(u * gap, axis=0),
        )

    none = jnp.zeros((16, 128), f32)
    squares, plain, cross = lax.fori_loop(
        0, 16, spread, (none, none, none), unroll=2
    )
    sums[0] = mean_s
    sums[1] = plain
    sums[2] = cross
    sums[3] = squares


def make_back_two_body(entries):
    def body(io, idx, glu, logit, up, mask, pull, gains, sums, w, gap, gap_other, messages, *outs):
        grad, own, other, small, stat, mine = outs
        messages = message_list([messages])
        mean, inverse = total_stats(messages, entries)
        plain = tree([g[12:16] for g in messages])
        cross = inverse * tree([g[16:20] + g[12:16] * (g[4:8] - mean) for g in messages])
        m = mask[...]
        mean_s, inverse_s = per_sample(m, mean), per_sample(m, inverse)
        gain, shift = gains[2:3], gains[3:4]
        stat[0] = mean_s
        stat[1] = inverse_s
        weight, gate = pull[0], pull[1]
        centred = sums[2] + sums[1] * (sums[0] - mean_s)
        small[2] = weight * (gain * inverse_s * centred + shift * sums[1])
        mine[2, 0:1] = jnp.sum(cross, axis=0, keepdims=True)
        mine[2, 1:2] = jnp.sum(plain, axis=0, keepdims=True)
        mine[2, 2:] = jnp.zeros((14, 128), f32)
        plain_s = per_sample(m, plain) * (1.0 / entries)
        cross_s = per_sample(m, cross) * (1.0 / entries)
        scale = inverse_s * gain
        factor = weight * gate
        io.need(0, 1, 2)
        zero = jnp.zeros((18, 16, 256), bf16)
        grad[0] = zero
        grad[17] = zero
        grad[:, 0] = zero
        grad[:, 17] = zero

        def step(y, carry):
            g = glu[y]
            s = sigmoid(logit[y].astype(f32))
            hat = (g - mean_s) * inverse_s
            d = scale * (up[y].astype(f32) * factor - plain_s - hat * cross_s)
            grad[y + 1, 1:17, :, 0:128] = (d * s).astype(bf16)
            grad[y + 1, 1:17, :, 128:256] = (d * g * (1.0 - s)).astype(bf16)
            return carry

        lax.fori_loop(0, 16, step, 0, unroll=2)
        io.send(0)
        io.need(7, 8, 9)

        def rows(step, acc):
            y = step * 4
            lhs = jnp.concatenate(
                [
                    grad[pl.ds(y + 2 - t // 3, 4), 2 - t % 3 : 18 - t % 3].reshape(1024, 256)
                    for t in range(9)
                ],
                axis=-1,
            )
            c = dot(lhs, w[...].reshape(2304, 256)).astype(bf16)
            out = []
            first = idx[2] == 0
            mine_c = jnp.where(first, c[:, :128], c[:, 128:])
            their_c = jnp.where(first, c[:, 128:], c[:, :128])
            for k, ref, at, d in ((1, own, gap, mine_c), (2, other, gap_other, their_c)):
                d = d.reshape(4, 16, 16, 128)
                ref[pl.ds(y, 4)] = d
                io.send(k, step, 4)
                d = d.astype(f32)
                out.append(jnp.sum(d, axis=(0, 1)))
                out.append(jnp.sum(d * at[pl.ds(y, 4)].astype(f32), axis=(0, 1)))
            return tuple(p + q for p, q in zip(acc, out))

        none = jnp.zeros((16, 128), f32)
        mine[0], mine[1], small[0], small[1] = lax.fori_loop(
            0, 4, rows, (none,) * 4, unroll=True
        )

    return body


def output_part(idx, glu, stat, pull, gains, own, other, turned):
    swap = sixteen_swap()
    mean_s, inverse_s = stat[0], stat[1]
    gain, shift = gains[2:3], gains[3:4]
    gate = pull[1]

    def step(y, carry):
        o = (((glu[y] - mean_s) * inverse_s) * gain + shift) * gate
        o = dot(swap, o.astype(bf16).reshape(256, 128)).astype(bf16)
        turned[:, pl.ds(pl.multiple_of(y * 16, 16), 16), :] = o.reshape(16, 16, 128)
        return carry

    lax.fori_loop(0, 16, step, 0, unroll=4)
    ident = eye(128)
    first = idx[1] == 0

    def turn(s, carry):
        t = dot(ident, turned[s], NT).astype(bf16)
        own[s] = jnp.where(first, t[:64], t[64:])
        other[s] = jnp.where(first, t[64:], t[:64])
        return carry

    lax.fori_loop(0, 16, turn, 0, unroll=4)


def refiner_grad_body(
    io, idx, grad, held, glu, stat, pull, gains, own, other, out_own, out_other, work, turned
):
    core = idx[1]

    def tap(t, carry):
        d = grad[1:17, 1:17].reshape(4096, 256)
        h = held[pl.ds(t // 3, 16), pl.ds(t % 3, 16)].reshape(4096, 256)
        work[t] = dot(d, h, TN).astype(bf16)
        return carry

    lax.fori_loop(0, 9, tap, 0, unroll=3)
    for out, side in ((own, core), (other, 1 - core)):
        start = pl.multiple_of(side * 64, 64)
        for row in range(5):
            pieces = [
                work[q // 2, pl.ds(start + (q % 2) * 128, 64), :]
                for q in range(4 * row, min(4 * row + 4, 18))
            ]
            pieces += [jnp.zeros((64, 256), bf16)] * (4 - len(pieces))
            for k in range(8):
                lanes = slice(k * 32, k * 32 + 32)
                out[k, row] = jnp.concatenate([p[:, lanes] for p in pieces], axis=-1)
    io.send(0)
    io.send(1)
    io.need(2, 3, 4, 5)
    output_part(idx, glu, stat, pull, gains, out_own, out_other, turned)


def refiner_sum_body(parts, out):
    total = tree([parts[k, :320].astype(f32) for k in range(8)])
    for row in range(5):
        turned = total[row * 64 : row * 64 + 64].T
        for q in range(4 * row, min(4 * row + 4, 18)):
            out[q // 2, q % 2] = turned[(q % 4) * 32 : (q % 4) * 32 + 32]


def first_sums_body(mine, theirs, mask, stat, payload):
    m = mask[...]
    plain = mine[0] + theirs[0]
    cross = mine[1] + theirs[1] + stat[0] * plain
    msg = jnp.concatenate([over_samples(m, plain), over_samples(m, cross * stat[1])], axis=0)
    for k in range(payload.shape[0]):
        payload[k] = msg


def make_back_one_body(entries):
    def body(
        io,
        idx,
        gap,
        logit,
        base,
        own,
        other,
        mask,
        stat,
        gains,
        messages,
        x,
        grad,
        small,
        keep,
        send,
        work,
    ):
        messages = message_list([messages])
        plain = tree([g[0:4] for g in messages])
        cross = tree([g[4:8] for g in messages])
        small[0:1] = jnp.sum(cross, axis=0, keepdims=True)
        small[1:2] = jnp.sum(plain, axis=0, keepdims=True)
        small[2:8] = jnp.zeros((6, 128), f32)
        io.send(1)
        m = mask[...]
        plain_s = per_sample(m, plain) * (1.0 / entries)
        cross_s = per_sample(m, cross) * (1.0 / entries)
        shift_s, inverse_s = stat[0], stat[1]
        mean = base[...]
        scale = inverse_s * gains[0:1]
        zero = jnp.zeros((10, 16, 256), bf16)
        for a in range(2):
            for b in range(2):
                grad[a, b, 0] = zero
                grad[a, b, 9] = zero
                grad[a, b, :, 0] = zero
                grad[a, b, :, 9] = zero

        def step(i, carry):
            for a in range(2):
                for b in range(2):
                    g = gap[i, a, :, b].astype(f32)
                    s = sigmoid(logit[i, a, :, b].astype(f32))
                    hat = (g + shift_s) * inverse_s
                    g = g + mean
                    d = own[i, a, :, b].astype(f32) + other[i, a, :, b].astype(f32)
                    d = scale * (d - plain_s - hat * cross_s)
                    grad[a, b, i + 1, 1:9, :, 0:128] = (d * s).astype(bf16)
                    grad[a, b, i + 1, 1:9, :, 128:256] = (d * g * (1.0 - s)).astype(bf16)
            return carry

        lax.fori_loop(0, 8, step, 0, unroll=2)
        io.send(0)
        io.need(9)
        widener_grad(idx[1], grad, x, keep, send, work)

    return body


def widener_grad(core, grad, x, own, other, work):
    def phase(n, carry):
        a, b = n // 2, n % 2
        d = grad[a, b, 1:9, 1:9].reshape(1024, 256)
        for u in range(2):
            for v in range(2):
                f = x[pl.ds(u + a, 8), pl.ds(v + b, 8)].reshape(1024, 512)
                work[n, 2 * u + v] = dot(d, f, TN)
        return carry

    lax.fori_loop(0, 4, phase, 0, unroll=2)
    source = {0: (0, 0), 1: (1, 0), 2: (1, 1)}
    for out, side in ((own, core), (other, 1 - core)):
        start = pl.multiple_of(side * 64, 64)
        for pair in range(4):
            lanes = slice(pair * 128, pair * 128 + 128)
            for r in range(3):
                for s in range(3):
                    both = []
                    for half in range(2):
                        rows = pl.ds(start + half * 128, 64)
                        both.append(
                            sum(
                                work[2 * a + b, 2 * source[r][a] + source[s][b], rows, lanes]
                                for a in range(2)
                                for b in range(2)
                            )
                        )
                    first, second = both
                    out[2 * pair, 3 * r + s] = jnp.concatenate(
                        [first[:, :64], second[:, :64]], axis=-1
                    ).astype(bf16)
                    out[2 * pair + 1, 3 * r + s] = jnp.concatenate(
                        [first[:, 64:], second[:, 64:]], axis=-1
                    ).astype(bf16)


def pair_sum_body(io, own, other, out):
    for k in range(8):
        io.need_part(0, k)
        io.need_part(1, k)
        out[k] = (own[k].astype(f32) + other[k].astype(f32)).astype(bf16)
        io.send(0, k, 8)


def widener_sum_body(parts, out):
    for t in range(9):
        total = tree([parts[k, t].astype(f32) for k in range(8)])
        out[t, 0] = total[:, :64]
        out[t, 1] = total[:, 64:]


def skip_quarter_body(idx, skip, out):
    rows = pl.ds(pl.multiple_of(idx[0] * 8, 8), 8)
    for i in range(8):
        out[i] = skip[rows, i * 16 : i * 16 + 16, :]


def squeeze_body(skip, kernels, msg, kept, out, rows):
    rows[...] = skip[...].astype(f32).reshape(1024, 128)
    for k in range(16):
        kept[:, k * 128 : k * 128 + 128] = rows[pl.ds(k, 64, stride=16), :].astype(bf16)
    part = dot(kept[...], kernels[...], NT)
    for i in range(8):
        for c in range(2):
            out[2 * i + c, 0:16] = msg[...]
            out[2 * i + c, 16:24] = part[i * 8 : i * 8 + 8, :128]
            out[2 * i + c, 24:32] = part[i * 8 : i * 8 + 8, 128:]


def gate_body(idx, s0, s1, s2, s3, ex, weight, out, squeezed):
    j, core = idx[0], idx[1]
    for n, part in enumerate((s0, s1, s2, s3)):
        rows = pl.ds(pl.multiple_of((j ^ n) * 8, 8), 8)
        squeezed[rows, :128] = part[2, 0:8]
        squeezed[rows, 128:] = part[2, 8:16]
    mine = squeezed[pl.ds(pl.multiple_of(core * 16, 16), 16), :]
    excited = dot((mine * sigmoid(mine)).astype(bf16), ex[...], NT)
    out[0] = weight[...]
    out[1] = sigmoid(excited)


def gate_message_body(idx, s0, s1, s2, s3, ex, weight, mask, sums, out, squeezed, payload):
    gate_body(idx, s0, s1, s2, s3, ex, weight, out, squeezed)
    message_two_body(mask, out, sums, payload)


def message_two_body(mask, pull, sums, payload):
    mean_s, plain, cross = sums[0], sums[1], sums[2]
    m = mask[...]
    n, mean, squares = local_stats(m, mean_s, sums[3])
    factor = pull[0] * pull[1]
    spread = over_samples(m, factor * (cross + plain * (mean_s - per_sample(m, mean))))
    rows = [n, mean, squares, over_samples(m, factor * plain), spread, jnp.zeros((4, 128), f32)]
    msg = jnp.concatenate(rows, axis=0)
    for k in range(payload.shape[0]):
        payload[k] = msg


def excite_back_body(idx, g0, g1, squeezed, ex_own, ex_other, fine, recv, vectors, out):
    chip = idx[2]
    s = squeezed[...]
    sigm = sigmoid(s)
    swish = (s * sigm).astype(bf16)
    mine, theirs = ex_own[...], ex_other[...]
    ex = jnp.where(
        chip == 0, jnp.concatenate([mine, theirs], axis=0), jnp.concatenate([theirs, mine], axis=0)
    )
    gate = sigmoid(dot(swish, ex, NT))
    core = idx[1]
    rows = []
    for half in range(2):
        own = jnp.where(core == half, g0[0], g1[0])
        other = jnp.where(core == half, g0[1], g1[1])
        lo, hi = jnp.where(chip == 0, own, other), jnp.where(chip == 0, other, own)
        rows.append(jnp.concatenate([lo, hi], axis=-1))
    grad_gate = jnp.concatenate(rows, axis=0)
    d_excited = (grad_gate * gate * (1.0 - gate)).astype(bf16)
    d_swish = dot(d_excited, ex)
    d_squeezed = d_swish * (sigm * (1.0 + s * (1.0 - sigm)))
    j = idx[0]
    pick_out = onehot(iota((256, 64), 0) == iota((256, 64), 1) + j * 64)
    both = jnp.concatenate(
        [dot(d_squeezed.astype(bf16), pick_out), dot(d_excited, pick_out)], axis=-1
    ).astype(bf16)
    vectors[...] = both
    none = jnp.zeros((32, 96), bf16)
    total = (fine[...].astype(f32) + recv[...].astype(f32)).astype(bf16)
    out[:, :320] = total.reshape(8, 320, 128)
    for k in range(8):
        out[k, 320:352] = both
        out[k, 352:384] = jnp.concatenate([swish[:, k * 32 : k * 32 + 32], none], axis=-1)


def quarters_first(v):
    v = v.astype(f32)
    return jnp.concatenate(
        [v[i * 32 + q * 8 : i * 32 + q * 8 + 8] for q in range(4) for i in range(8)], axis=0
    )


def squeeze_back_body(parts, skips, ex_grad, sq_grad, refiner_out):
    refiner_sum_body(parts, refiner_out)
    vectors = jnp.concatenate([parts[k, 320:352] for k in range(8)], axis=0)
    swish = jnp.concatenate([parts[k, 352:384] for k in range(8)], axis=0)
    ex_grad[...] = dot(swish, vectors, TN)[:32, 64:]
    grad = dot(quarters_first(vectors).astype(bf16), skips[...], TN)
    for t in range(16):
        sq_grad[t] = grad[:64, t * 128 : t * 128 + 128]


def skip_back_body(io, idx, vectors, kernels, keep, send):
    d = vectors[:, :64]
    for i in range(8):
        io.need_part(1, i)
        pooled = dot(d, kernels[i * 64 : i * 64 + 64, :]).astype(bf16)
        lanes = slice((i % 4) * 2048, (i % 4) * 2048 + 2048)
        mine = idx[2] == i // 4

        @pl.when(mine)
        def _():
            keep[:, lanes] = pooled

        @pl.when(jnp.logical_not(mine))
        def _():
            send[:, lanes] = pooled


def skip_add_body(idx, own, other, keep, send):
    first = idx[1] == 0
    total = own[...].astype(f32) + other[...].astype(f32)
    lo, hi = total[:, :4096], total[:, 4096:]
    keep[...] = jnp.where(first, lo, hi)
    send[...] = jnp.where(first, hi, lo).astype(bf16)


def last_join_body(io, idx, b0, b1, b2, b3, own, other, out, skip):
    input_join_body(idx, b0, b1, b2, b3, out)
    io.send(0)
    io.need(4, 5)
    for r in range(32):
        lanes = slice(r * 128, r * 128 + 128)
        skip[:, r, :] = own[:, lanes] + other[:, lanes].astype(f32)


def swap_with(v, axis, k):
    return lax.ppermute(v, axis, [(n, n ^ k) for n in range(lax.axis_size(axis))])


def on_device(
    features,
    skip_feature,
    section_ids,
    micro_ids,
    widener,
    refiner,
    squeezer,
    exciter,
    gain_one,
    bias_one,
    gain_two,
    bias_two,
    upstream,
):
    nb = lax.axis_size("batch")
    eight = nb == 8
    samples = features.shape[0]
    entries = float(samples * nb // MB * 256)
    i = lax.axis_index("batch")
    j = lax.axis_index("chan")
    core, chip = j % 2, j // 2
    idx = jnp.stack([j, core, chip, i]).astype(jnp.int32)

    def half(v, which):
        return lax.dynamic_slice_in_dim(v, which * 16, 16, axis=0)

    def natural(own, other, axis):
        return jnp.where(
            core == 0,
            jnp.concatenate([own, other], axis=axis),
            jnp.concatenate([other, own], axis=axis),
        )

    def over_batch(v):
        return lax.all_to_all(v, "batch", 0, 0, tiled=True)

    f_keep, f_send = half(features, core), half(features, 1 - core)
    f_blocks = [f_keep] + [
        swap_with(f_send if k % 2 else f_keep, "chan", k) for k in range(1, 4)
    ]
    if eight:
        (wide,) = call(
            pack_wide_body, [((8, 9, 64, 128), bf16)], (widener,), "pack_wide", smem=0, plain=True
        )
        wide_own = over_batch(wide)
    else:
        w_all = lax.all_gather(widener, "batch", axis=3, tiled=True)
        wide_own = w_all.reshape(9, 2, 64, 8, 64).transpose(3, 0, 2, 1, 4).reshape(8, 9, 64, 128)

    gains = jnp.stack([gain_one, bias_one, gain_two, bias_two], axis=0)
    gains = natural(gains, swap_with(gains, "chan", 1), 1)
    ids = half(micro_ids, core)
    mask = jnp.broadcast_to(
        (ids[None, :, None] == jnp.arange(MB, dtype=jnp.int32)[:, None, None]).astype(f32),
        (MB, 16, 128),
    )
    weight_of = jnp.where(section_ids == 0, 1.0, jnp.where(section_ids == 1, 2.0, 4.0)).astype(f32)
    weight = jnp.broadcast_to(half(weight_of, core)[:, None], (16, 128))

    groups = [[n * 4 + 2 * x + c for n in range(nb) for c in range(2)] for x in range(2)]

    def exchange(copies):
        return lax.all_to_all(
            copies, ("batch", "chan"), 0, 0, tiled=True, axis_index_groups=groups
        )

    def share(msg):
        if eight:
            return exchange(jnp.broadcast_to(msg, (16,) + msg.shape))
        pair = jnp.stack([msg, swap_with(msg, "chan", 1)], axis=0)
        return lax.all_gather(pair, "batch").reshape((-1,) + msg.shape)

    u_keep = half(upstream, core)
    u_other = swap_with(half(upstream, 1 - core), "chan", 1)
    (up,) = call(
        upstream_body,
        [((16, 16, 16, 128), bf16)],
        (idx, u_keep, u_other),
        "upstream_turned",
        scratch=[pltpu.VMEM((16, 256, 128), bf16)],
    )
    (field,) = call(
        feature_body,
        [((10, 10, 16, 512), bf16)],
        (idx, *f_blocks),
        "features_turned",
        scratch=[pltpu.VMEM((16, 64, 512), bf16)],
        deps=(up, gains, mask, weight),
    )
    if eight:
        by_tap = skip_feature.reshape(32, 2, 16, 8, 16).transpose(0, 1, 4, 2, 3)
        skip_full = lax.all_gather(by_tap.reshape(32, 32, 128), "chan", axis=1, tiled=True)
        flat = squeezer.reshape(16, 64, 16, 8).transpose(1, 2, 3, 0).reshape(64, 2048)
        squeezer_whole = lax.all_gather(
            squeezer.transpose(1, 0, 2).reshape(64, 2048), "chan", axis=0, tiled=True
        )
        (quarter,) = call(
            skip_quarter_body,
            [((8, 8, 16, 128), bf16)],
            (idx, skip_full),
            "skip_quarter", plain=True,
        )
        wide_own = after(wide_own, field, quarter)
        quarter = over_batch(after(quarter, wide_own))

        (fine,) = call(
            pack_fine_body,
            [((8, 64, 128), bf16)],
            (refiner, exciter, swap_with(exciter, "chan", 2)),
            "pack_fine",
            smem=0, plain=True,
            deps=(field,),
        )
        fine_own = lax.all_gather(fine, "batch")
    else:
        r_all = lax.all_gather(refiner, "batch", axis=3, tiled=True)
        e_all = lax.all_gather(exciter, "batch", axis=1, tiled=True)
        r_all = jnp.concatenate(
            [r_all.reshape(18, 64, 256), e_all[None], jnp.zeros((1, 64, 256), bf16)], axis=0
        )
        r_all = r_all.reshape(5, 4, 64, 8, 32).transpose(3, 0, 2, 1, 4).reshape(8, 5, 64, 128)
        fine_own = jnp.pad(r_all, ((0, 0), (0, 3), (0, 0), (0, 0)))

    wide_other = swap_with(wide_own, "chan", 1)
    gap, logit_one, base, msg_one, wide_w = call(
        conv_one_body,
        [
            ((8, 2, 8, 2, 16, 128), bf16, 2),
            ((8, 2, 8, 2, 16, 128), bf16),
            ((16, 128), f32),
            ((16, 128), f32),
            ((16, 256, 512), bf16),
        ],
        (idx, wide_own, wide_other, field, mask),
        "conv_one",
        scratch=[pltpu.VMEM((2, 2, 8, 8, 16, 128), f32)],
        late=(2, 3),
    )
    gap_other = tuple(swap_with(v, "chan", 2).reshape(8, 16, 16, 128) for v in gap)
    gap_flat = tuple(v.reshape(8, 16, 16, 128) for v in gap)

    if eight:
        skips, payload = call(
            squeeze_body,
            [((64, 2048), bf16), ((16, 32, 128), f32)],
            (quarter, squeezer_whole, msg_one),
            "squeeze",
            scratch=[pltpu.VMEM((1024, 128), f32)],
            smem=0,
        )
        shared_one = exchange(payload)
    else:
        shared_one = share(msg_one)
    shared_one = after(shared_one, *gap_other)
    line, stat_one = call(
        make_scale_body(entries),
        [((3, 16, 128), f32), ((2, 16, 128), f32)],
        (idx, mask, gains, base, shared_one),
        "scale",
        plain=True,
    )
    fine_own = after(fine_own, shared_one)
    fine_other = swap_with(fine_own, "chan", 1)
    fine_w, exciter_own, exciter_other = call(
        refiner_body,
        [((9, 256, 256), bf16), ((128, 256), bf16), ((128, 256), bf16)],
        (idx, fine_own, fine_other),
        "refiner_taps", plain=True,
    )
    line_other = swap_with(line, "chan", 2)
    if eight:
        squeezed = (line, swap_with(line, "chan", 1), line_other, swap_with(line_other, "chan", 1))
        skips_all = lax.all_gather(after(skips, line_other), "chan", axis=0, tiled=True)

    held, glu_two, logit_two, sums_two = call(
        conv_two_body,
        [
            ((18, 18, 16, 256), bf16),
            ((16, 16, 16, 128), f32),
            ((16, 16, 16, 128), bf16),
            ((4, 16, 128), f32),
        ],
        (idx, gap_flat, gap_other, line, line_other, fine_w, up),
        "conv_two",
        late=(4, 5),
    )
    if eight:
        pull, squeezed, payload_two = call(
            gate_message_body,
            [((2, 16, 128), f32), ((32, 256), f32), ((16, 24, 128), f32)],
            (idx, *squeezed, exciter_own, weight, mask, sums_two),
            "gate",
        )
        shared_two = exchange(payload_two)
    else:
        skip_full = lax.all_gather(skip_feature, "chan", axis=1, tiled=True)
        squeezer_full = lax.all_gather(squeezer, "batch", axis=2, tiled=True)
        pooled = skip_full.reshape(samples, -1, 16)
        squeezed = jnp.einsum("toc,bct->bo", squeezer_full, pooled, preferred_element_type=f32)
        squeeze_sig = jax.nn.sigmoid(squeezed)
        swish = (squeezed * squeeze_sig).astype(bf16)
        swish_full = lax.all_gather(swish, "chan", axis=1, tiled=True)
        exciter_full = lax.all_gather(exciter, "batch", axis=1, tiled=True)
        excited = jnp.einsum("oc,bc->bo", exciter_full, swish_full, preferred_element_type=f32)
        gate = jax.nn.sigmoid(excited)
        gate_mine = natural(half(gate, core), swap_with(half(gate, 1 - core), "chan", 1), 1)
        pull = jnp.stack([weight, gate_mine], axis=0)
        (msg_two,) = call(
            message_two_body, [((1, 24, 128), f32)], (mask, pull, sums_two), "message", smem=0
        )
        shared_two = share(msg_two[0])
    if eight:
        flats = lax.all_gather(after(flat, shared_two), "batch", axis=0, tiled=True)
    grad_two, dh_own, dh_send, small, stat_two, mine = call(
        make_back_two_body(entries),
        [
            ((18, 18, 16, 256), bf16),
            ((16, 16, 16, 128), bf16),
            ((16, 16, 16, 128), bf16),
            ((3, 16, 128), f32),
            ((2, 16, 128), f32),
            ((3, 16, 128), f32),
        ],
        (
            idx,
            glu_two,
            logit_two,
            up,
            mask,
            pull,
            gains,
            sums_two,
            fine_w,
            gap_flat,
            gap_other,
            shared_two,
        ),
        "back_two",
        deps=(skips_all,) if eight else (),
        late=(0, 1, 2, 7, 8, 9),
    )
    theirs = swap_with(small, "chan", 2)
    dh_other = swap_with(after(dh_send, theirs), "chan", 2)
    (payload_three,) = call(
        first_sums_body,
        [((16 if eight else 1, 8, 128), f32)],
        (mine, theirs, mask, stat_one),
        "first_sums",
        smem=0,
        plain=True,
    )
    shared_three = exchange(payload_three) if eight else share(payload_three[0])
    fine_keep, fine_send, out_own, out_send = call(
        refiner_grad_body,
        [
            ((8, 5, 64, 128), bf16),
            ((8, 5, 64, 128), bf16),
            ((16, 64, 256), bf16),
            ((16, 64, 256), bf16),
        ],
        (idx, grad_two, held, glu_two, stat_two, pull, gains),
        "refiner_grad",
        scratch=[pltpu.VMEM((9, 256, 256), bf16), pltpu.VMEM((16, 256, 128), bf16)],
        late=(2, 3, 4, 5),
    )
    output = natural(out_own, swap_with(out_send, "chan", 1), 0)
    fine_recv = swap_with(after(fine_send, shared_three), "chan", 1)

    def pair(keep, recv, name):
        return call(
            pair_sum_body,
            [(keep.shape, bf16)],
            (keep, recv),
            name,
            smem=0,
            late=(0, 1),
            cuts={0: 8, 1: 8},
        )[0]

    if eight:
        both = jnp.stack([small[2], theirs[2]], axis=0)
        vectors, combined = call(
            excite_back_body,
            [((32, 128), bf16), ((8, 384, 128), bf16)],
            (
                idx,
                both,
                swap_with(both, "chan", 1),
                squeezed,
                exciter_own,
                exciter_other,
                fine_keep,
                fine_recv,
            ),
            "excite_back",
            deps=(shared_three,),
        )
        parts = over_batch(combined)
        ready = (combined, out_own)
    else:
        refiner_pair = pair(fine_keep, fine_recv, "refiner_pair")
        ready = (refiner_pair, out_own)
        v = refiner_pair.reshape(8, 5, 64, 4, 32).transpose(1, 3, 2, 0, 4).reshape(20, 64, 256)
        v = v[:18].reshape(9, 2, 64, 256).astype(f32)
        refiner_sum = lax.psum_scatter(v, "batch", scatter_dimension=3, tiled=True)

    by_phase = (8, 2, 8, 2, 16, 128)
    grad_one, small_one, wide_keep, wide_send = call(
        make_back_one_body(entries),
        [
            ((2, 2, 10, 10, 16, 256), bf16),
            ((8, 128), f32),
            ((8, 9, 64, 128), bf16),
            ((8, 9, 64, 128), bf16),
        ],
        (
            idx,
            gap,
            logit_one,
            base,
            dh_own.reshape(by_phase),
            dh_other.reshape(by_phase),
            mask,
            stat_one,
            gains,
            shared_three,
            field,
        ),
        "back_one",
        scratch=[pltpu.VMEM((4, 4, 256, 512), f32)],
        deps=ready,
        late=(9,),
    )
    widener_pair = pair(wide_keep, swap_with(wide_send, "chan", 1), "widener_pair")
    if eight:
        widener_pair = after(widener_pair, parts)
        widener_parts = over_batch(widener_pair)
    else:
        v = widener_pair.reshape(8, 9, 64, 2, 64).transpose(1, 3, 2, 0, 4).reshape(9, 2, 64, 512)
        widener_sum = lax.psum_scatter(v.astype(f32), "batch", scatter_dimension=3, tiled=True)
    if eight:
        skip_keep, skip_send = call(
            skip_back_body,
            [((32, 8192), bf16), ((32, 8192), bf16)],
            (idx, vectors, flats),
            "skip_back",
            deps=(widener_pair,),
            late=(1,),
            cuts={1: 8},
        )
    blocks = call(
        input_back_body,
        [((16, 64, 128), bf16)] * 4,
        (idx, grad_one, wide_w),
        "input_back",
        scratch=[pltpu.VMEM((16, 64, 512), bf16)],
        deps=(skip_send,) if eight else (widener_pair,),
        late=(0, 1),
        cuts={0: 2, 1: 4},
    )
    if eight:
        skip_recv = swap_with(skip_send, "chan", 2)
        skip_own, skip_other = call(
            skip_add_body,
            [((32, 4096), f32), ((32, 4096), bf16)],
            (idx, skip_keep, skip_recv),
            "skip_add", plain=True,
        )
        blocks = [blocks[0]] + [after(b, skip_recv) for b in blocks[1:]]
    got = [blocks[0]] + [swap_with(blocks[k], "chan", k) for k in range(1, 4)]
    if eight:
        exciter_sum, squeezer_sum, refiner_sum = call(
            squeeze_back_body,
            [((32, 64), f32), ((16, 64, 128), f32), ((9, 2, 32, 64), f32)],
            (parts, skips_all),
            "squeeze_back",
            smem=0,
            deps=(widener_pair,),
        )
        exciter_sum = exciter_sum.T
        refiner_sum = refiner_sum.transpose(0, 1, 3, 2)
        (widener_sum,) = call(
            widener_sum_body,
            [(widener.shape, f32)],
            (widener_parts,),
            "widener_sum",
            smem=0,
        )
        input_grad, skip_grad = call(
            last_join_body,
            [(features.shape, f32), (skip_feature.shape, f32)],
            (idx, *got, skip_own, swap_with(skip_other, "chan", 1)),
            "last_join",
            late=(4, 5),
            deps=(widener_sum, squeezer_sum, output),
        )
    else:
        (input_grad,) = call(input_join_body, [(features.shape, f32)], (idx, *got), "input_join")
        lo, hi = small[2, :, :64], small[2, :, 64:]
        keep, send = jnp.where(core == 0, lo, hi), jnp.where(core == 0, hi, lo)
        grad_gate = natural(keep, swap_with(send, "chan", 1), 0)
        grad_excited = (grad_gate * gate * (1.0 - gate)).astype(bf16)
        exciter_grad = jnp.einsum(
            "bo,bc->oc", grad_excited, swish_full, preferred_element_type=f32
        )
        partial_swish = jnp.einsum(
            "bo,oc->bc", grad_excited, exciter_full, preferred_element_type=f32
        )
        grad_swish = lax.psum_scatter(
            partial_swish.astype(bf16), "chan", scatter_dimension=1, tiled=True
        ).astype(f32)
        grad_squeezed = grad_swish * squeeze_sig * (1.0 + squeezed * (1.0 - squeeze_sig))
        grad_squeezed = grad_squeezed.astype(bf16)
        squeezer_grad = jnp.einsum(
            "bo,bct->toc", grad_squeezed, pooled, preferred_element_type=f32
        )
        partial_pooled = jnp.einsum(
            "bo,toc->bct", grad_squeezed, squeezer_full, preferred_element_type=f32
        ).reshape(samples, -1, 128)
        skip_grad = lax.psum_scatter(
            partial_pooled.astype(bf16), "chan", scatter_dimension=1, tiled=True
        ).astype(f32)
        squeezer_sum = lax.psum_scatter(squeezer_grad, "batch", scatter_dimension=2, tiled=True)
        exciter_sum = lax.psum_scatter(exciter_grad, "batch", scatter_dimension=1, tiled=True)

    norms = jnp.concatenate([small_one[0:2], mine[2, 0:2]], axis=0)
    norm_grads = jnp.where(core == 0, norms[:, :64], norms[:, 64:])
    return (
        output,
        input_grad,
        skip_grad,
        widener_sum,
        refiner_sum,
        squeezer_sum,
        exciter_sum,
        norm_grads,
    )


def solution(mesh):
    placed = (
        P("batch", "chan", None),
        P("batch", "chan", None),
        P("batch"),
        P("batch"),
        P(None, None, "chan", "batch"),
        P(None, None, "chan", "batch"),
        P(None, "chan", "batch"),
        P("chan", "batch"),
        P("chan"),
        P("chan"),
        P("chan"),
        P("chan"),
        P("batch", "chan", None),
    )
    return jax.shard_map(
        on_device,
        mesh=mesh,
        in_specs=placed,
        out_specs=(
            P("batch", "chan", None),
            P("batch", "chan", None),
            P("batch", "chan", None),
            P(None, None, "chan", "batch"),
            P(None, None, "chan", "batch"),
            P(None, "chan", "batch"),
            P("chan", "batch"),
            P(None, "chan"),
        ),
        check_vma=False,
    )
```
